32 devices in a mesh: dp: 8 (over z, y), head: 4 (over x, core).
Axes of the slice: x: 2, y: 2, z: 4, core: 2. Of those that a mesh axis runs over, the one named last changes fastest.
Arguments:
- block_input: bfloat16 [8192, 768], P(('dp', 'head')), may hold values from -6 to 6
- cotangent: bfloat16 [8192, 768], P(('dp', 'head')), may hold values from -6 to 6
- marked: int32 [8, 1024], P('dp', 'head'), may hold values from 0 to 1, as said below
- segments: int32 [8, 1024], P('dp'), may hold values from 0 to 15, never falling along the last dimension, each value on 1 to 770 neighbouring positions
- feature_map: float32 [2, 64, 32], replicated, may hold values from -4 to 4
- vectors: float32 [2, 5, 768], replicated, may hold values from -0.5 to 1.3, as said below
- bias_up: float32 [2, 3072], P(None, 'head'), may hold values from -1.5 to 1.5
- w_query_key: float32 [2, 768, 2, 768], P(None, 'dp', None, 'head'), may hold values from -0.109375 to 0.109375
- w_value: float32 [2, 768, 768], P(None, 'dp', 'head'), may hold values from -0.21875 to 0.21875
- w_out: float32 [2, 768, 768], P(None, 'head', 'dp'), may hold values from -0.625 to 0.625
- w_up: float32 [2, 768, 3072], P(None, 'dp', 'head'), may hold values from -0.21875 to 0.21875
- w_down: float32 [2, 3072, 768], P(None, 'head', 'dp'), may hold values from -0.109375 to 0.109375
- moment_query_key: float32 [2, 768, 2, 768], P(None, 'dp', None, 'head'), may hold values from -20 to 20
- moment_value: float32 [2, 768, 768], P(None, 'dp', 'head'), may hold values from -56 to 56
- moment_out: float32 [2, 768, 768], P(None, 'head', 'dp'), may hold values from -56 to 56
- moment_up: float32 [2, 768, 3072], P(None, 'dp', 'head'), may hold values from -56 to 56
- moment_down: float32 [2, 3072, 768], P(None, 'head', 'dp'), may hold values from -56 to 56
- vector_first: float32 [2, 5, 768], replicated, may hold values from -20 to 20
- vector_second: float32 [2, 5, 768], replicated, may hold values from 10.24 to 40.96
- bias_first: float32 [2, 3072], P(None, 'head'), may hold values from -4 to 4
- bias_second: float32 [2, 3072], P(None, 'head'), may hold values from 2.048 to 8.192
Outputs:
- activations: bfloat16 [8192, 768], P(('dp', 'head'))
- input_grad: float32 [8192, 768], P(('dp', 'head'))
- next_w_query_key: float32 [2, 768, 2, 768], P(None, 'dp', None, 'head')
- next_w_value: float32 [2, 768, 768], P(None, 'dp', 'head')
- next_w_out: float32 [2, 768, 768], P(None, 'head', 'dp')
- next_w_up: float32 [2, 768, 3072], P(None, 'dp', 'head')
- next_w_down: float32 [2, 3072, 768], P(None, 'head', 'dp')
- next_moment_query_key: float32 [2, 768, 2, 768], P(None, 'dp', None, 'head')
- next_moment_value: float32 [2, 768, 768], P(None, 'dp', 'head')
- next_moment_out: float32 [2, 768, 768], P(None, 'head', 'dp')
- next_moment_up: float32 [2, 768, 3072], P(None, 'dp', 'head')
- next_moment_down: float32 [2, 3072, 768], P(None, 'head', 'dp')
- copy_query_key: bfloat16 [2, 768, 2, 768], P(None, 'dp', None, 'head')
- copy_value: bfloat16 [2, 768, 768], P(None, 'dp', 'head')
- copy_out: bfloat16 [2, 768, 768], P(None, 'head', 'dp')
- copy_up: bfloat16 [2, 768, 3072], P(None, 'dp', 'head')
- copy_down: bfloat16 [2, 3072, 768], P(None, 'head', 'dp')
- next_vectors: float32 [2, 5, 768], replicated
- next_vector_first: float32 [2, 5, 768], replicated
- next_vector_second: float32 [2, 5, 768], replicated
- next_bias_up: float32 [2, 3072], P(None, 'head')
- next_bias_first: float32 [2, 3072], P(None, 'head')
- next_bias_second: float32 [2, 3072], P(None, 'head')
The draws below stay inside these ranges and needn't reach their ends.
Inputs may be any that keep to these rules, and one draw needn't show every extreme that they name: `marked`: each sequence marks its own share of positions; some sequences may mark none. `segments`: never falling along a sequence; each sequence holds 16 documents, one of exactly 770 positions. `vectors`: rows 0 and 2 of each layer are gains, rows 1, 3 and 4 shifts.
All inputs are finite; a program needn't handle non-finite values.
Results may differ from the reference program's by a relative error of at most 0.022.
Values may be sent and summed in bfloat16 or wider, within the bound.
No kernel may reach another device: no remote copies, remote signals or barrier semaphores. Data moves between devices by JAX's collectives and lax.ppermute only.
A program may use at most 256 MiB of HBM per device.

```python
import math
import jax
import jax.numpy as jnp
import numpy as np
from jax import lax

D = 768
HEADS = 12
HEAD_DIM = 64
FF = 3072
FEATS = 32
BLOCK = 192
LAYERS = 2
NS_STEPS = 5
STEP = 10
DOCS = 16
TOK_DEV = 1024
MOST_DOC = 770
TOKENS = 8192
N_DP = 8


def draw_marked(key, part):
    key = jax.random.fold_in(key, 11)
    rate_key, roll_key, chosen_key = jax.random.split(key, 3)
    rates = jax.random.randint(rate_key, (N_DP,), 0, 6)
    chosen = jax.random.randint(chosen_key, (), 0, N_DP)
    rates = jnp.where(jnp.arange(N_DP) == chosen, 6, rates)
    rolls = jax.random.randint(roll_key, (N_DP, TOK_DEV), 0, 20)
    return (rolls < rates[:, None]).astype(jnp.int32)


def draw_vectors(key, part):
    key = jax.random.fold_in(key, 7)
    gain_key, shift_key = jax.random.split(key)
    gains = jax.random.uniform(gain_key, (LAYERS, 5, D), jnp.float32, 0.7, 1.3)
    shifts = jnp.clip(0.25 * jax.random.normal(shift_key, (LAYERS, 5, D), jnp.float32), -0.5, 0.5)
    row_index = jnp.arange(5)[None, :, None]
    gain_rows = (row_index % 2 == 0) & (row_index < 4)
    return jnp.where(gain_rows, gains, shifts)


def levels(rng, extent, cuts, low, largest):
    def one(position, parts):
        draws = jax.random.uniform(jax.random.fold_in(jax.random.fold_in(rng, 6), position), (parts,), jnp.float32, low / len(cuts), largest / len(cuts))
        return jnp.repeat(jnp.exp(draws), extent[position] // parts).reshape((-1,) + (1,) * (len(extent) - position - 1))

    loudness = one(*cuts[0])
    for cut in cuts[1:]:
        loudness = loudness * one(*cut)
    return loudness


def split_up(number_of, total, bound, skew):
    loads = [(1 << 20) // math.isqrt(grade ** skew) + 1 for grade in range(2, number_of + 1)]
    spare, holding = total - bound - (number_of - 1), [1] * (number_of - 1)
    while spare > 0:
        movable = [i for i in range(number_of - 1) if holding[i] < bound]
        mass, budget = sum([loads[i] for i in movable]), spare
        for i in movable:
            addition = min(bound - holding[i], max(1, budget * loads[i] // mass), spare)
            holding[i] = holding[i] + addition
            spare = spare - addition
    return np.array([bound] + holding)


def ragged(key, number_of, total, limit, slope):
    if number_of == 2:
        one = jax.random.randint(key, (), max(1, total - limit), min(limit, total - 1) + 1)
        return jnp.stack([one, total - one])
    lengths = jnp.asarray(split_up(number_of, total, limit, slope), jnp.int32)
    pairs = (number_of - 1) // 2
    giver, taker = lengths[1:1 + 2 * pairs:2], lengths[2:2 + 2 * pairs:2]
    margin = jnp.minimum(giver - 1, limit - taker)
    moved = jax.random.randint(jax.random.fold_in(key, 1), (pairs,), 0, 1 << 20) % (margin + 1)
    lengths = lengths.at[1:1 + 2 * pairs:2].set(giver - moved).at[2:2 + 2 * pairs:2].set(taker + moved)
    return lengths[jax.random.permutation(jax.random.fold_in(key, 2), number_of)]


def scatter_about(own_key, dims, width, limit, cuts=(), kind=jnp.bfloat16):
    drawn = width * jax.random.normal(own_key, dims, jnp.float32)
    if cuts:
        drawn = drawn * levels(own_key, dims, cuts, -0.22, 0.18)
    return jnp.clip(drawn, -limit, limit).astype(kind)


def setup_inputs(seed: int = 0) -> dict:
    keys = jax.random.split(jax.random.key(seed), 22)
    block_input = scatter_about(keys[0], (TOKENS, D), 1.0, 6.0, ((0, 32),))
    cotangent = scatter_about(keys[1], (TOKENS, D), 1.0, 6.0, ((0, 32),))
    marked = draw_marked(jax.random.fold_in(keys[21], 71), 0)
    segments = jax.vmap(lambda own: jnp.searchsorted(jnp.cumsum(ragged(own, DOCS, TOK_DEV, MOST_DOC, 2)), jnp.arange(TOK_DEV), side="right"))(jax.random.split(keys[3], N_DP)).reshape((N_DP, TOK_DEV)).astype(jnp.int32)
    feature_map = scatter_about(keys[4], (LAYERS, HEAD_DIM, FEATS), 1.0, 4.0, (), jnp.float32)
    vectors = draw_vectors(jax.random.fold_in(keys[21], 71), 0)
    bias_up = scatter_about(keys[6], (LAYERS, FF), 0.3, 1.5, ((1, 4),), jnp.float32)
    w_query_key = scatter_about(keys[7], (LAYERS, D, 2, D), (4 * D) ** -0.5, 0.109375, ((1, 8), (3, 4)), jnp.float32)
    w_value = scatter_about(keys[8], (LAYERS, D, D), D ** -0.5, 0.21875, ((1, 8), (2, 4)), jnp.float32)
    w_out = scatter_about(keys[9], (LAYERS, D, D), (D // 8) ** -0.5, 0.625, ((1, 4), (2, 8)), jnp.float32)
    w_up = scatter_about(keys[10], (LAYERS, D, FF), D ** -0.5, 0.21875, ((1, 8), (2, 4)), jnp.float32)
    w_down = scatter_about(keys[11], (LAYERS, FF, D), FF ** -0.5, 0.109375, ((1, 4), (2, 8)), jnp.float32)
    moment_query_key = scatter_about(keys[12], (LAYERS, D, 2, D), (0.1 * (TOKENS // 8) ** 0.5), 20.0, ((1, 8), (3, 4)), jnp.float32)
    moment_value = scatter_about(keys[13], (LAYERS, D, D), (0.3 * (TOKENS // 8) ** 0.5), 56.0, ((1, 8), (2, 4)), jnp.float32)
    moment_out = scatter_about(keys[14], (LAYERS, D, D), (0.3 * (TOKENS // 8) ** 0.5), 56.0, ((1, 4), (2, 8)), jnp.float32)
    moment_up = scatter_about(keys[15], (LAYERS, D, FF), (0.3 * (TOKENS // 8) ** 0.5), 56.0, ((1, 8), (2, 4)), jnp.float32)
    moment_down = scatter_about(keys[16], (LAYERS, FF, D), (0.3 * (TOKENS // 8) ** 0.5), 56.0, ((1, 4), (2, 8)), jnp.float32)
    vector_first = scatter_about(keys[17], (LAYERS, 5, D), (0.11 * (TOKENS // 8) ** 0.5), 20.0, (), jnp.float32)
    vector_second = jnp.clip(jnp.exp(jax.random.uniform(keys[18], (LAYERS, 5, D), jnp.float32, math.log(10.24), math.log(40.96))), 10.24, 40.96)
    bias_first = scatter_about(keys[19], (LAYERS, FF), (0.05 * (TOKENS // 8) ** 0.5), 4.0, ((1, 4),), jnp.float32)
    bias_second = jnp.clip(jnp.exp(math.log(8.192) - 1.3862944 * jax.random.uniform(keys[20], (LAYERS, FF), jnp.float32) ** levels(keys[20], (LAYERS, FF), ((1, 4),), -0.2, 0.2)), 2.048, 8.192)
    return {"block_input": block_input, "cotangent": cotangent, "marked": marked, "segments": segments, "feature_map": feature_map, "vectors": vectors, "bias_up": bias_up, "w_query_key": w_query_key, "w_value": w_value, "w_out": w_out, "w_up": w_up, "w_down": w_down, "moment_query_key": moment_query_key, "moment_value": moment_value, "moment_out": moment_out, "moment_up": moment_up, "moment_down": moment_down, "vector_first": vector_first, "vector_second": vector_second, "bias_first": bias_first, "bias_second": bias_second}


@jax.custom_vjp
def low(v):
    return lax.optimization_barrier(v.astype(jnp.bfloat16)).astype(jnp.float32)

@jax.custom_vjp
def low_back(v):
    return v

def low_keep(v):
    return (low(v), None)

def low_pass(kept, grad):
    return (grad,)

def back_keep(v):
    return (v, None)

def back_low(kept, grad):
    return (low(grad),)
low.defvjp(low_keep, low_pass)
low_back.defvjp(back_keep, back_low)
ORTHO_LINEAR = 3.4445
ORTHO_CUBIC = -4.775
ORTHO_QUINTIC = 2.0315
ORTHO_EPSILON = 1e-07
MOMENTUM_DECAY = 0.95
MUON_RATE = 0.2
WEIGHT_DECAY = 0.1
BETA_FIRST = 0.9
BETA_SECOND = 0.99
ADAM_RATE = 0.2
ADAM_EPSILON = 1e-08
NORM_EPSILON = 1e-05
ATTEND_EPSILON = 1e-06
ROPE_BASE = 10000.0
EXACT = lax.Precision.HIGHEST

def exact_dot(left, right):
    return jnp.dot(left, right, precision=EXACT, preferred_element_type=jnp.float32)

def layer_norm(values, gain, shift):
    row_mean = lax.optimization_barrier(jnp.mean(values, axis=-1, keepdims=True))
    centred = values - row_mean
    variance = lax.optimization_barrier(jnp.mean(centred * centred, axis=-1, keepdims=True))
    return centred * lax.rsqrt(variance + NORM_EPSILON) * gain + shift

def doc_tables(segment_row):
    labels = jnp.arange(DOCS, dtype=jnp.int32)
    member = (segment_row[:, None] == labels[None, :]).astype(jnp.int32)
    counts = lax.optimization_barrier(jnp.sum(member, axis=0, dtype=jnp.int32))
    starts = jnp.cumsum(counts, dtype=jnp.int32) - counts
    offsets = jnp.arange(segment_row.shape[0], dtype=jnp.int32) - lax.optimization_barrier(jnp.sum(member * starts[None, :], axis=1, dtype=jnp.int32))
    return (member.astype(jnp.float32), offsets.astype(jnp.float32))

def rotate(values, offsets):
    half_width = values.shape[-1] // 2
    frequency = ROPE_BASE ** (-jnp.arange(half_width, dtype=jnp.float32) / half_width)
    angles = offsets[:, None] * frequency[None, :]
    cosine = jnp.cos(angles)[:, None, :]
    sine_part = jnp.sin(angles)[:, None, :]
    first_half = values[..., :half_width]
    second_half = values[..., half_width:]
    return jnp.concatenate([first_half * cosine - second_half * sine_part, second_half * cosine + first_half * sine_part], axis=-1)

def features(values, feature_map):
    scaled = values * values.shape[-1] ** (-0.25)
    projected = jnp.einsum('shd,df->shf', scaled, feature_map, precision=EXACT)
    squared = 0.5 * lax.optimization_barrier(jnp.sum(scaled * scaled, axis=-1, keepdims=True))
    return jnp.exp(projected - squared) * feature_map.shape[-1] ** (-0.5)

def linear_attention(queries, key_rows, value_rows, feature_map, member, offsets):
    row_total, head_count, feat_count = (queries.shape[0], queries.shape[1], feature_map.shape[1])
    phi_query = features(rotate(queries, offsets), feature_map)
    phi_key = features(rotate(key_rows, offsets), feature_map)
    spread_key = (member[:, None, :, None] * phi_key[:, :, None, :]).reshape(row_total, head_count, -1)
    summary = jnp.einsum('shx,shd->hxd', spread_key, value_rows, precision=EXACT)
    totals = lax.optimization_barrier(jnp.sum(spread_key, axis=0))
    spread_query = (member[:, None, :, None] * phi_query[:, :, None, :]).reshape(row_total, head_count, -1)
    numerator = jnp.einsum('shx,hxd->shd', spread_query, summary, precision=EXACT)
    denominator = jnp.einsum('shx,hx->sh', spread_query, totals, precision=EXACT)
    return numerator / (denominator[..., None] + ATTEND_EPSILON)

def layer_forward(resid, weight_set, feature_map, member, offsets):
    query_key, value_weight, out_weight, up_weight, down_weight, vector_set, bias_set = weight_set
    row_total = resid.shape[0]
    head_shape = (row_total, HEADS, HEAD_DIM)
    normed = low(layer_norm(resid, vector_set[0], vector_set[1]))
    queries = low_back(exact_dot(normed, query_key[:, 0, :]))
    key_rows = low_back(exact_dot(normed, query_key[:, 1, :]))
    value_rows = low_back(exact_dot(normed, value_weight))
    context = linear_attention(queries.reshape(head_shape), key_rows.reshape(head_shape), value_rows.reshape(head_shape), feature_map, member, offsets)
    context = low(context.reshape(row_total, D))
    middle = resid + low_back(exact_dot(context, out_weight))
    normed_two = low(layer_norm(middle, vector_set[2], vector_set[3]))
    upper = low_back(exact_dot(normed_two, up_weight) + bias_set)
    active = low(jax.nn.gelu(upper, approximate=False))
    return middle + low_back(exact_dot(active, down_weight) + vector_set[4])

def model(weight_set, resid, feature_map, member, offsets):
    for layer_index in range(LAYERS):
        layer_set = tuple((weight[layer_index] for weight in weight_set))
        resid = layer_forward(resid, layer_set, feature_map[layer_index], member, offsets)
    return resid

def local_gram(iterate):
    return jnp.einsum('brc,brd->bcd', iterate, iterate, precision=EXACT)

def orthogonalize(blocks):
    gram_matrix = local_gram(blocks)
    norm_total = jnp.sqrt(jnp.trace(gram_matrix, axis1=1, axis2=2)) + ORTHO_EPSILON
    iterate = blocks / norm_total[:, None, None]
    gram_matrix = gram_matrix / (norm_total * norm_total)[:, None, None]
    for iteration in range(NS_STEPS):
        polynomial = ORTHO_CUBIC * gram_matrix + ORTHO_QUINTIC * jnp.einsum('bcd,bde->bce', gram_matrix, gram_matrix, precision=EXACT)
        iterate = ORTHO_LINEAR * iterate + jnp.einsum('brc,bcd->brd', iterate, polynomial, precision=EXACT)
        if iteration + 1 < NS_STEPS:
            gram_matrix = local_gram(iterate)
    return iterate

def column_blocks(matrix):
    layer_total, row_total, col_total = matrix.shape
    return jnp.transpose(matrix.reshape(layer_total, row_total, col_total // BLOCK, BLOCK), (0, 2, 1, 3)).reshape(-1, row_total, BLOCK)

def column_merge(blocks, layer_total, row_total, col_total):
    return jnp.transpose(blocks.reshape(layer_total, col_total // BLOCK, row_total, BLOCK), (0, 2, 1, 3)).reshape(layer_total, row_total, col_total)

def muon_update(master, moment, gradient, to_view, from_view):
    moment_next = MOMENTUM_DECAY * moment + gradient
    viewed = to_view(moment_next)
    ortho = column_merge(orthogonalize(column_blocks(viewed)), viewed.shape[0], viewed.shape[1], viewed.shape[2])
    master_next = master * (1.0 - MUON_RATE * WEIGHT_DECAY) - MUON_RATE * (D / BLOCK) ** 0.5 * from_view(ortho)
    return (master_next, moment_next)

def adam_update(parameter, gradient, first_moment, second_moment):
    first_moment = BETA_FIRST * first_moment + (1.0 - BETA_FIRST) * gradient
    second_moment = BETA_SECOND * second_moment + (1.0 - BETA_SECOND) * gradient * gradient
    first_hat = first_moment / (1.0 - BETA_FIRST ** STEP)
    second_hat = second_moment / (1.0 - BETA_SECOND ** STEP)
    return (parameter - ADAM_RATE * first_hat / (jnp.sqrt(second_hat) + ADAM_EPSILON), first_moment, second_moment)

def query_key_view(array):
    return jnp.transpose(array, (0, 2, 1, 3)).reshape(-1, D, D)

def query_key_back(array):
    return jnp.transpose(array.reshape(LAYERS, 2, D, D), (0, 2, 1, 3))

def same_view(array):
    return array

def swap_view(array):
    return jnp.transpose(array, (0, 2, 1))

def reference(block_input, cotangent, marked, segments, feature_map, vectors, bias_up, w_query_key, w_value, w_out, w_up, w_down, moment_query_key, moment_value, moment_out, moment_up, moment_down, vector_first, vector_second, bias_first, bias_second):
    masters = (w_query_key, w_value, w_out, w_up, w_down)
    weight_set = tuple((low(master) for master in masters)) + (vectors, bias_up)
    sequences = (block_input.reshape(N_DP, TOK_DEV, D), cotangent.reshape(N_DP, TOK_DEV, D), marked, segments)

    def one_sequence(running, items):
        seq_input, seq_cotangent, seq_marked, seq_segments = items
        member, offsets = doc_tables(seq_segments)

        def forward(weights_now, resid):
            return model(weights_now, resid, feature_map, member, offsets)
        output, pullback = jax.vjp(forward, weight_set, seq_input.astype(jnp.float32))
        start_grad = seq_cotangent.astype(jnp.float32) * seq_marked[:, None].astype(jnp.float32)
        weight_grads, input_part = pullback(start_grad)
        running = jax.tree.map(jnp.add, running, weight_grads)
        return (running, (output.astype(jnp.bfloat16), input_part))
    zeros = jax.tree.map(jnp.zeros_like, weight_set)
    totals, (outputs, input_parts) = lax.scan(one_sequence, zeros, sequences)
    grad_query_key, grad_value, grad_out, grad_up, grad_down, grad_vectors, grad_bias = totals
    next_query_key, moment_qk_next = muon_update(w_query_key, moment_query_key, grad_query_key, query_key_view, query_key_back)
    next_value, moment_value_next = muon_update(w_value, moment_value, grad_value, same_view, same_view)
    next_out, moment_out_next = muon_update(w_out, moment_out, grad_out, swap_view, swap_view)
    next_up, moment_up_next = muon_update(w_up, moment_up, grad_up, same_view, same_view)
    next_down, moment_down_next = muon_update(w_down, moment_down, grad_down, swap_view, swap_view)
    vectors_next, vector_first_next, vector_second_next = adam_update(vectors, grad_vectors, vector_first, vector_second)
    bias_next, bias_first_next, bias_second_next = adam_update(bias_up, grad_bias, bias_first, bias_second)
    return (outputs.reshape(TOKENS, D), input_parts.reshape(TOKENS, D), next_query_key, next_value, next_out, next_up, next_down, moment_qk_next, moment_value_next, moment_out_next, moment_up_next, moment_down_next, next_query_key.astype(jnp.bfloat16), next_value.astype(jnp.bfloat16), next_out.astype(jnp.bfloat16), next_up.astype(jnp.bfloat16), next_down.astype(jnp.bfloat16), vectors_next, vector_first_next, vector_second_next, bias_next, bias_first_next, bias_second_next)
```

```python
from functools import partial

import jax
import jax.numpy as jnp
from jax import lax
from jax.experimental import pallas as pl
from jax.experimental.pallas import tpu as pltpu
from jax.sharding import PartitionSpec as P

HEAD_DIM = 64
FEATS = 32
NS_STEPS = 5
STEP = 10


ORTHO_LINEAR = 3.4445
ORTHO_CUBIC = -4.775
ORTHO_QUINTIC = 2.0315
ORTHO_EPSILON = 1e-07
MOMENTUM_DECAY = 0.95
MUON_RATE = 0.2
WEIGHT_DECAY = 0.1
BETA_FIRST = 0.9
BETA_SECOND = 0.99
ADAM_RATE = 0.2
ADAM_EPSILON = 1e-08
NORM_EPSILON = 1e-05
ATTEND_EPSILON = 1e-06
ROPE_BASE = 10000.0
EXACT = lax.Precision.HIGHEST

F32 = jnp.float32
BF16 = jnp.bfloat16
CHUNK = 4 * HEAD_DIM
FEAT_CHUNK = 4 * FEATS
VMEM_BYTES = 56 * 1024 * 1024


def dot_nn(left, right):
    return lax.dot_general(left, right, (((1,), (0,)), ((), ())), preferred_element_type=F32)


def dot_nt(left, right):
    return lax.dot_general(left, right, (((1,), (1,)), ((), ())), preferred_element_type=F32)


def dot_tn(left, right):
    return lax.dot_general(left, right, (((0,), (0,)), ((), ())), preferred_element_type=F32)


def iota(shape, axis):
    return lax.broadcasted_iota(jnp.int32, shape, axis)


def swap_head(values, offset):
    return lax.ppermute(values, "head", [(h, h ^ offset) for h in range(lax.axis_size("head"))])


def swap_dp(values, offset):
    return lax.ppermute(values, "dp", [(d, d ^ offset) for d in range(lax.axis_size("dp"))])


def gather_weight(part, y_first):
    if lax.axis_size("dp") != 8:
        whole = lax.all_gather(part, "dp", axis=0, tiled=True)
        return [[whole]] + [[swap_head(whole, slot)] for slot in (1, 2, 3)]
    near = swap_dp(part, 2)
    line = jnp.concatenate([part, near, swap_dp(part, 4), swap_dp(near, 4)], axis=0)
    if y_first:
        own = [line, swap_dp(line, 1)]
        other = [swap_head(item, 2) for item in own]
    else:
        across = swap_head(line, 2)
        own = [line, swap_dp(line, 1)]
        other = [across, swap_dp(across, 1)]
    core = [[swap_head(item, 1) for item in group] for group in (own, other)]
    return [own, core[0], other, core[1]]


def fetch(refs, scratch, sems, base, lanes):
    per_slot = len(refs) // 4
    rows_in = refs[0].shape[0]
    pieces = 4 if per_slot > 1 else 1
    size = rows_in // pieces
    index = lax.axis_index("dp")
    waits = []
    count = base
    for slot in range(4):
        mine = []
        for y_offset in range(per_slot):
            for z_offset in range(pieces):
                if per_slot > 1:
                    start = pl.multiple_of((index ^ (z_offset * 2 + y_offset)) * size, 16)
                else:
                    start = 0
                copy = pltpu.make_async_copy(
                    refs[slot * per_slot + y_offset].at[
                        pl.ds(z_offset * size, size), pl.ds(lanes[0], lanes[1] - lanes[0])
                    ],
                    scratch.at[slot, pl.ds(start, size), :],
                    sems.at[count],
                )
                copy.start()
                mine.append(copy)
                count += 1
        waits.append(mine)
    return waits


def arrive(copies):
    for copy in copies:
        copy.wait()


def norm_parts(values):
    row_mean = jnp.mean(values, axis=-1, keepdims=True)
    centred = values - row_mean
    variance = jnp.mean(centred * centred, axis=-1, keepdims=True)
    scale = lax.rsqrt(variance + NORM_EPSILON)
    return centred * scale, scale


def norm_backward(values, gain, incoming):
    unit, scale = norm_parts(values)
    gain_grad = jnp.sum(incoming * unit, axis=0, keepdims=True)
    shift_grad = jnp.sum(incoming, axis=0, keepdims=True)
    inner = incoming * gain
    inner_mean = jnp.mean(inner, axis=-1, keepdims=True)
    along = jnp.mean(inner * unit, axis=-1, keepdims=True)
    return scale * (inner - inner_mean - unit * along), gain_grad, shift_grad


def swap_halves(values):
    width = values.shape[1]
    half = HEAD_DIM // 2
    lower = iota(values.shape, 1) % HEAD_DIM < half
    return jnp.where(lower, pltpu.roll(values, width - half, 1), pltpu.roll(values, half, 1))


def split_low(values):
    high = values.astype(BF16)
    return high, (values - high.astype(F32)).astype(BF16)


def lane_mask(index, per_head, width):
    return (iota((1, width), 1) // per_head == index).astype(BF16)


def feature_ones():
    return iota((CHUNK, FEAT_CHUNK), 0) // HEAD_DIM == iota((CHUNK, FEAT_CHUNK), 1) // FEATS


def features(values, map_high, map_low):
    high, low_part = split_low(values)
    square_high, square_low = split_low(0.5 * values * values)
    ones = -feature_ones().astype(BF16)
    left = jnp.concatenate([high, low_part, high, square_high, square_low], axis=1)
    right = jnp.concatenate([map_high, map_high, map_low, ones, ones], axis=0)
    return jnp.exp(dot_nn(left, right)) * FEATS ** (-0.5)


def fold_matrix():
    rows = iota((2 * CHUNK, 2 * HEAD_DIM), 0)
    columns = iota((2 * CHUNK, 2 * HEAD_DIM), 1)
    return (rows // CHUNK * HEAD_DIM + rows % HEAD_DIM == columns).astype(BF16)


def spread_matrix():
    rows = iota((2 * HEAD_DIM, 2 * CHUNK), 0)
    columns = iota((2 * HEAD_DIM, 2 * CHUNK), 1)
    return (columns // CHUNK * HEAD_DIM + columns % HEAD_DIM == rows).astype(BF16)


def same_head(feature_rows):
    shape = (feature_rows, 2 * CHUNK)
    return iota(shape, 0) % FEAT_CHUNK // FEATS == iota(shape, 1) % CHUNK // HEAD_DIM


def edge_masks(segment_column):
    first = segment_column[0:1, :]
    last = segment_column[segment_column.shape[0] - 1 :, :]
    in_first = (segment_column == first).astype(F32)
    in_last = (segment_column == last).astype(F32) * (1.0 - in_first)
    return in_first, in_last


def edge_summary(edges, weighted):
    full = dot_tn(edges, weighted)
    full = jnp.where(same_head(2 * FEAT_CHUNK), full, 0.0).astype(BF16)
    return dot_nn(full, fold_matrix()).astype(BF16)


def edges_of(phi, in_first, in_last):
    wide = phi.astype(F32)
    return jnp.concatenate([wide * in_first, wide * in_last], axis=1).astype(BF16)


def combine_edges(received, coefficients):
    totals = [None, None]
    rows = received[0].shape[1] // 4
    for position, ref in enumerate(received):
        offset = position + 1
        pair = []
        for which in range(2):
            value = ref[which].astype(F32)
            pair.append(
                jnp.concatenate(
                    [value[(slot ^ offset) * rows : ((slot ^ offset) + 1) * rows] for slot in range(4)], axis=0
                )
            )
        for which in range(2):
            part = coefficients[position, 2 * which] * pair[0] + coefficients[position, 2 * which + 1] * pair[1]
            totals[which] = part if totals[which] is None else totals[which] + part
    return totals


def spread_edges(totals, chunk):
    rows = slice(chunk * FEAT_CHUNK, (chunk + 1) * FEAT_CHUNK)
    joined = jnp.concatenate([totals[0][rows], totals[1][rows]], axis=0).astype(BF16)
    return jnp.where(same_head(2 * FEAT_CHUNK), dot_nn(joined, spread_matrix()), 0.0).astype(BF16)


def lanes_of(slot, width):
    return slice(slot * width, (slot + 1) * width)


def project_kernel(weight_count, resid, vectors, cosine, sine, feature_map, segment_column, *rest):
    weight_refs, rest = rest[:weight_count], rest[weight_count:]
    normed_out, phi_query_out, phi_key_out, value_out, query_out, key_out, summary_out, weight, sems = rest
    waits = fetch(weight_refs, weight, sems, 0, (0, weight.shape[2]))
    unit, _ = norm_parts(resid[...])
    normed = (unit * vectors[0:1, :] + vectors[1:2, :]).astype(BF16)
    normed_out[...] = normed
    width = resid.shape[1] // 4
    pieces = [[], [], []]
    for slot in range(4):
        arrive(waits[slot])
        product = dot_nn(normed, weight[slot, :, 0 : 3 * width])
        for which in range(3):
            pieces[which].append(product[:, lanes_of(which, width)])
    queries, key_rows, value_rows = (jnp.concatenate(piece, axis=1) for piece in pieces)
    value_rows = value_rows.astype(BF16)
    value_out[...] = value_rows
    map_high, map_low = split_low(feature_map[...])
    in_first, in_last = edge_masks(segment_column[...])
    ones = jnp.ones((resid.shape[0], CHUNK), BF16)
    for chunk in range(resid.shape[1] // CHUNK):
        lanes = lanes_of(chunk, CHUNK)
        feats = lanes_of(chunk, FEAT_CHUNK)
        turned = []
        for source, scaled_out, phi_out in (
            (queries, query_out, phi_query_out),
            (key_rows, key_out, phi_key_out),
        ):
            part = source[:, lanes]
            scaled = part * cosine[...] + swap_halves(part) * sine[...]
            scaled_out[:, lanes] = scaled
            phi = features(scaled, map_high, map_low).astype(BF16)
            phi_out[:, feats] = phi
            turned.append(phi)
        folded = edge_summary(
            edges_of(turned[1], in_first, in_last), jnp.concatenate([value_rows[:, lanes], ones], axis=1)
        )
        summary_out[0, feats, :] = folded[0:FEAT_CHUNK]
        summary_out[1, feats, :] = folded[FEAT_CHUNK:]


def mix_kernel(
    counts, resid, vectors, bias, phi_query, phi_key, value, segment_column, segment_row, recv_one, recv_two,
    recv_three, coefficients, *rest
):
    out_refs, rest = rest[: counts[0]], rest[counts[0] :]
    up_refs, rest = rest[: counts[0]], rest[counts[0] :]
    down_refs, rest = rest[: counts[0]], rest[counts[0] :]
    (context_out, inverse_out, middle_out, normed_out, slope_keep, slope_send, active_keep, active_send,
     resid_out, out_weight, up_weight, down_weight, sems) = rest
    total = counts[1]
    out_waits = fetch(out_refs, out_weight, sems, 0, (512, 768))
    up_waits = fetch(up_refs, up_weight, sems, total, (0, 768))
    down_waits = fetch(down_refs, down_weight, sems, 2 * total, (0, 768))
    same = (segment_column[...] == segment_row[...]).astype(F32)
    in_first, in_last = edge_masks(segment_column[...])
    totals = combine_edges((recv_one, recv_two, recv_three), coefficients)
    rows = resid.shape[0]
    contexts = []
    for chunk in range(resid.shape[1] // CHUNK):
        lanes = lanes_of(chunk, CHUNK)
        feats = lanes_of(chunk, FEAT_CHUNK)
        query = phi_query[:, feats]
        key = phi_key[:, feats]
        values = value[:, lanes]
        left = []
        right = []
        for head in range(4):
            scores = dot_nt(query * lane_mask(head, FEATS, FEAT_CHUNK), key)
            left.append((scores * same).astype(BF16))
            mask = lane_mask(head, HEAD_DIM, CHUNK)
            right.append(jnp.concatenate([values * mask, jnp.broadcast_to(mask, (rows, CHUNK))], axis=1))
        left.append(edges_of(query, in_first, in_last))
        right.append(spread_edges(totals, chunk))
        both = dot_nn(jnp.concatenate(left, axis=1), jnp.concatenate(right, axis=0))
        inverse = 1.0 / (both[:, CHUNK:] + ATTEND_EPSILON)
        context = both[:, :CHUNK] * inverse
        inverse_out[:, lanes] = inverse
        context_out[:, lanes] = context
        contexts.append(context.astype(BF16))
    context = jnp.concatenate(contexts, axis=1)
    width = resid.shape[1] // 4
    middle = resid[...]
    for slot in range(4):
        arrive(out_waits[slot])
        middle = middle + dot_nt(context[:, lanes_of(slot, width)], out_weight[slot, :, 64:])
    middle_out[...] = middle
    unit, _ = norm_parts(middle)
    normed = (unit * vectors[2:3, :] + vectors[3:4, :]).astype(BF16)
    normed_out[...] = normed
    output = middle + vectors[4:5, :]
    for slot in range(4):
        arrive(up_waits[slot])
        upper = dot_nn(normed, up_weight[slot]) + bias[slot : slot + 1, :]
        below = 0.5 * (1.0 + lax.erf(upper * 2.0**-0.5))
        slope = below + upper * (jnp.exp(-0.5 * upper * upper) * 0.3989422804014327)
        active = (upper * below).astype(BF16)
        if slot % 2 == 0:
            slope_keep[slot // 2] = slope.astype(BF16)
            active_keep[slot // 2] = active
        else:
            slope_send[slot // 2] = slope.astype(BF16)
            active_send[slot // 2] = active
        arrive(down_waits[slot])
        output = output + dot_nt(active, down_weight[slot])
    resid_out[...] = output


def back_mix_kernel(
    counts, grad, vectors, middle, slope_keep, slope_send, inverse, context, phi_query, segment_column, *rest
):
    out_refs, rest = rest[: counts[0]], rest[counts[0] :]
    up_refs, rest = rest[: counts[0]], rest[counts[0] :]
    down_refs, rest = rest[: counts[0]], rest[counts[0] :]
    (branch_out, upper_keep, upper_send, middle_grad_out, attn_out, numer_out, denom_out, summary_out, vector_out,
     bias_out, out_weight, up_weight, down_weight, sems) = rest
    total = counts[1]
    down_waits = fetch(down_refs, down_weight, sems, 2 * total, (0, 768))
    up_waits = fetch(up_refs, up_weight, sems, total, (0, 768))
    out_waits = fetch(out_refs, out_weight, sems, 0, (512, 768))
    grad_out = grad[...]
    branch = grad_out.astype(BF16)
    branch_out[...] = branch
    shift_out = jnp.sum(branch.astype(F32), axis=0, keepdims=True)
    normed_grad = None
    for slot in range(4):
        arrive(down_waits[slot])
        hidden = dot_nn(branch, down_weight[slot])
        slope = slope_keep[slot // 2] if slot % 2 == 0 else slope_send[slot // 2]
        upper = (hidden * slope.astype(F32)).astype(BF16)
        if slot % 2 == 0:
            upper_keep[slot // 2] = upper
        else:
            upper_send[slot // 2] = upper
        bias_out[slot : slot + 1, :] = jnp.sum(upper.astype(F32), axis=0, keepdims=True)
        arrive(up_waits[slot])
        part = dot_nt(upper, up_weight[slot])
        normed_grad = part if normed_grad is None else normed_grad + part
    inward, gain_grad, shift_grad = norm_backward(middle[...], vectors[2:3, :], normed_grad)
    middle_grad = grad_out + inward
    middle_grad_out[...] = middle_grad
    attn = middle_grad.astype(BF16)
    attn_out[...] = attn
    zero_row = jnp.zeros_like(shift_out)
    vector_out[...] = jnp.concatenate([zero_row, zero_row, gain_grad, shift_grad, shift_out] + [zero_row] * 3, axis=0)
    pieces = []
    for slot in range(4):
        arrive(out_waits[slot])
        pieces.append(dot_nn(attn, out_weight[slot, :, 64:]))
    context_grad = jnp.concatenate(pieces, axis=1)
    in_first, in_last = edge_masks(segment_column[...])
    head_ones = (iota((CHUNK, CHUNK), 0) // HEAD_DIM == iota((CHUNK, CHUNK), 1) // HEAD_DIM).astype(BF16)
    for chunk in range(grad.shape[1] // CHUNK):
        lanes = lanes_of(chunk, CHUNK)
        feats = lanes_of(chunk, FEAT_CHUNK)
        numer = context_grad[:, lanes] * inverse[:, lanes]
        denom = -dot_nn((numer * context[:, lanes]).astype(BF16), head_ones)
        numer = numer.astype(BF16)
        denom = denom.astype(BF16)
        numer_out[:, lanes] = numer
        denom_out[:, lanes] = denom
        folded = edge_summary(
            edges_of(phi_query[:, feats], in_first, in_last), jnp.concatenate([numer, denom], axis=1)
        )
        summary_out[0, feats, :] = folded[0:FEAT_CHUNK]
        summary_out[1, feats, :] = folded[FEAT_CHUNK:]


def back_project_kernel(
    weight_count, resid, vectors, cosine, sine, feature_map, segment_column, segment_row, phi_query, phi_key, value,
    query_scaled, key_scaled, numer, denom, context, middle_grad, recv_one, recv_two, recv_three, back_one, back_two,
    back_three, coefficients, *rest
):
    weight_refs, rest = rest[:weight_count], rest[weight_count:]
    stacked_keep, stacked_send, grad_out, vector_out, weight, sems = rest
    waits = fetch(weight_refs, weight, sems, 0, (0, weight.shape[2]))
    same = (segment_column[...] == segment_row[...]).astype(F32)
    in_first, in_last = edge_masks(segment_column[...])
    totals = combine_edges((recv_one, recv_two, recv_three), coefficients)
    back_totals = combine_edges((back_one, back_two, back_three), coefficients)
    rows = resid.shape[0]
    map_high = feature_map[...].astype(BF16)
    spread_map = jnp.concatenate([map_high, feature_ones().astype(BF16)], axis=0)
    share = jnp.full((rows, CHUNK), 1.0 / HEAD_DIM, BF16)
    grads = [[], [], []]
    for chunk in range(resid.shape[1] // CHUNK):
        lanes = lanes_of(chunk, CHUNK)
        feats = lanes_of(chunk, FEAT_CHUNK)
        query = phi_query[:, feats]
        key = phi_key[:, feats]
        values = value[:, lanes]
        both = jnp.concatenate([numer[:, lanes], denom[:, lanes]], axis=1)
        valued = jnp.concatenate([values, share], axis=1)
        query_left, query_right, key_left, key_right, value_left, value_right = [], [], [], [], [], []
        for head in range(4):
            feat_mask = lane_mask(head, FEATS, FEAT_CHUNK)
            mask = lane_mask(head, HEAD_DIM, CHUNK)
            both_mask = jnp.concatenate([mask, mask], axis=1)
            masked_query = query * feat_mask
            masked_both = both * both_mask
            query_left.append((dot_nt(masked_both, valued) * same).astype(BF16))
            query_right.append(key * feat_mask)
            key_left.append((dot_nt(valued, masked_both) * same).astype(BF16))
            key_right.append(masked_query)
            value_left.append((dot_nt(key, masked_query) * same).astype(BF16))
            value_right.append(masked_both[:, :CHUNK])
        forward_edges = spread_edges(totals, chunk)
        backward_edges = spread_edges(back_totals, chunk)
        query_edges = dot_nt(jnp.concatenate([numer[:, lanes], denom[:, lanes] * share], axis=1), forward_edges)
        key_edges = dot_nt(valued, backward_edges)
        query_edges = query_edges[:, :FEAT_CHUNK] * in_first + query_edges[:, FEAT_CHUNK:] * in_last
        key_edges = key_edges[:, :FEAT_CHUNK] * in_first + key_edges[:, FEAT_CHUNK:] * in_last
        value_left.append(edges_of(key, in_first, in_last))
        value_right.append(backward_edges[:, :CHUNK])
        phi_grads = (
            dot_nn(jnp.concatenate(query_left, axis=1), jnp.concatenate(query_right, axis=0)) + query_edges,
            dot_nn(jnp.concatenate(key_left, axis=1), jnp.concatenate(key_right, axis=0)) + key_edges,
        )
        grads[2].append(dot_nn(jnp.concatenate(value_left, axis=1), jnp.concatenate(value_right, axis=0)))
        for which, phi, scaled in ((0, query, query_scaled), (1, key, key_scaled)):
            inner = (phi_grads[which] * phi.astype(F32)).astype(BF16)
            wide = dot_nt(inner, spread_map)
            turned = wide[:, :CHUNK] - scaled[:, lanes] * wide[:, CHUNK:]
            grads[which].append(turned * cosine[...] + swap_halves(turned * sine[...]))
    joined = [jnp.concatenate(item, axis=1).astype(BF16) for item in grads]
    joined.append(context[...].astype(BF16))
    width = resid.shape[1] // 4
    normed_grad = None
    for slot in range(4):
        stacked = jnp.concatenate([item[:, lanes_of(slot, width)] for item in joined], axis=1)
        if slot % 2 == 0:
            stacked_keep[slot // 2] = stacked
        else:
            stacked_send[slot // 2] = stacked
        arrive(waits[slot])
        part = dot_nt(stacked[:, : 3 * width], weight[slot, :, 0 : 3 * width])
        normed_grad = part if normed_grad is None else normed_grad + part
    inward, gain_grad, shift_grad = norm_backward(resid[...], vectors[0:1, :], normed_grad)
    grad_out[...] = middle_grad[...] + inward
    zero_row = jnp.zeros_like(gain_grad)
    vector_out[...] = jnp.concatenate([gain_grad, shift_grad] + [zero_row] * 6, axis=0)


def hidden_grad_kernel(
    upper_own, upper_other, active_own, active_other, normed_own, normed_other, branch_own, branch_other, up_keep,
    up_send, down_keep, down_send
):
    normed = jnp.concatenate([normed_own[...], normed_other[...]], axis=0)
    branch = jnp.concatenate([branch_own[...], branch_other[...]], axis=0)
    for position, up_out, down_out in ((1, up_send, down_send), (0, up_keep, down_keep)):
        upper = jnp.concatenate([upper_own[position], upper_other[position]], axis=0)
        up_out[...] = dot_tn(upper, normed).astype(BF16)
        active = jnp.concatenate([active_own[position], active_other[position]], axis=0)
        down_out[...] = dot_tn(active, branch).astype(BF16)


def attend_grad_kernel(
    stacked_own, stacked_other, normed_own, normed_other, attn_own, attn_other, keep_out, send_out
):
    normed = jnp.concatenate([normed_own[...], normed_other[...]], axis=0)
    attn = jnp.concatenate([attn_own[...], attn_other[...]], axis=0)
    split = 3 * (normed.shape[1] // 4)
    for position, out in ((1, send_out), (0, keep_out)):
        stacked = jnp.concatenate([stacked_own[position], stacked_other[position]], axis=0)
        out[0:split, :] = dot_tn(stacked[:, :split], normed).astype(BF16)
        out[split:, :] = dot_tn(stacked[:, split:], attn).astype(BF16)


def ortho_kernel(pieces, grad_own, grad_other, moment, result, whole):
    index = lax.axis_index("dp")
    size = moment.shape[2]
    width = moment.shape[3]
    eye = (iota((width, width), 0) == iota((width, width), 1)).astype(F32)

    def exact(left, right, dims=(((1,), (0,)), ((), ()))):
        return lax.dot_general(left, right, dims, precision=EXACT, preferred_element_type=F32)

    count = grad_own.shape[0]
    grads, sources, grams, chains, norms = [], [], [], [], []
    for block in range(count):
        grad = grad_own[block].astype(F32) + grad_other[block].astype(F32)
        for piece in range(pieces):
            start = pl.multiple_of((index ^ piece) * size, size) if pieces > 1 else 0
            whole[block, pl.ds(start, size), :] = moment[piece, block].astype(F32)
        source = MOMENTUM_DECAY * whole[block].T + grad
        gram = exact(source, source, (((1,), (1,)), ((), ())))
        trace = jnp.sum(gram * eye)
        norm = jnp.sqrt(trace) + ORTHO_EPSILON
        grads.append(grad)
        sources.append(source)
        norms.append(norm)
        grams.append(gram / (norm * norm))
        chains.append(None)
    for iteration in range(NS_STEPS):
        steps = []
        for block in range(count):
            gram = grams[block]
            steps.append(ORTHO_LINEAR * eye + ORTHO_CUBIC * gram + ORTHO_QUINTIC * exact(gram, gram))
        for block in range(count):
            step = steps[block]
            chains[block] = step if iteration == 0 else exact(chains[block], step)
        if iteration + 1 < NS_STEPS:
            halves = [exact(steps[block], grams[block]) for block in range(count)]
            grams = [exact(halves[block], steps[block]) for block in range(count)]
    for block in range(count):
        ortho = dot_tn(sources[block].astype(BF16), (chains[block] / norms[block]).astype(BF16))
        for which, value in ((0, grads[block].T), (1, ortho)):
            if pieces == 1:
                result[0, block, which] = value.astype(BF16)
            else:
                whole[block] = value
                for piece in range(pieces):
                    start = pl.multiple_of((index ^ piece) * size, size)
                    result[piece, block, which] = whole[block, pl.ds(start, size), :].astype(BF16)


def vmem(count):
    return [pl.BlockSpec(memory_space=pltpu.VMEM)] * count


def anywhere(count):
    return [pl.BlockSpec(memory_space=pl.ANY)] * count


def scalars():
    return [pl.BlockSpec(memory_space=pltpu.SMEM)]


def shape(dims, dtype=F32):
    return jax.ShapeDtypeStruct(dims, dtype)


def call(kernel, name, in_specs, outs, scratch, flops, moved):
    return pl.pallas_call(
        kernel,
        name=name,
        out_shape=outs,
        in_specs=in_specs,
        out_specs=vmem(len(outs)),
        scratch_shapes=scratch,
        cost_estimate=pl.CostEstimate(flops=int(flops), bytes_accessed=int(moved), transcendentals=0),
        compiler_params=pltpu.CompilerParams(vmem_limit_bytes=VMEM_BYTES),
    )


def flat(weight):
    return [item for slot in weight for item in slot]


def copies_of(weight):
    return len(flat(weight)) * (4 if len(weight[0]) > 1 else 1)


def project(resid, vectors, tables, weight):
    rows, width = resid.shape
    refs = flat(weight)
    feats = width // HEAD_DIM * FEATS
    outs = [
        shape((rows, width), BF16),
        shape((rows, feats), BF16),
        shape((rows, feats), BF16),
        shape((rows, width), BF16),
        shape((rows, width)),
        shape((rows, width)),
        shape((2, feats, 2 * HEAD_DIM), BF16),
    ]
    return call(
        partial(project_kernel, len(refs)),
        "project",
        vmem(6) + anywhere(len(refs)),
        outs,
        [pltpu.VMEM((4, width, 640), BF16), pltpu.SemaphoreType.DMA((copies_of(weight),))],
        2 * rows * width * width * 3 * 1.5,
        8 * width * width,
    )(resid, vectors, tables["cosine"], tables["sine"], tables["map"], tables["column"], *refs)


def mix_scratch(width, weight):
    return [
        pltpu.VMEM((4, width, 256), BF16),
        pltpu.VMEM((4, width, width), BF16),
        pltpu.VMEM((4, width, width), BF16),
        pltpu.SemaphoreType.DMA((3 * copies_of(weight),)),
    ]


def mix(resid, vectors, bias, state, received, tables, weights):
    rows, width = resid.shape
    refs = [flat(weight) for weight in weights]
    counts = (len(refs[0]), copies_of(weights[0]))
    pair = (2, rows, width)
    outs = [
        shape((rows, width)),
        shape((rows, width)),
        shape((rows, width)),
        shape((rows, width), BF16),
        shape(pair, BF16),
        shape(pair, BF16),
        shape(pair, BF16),
        shape(pair, BF16),
        shape((rows, width)),
    ]
    return call(
        partial(mix_kernel, counts),
        "mix",
        vmem(11) + scalars() + anywhere(3 * counts[0]),
        outs,
        mix_scratch(width, weights[0]),
        2 * rows * width * width * 12,
        20 * width * width,
    )(
        resid, vectors, bias, state["phi_query"], state["phi_key"], state["value"], tables["column"], tables["row"],
        *received, tables["shares"], *refs[0], *refs[1], *refs[2],
    )


def back_mix(grad, vectors, state, tables, weights):
    rows, width = grad.shape
    refs = [flat(weight) for weight in weights]
    counts = (len(refs[0]), copies_of(weights[0]))
    pair = (2, rows, width)
    feats = width // HEAD_DIM * FEATS
    outs = [
        shape((rows, width), BF16),
        shape(pair, BF16),
        shape(pair, BF16),
        shape((rows, width)),
        shape((rows, width), BF16),
        shape((rows, width), BF16),
        shape((rows, width), BF16),
        shape((2, feats, 2 * HEAD_DIM), BF16),
        shape((8, width)),
        shape((4, width)),
    ]
    return call(
        partial(back_mix_kernel, counts),
        "back_mix",
        vmem(9) + anywhere(3 * counts[0]),
        outs,
        mix_scratch(width, weights[0]),
        2 * rows * width * width * 11,
        20 * width * width,
    )(
        grad, vectors, state["middle"], state["slope_keep"], state["slope_send"], state["inverse"], state["context"],
        state["phi_query"], tables["column"], *refs[0], *refs[1], *refs[2],
    )


def back_project(resid, vectors, state, back, received, back_received, tables, weight):
    rows, width = resid.shape
    refs = flat(weight)
    pair = (2, rows, width)
    outs = [shape(pair, BF16), shape(pair, BF16), shape((rows, width)), shape((8, width))]
    return call(
        partial(back_project_kernel, len(refs)),
        "back_project",
        vmem(22) + scalars() + anywhere(len(refs)),
        outs,
        [pltpu.VMEM((4, width, 640), BF16), pltpu.SemaphoreType.DMA((copies_of(weight),))],
        2 * rows * width * width * 8,
        8 * width * width,
    )(
        resid, vectors, tables["cosine"], tables["sine"], tables["map"], tables["column"], tables["row"],
        state["phi_query"], state["phi_key"], state["value"], state["query"], state["key"], back["numer"],
        back["denom"], state["context"], back["middle_grad"], *received, *back_received, tables["shares"], *refs,
    )


def hidden_grad(*operands):
    width = operands[4].shape[1]
    return call(
        hidden_grad_kernel, "hidden_grad", vmem(8), [shape((width, width), BF16)] * 4, [],
        2 * 512 * width * width * 4, 16 * width * width,
    )(*operands)


def attend_grad(*operands):
    width = operands[2].shape[1]
    return call(
        attend_grad_kernel, "attend_grad", vmem(6), [shape((width, width), BF16)] * 2, [],
        2 * 512 * width * width * 2, 8 * width * width,
    )(*operands)


def orthogonalize(grad_own, grad_other, moment):
    pieces, count, size, width = moment.shape
    return call(
        partial(ortho_kernel, pieces), "orthogonalize", vmem(3), [shape((pieces, count, 2, size, width), BF16)],
        [pltpu.VMEM((count, pieces * size, width), F32)],
        2 * 6 * 20 * count * width**3, 4 * count * width * pieces * size,
    )(grad_own, grad_other, moment)[0]


def doc_tables(segment_row, feature_map, rows):
    index = lax.axis_index("head")
    own = lax.dynamic_slice_in_dim(segment_row, index * rows, rows, 0)
    starts = jnp.sum((segment_row[None, :] < own[:, None]).astype(jnp.int32), axis=1, dtype=jnp.int32)
    offsets = (index * rows + jnp.arange(rows, dtype=jnp.int32) - starts).astype(F32)
    half = HEAD_DIM // 2
    frequency = ROPE_BASE ** (-jnp.arange(half, dtype=F32) / half)
    angles = offsets[:, None] * frequency[None, :]
    scale = HEAD_DIM ** (-0.25)
    cosine = jnp.cos(angles) * scale
    sine = jnp.sin(angles) * scale
    shares = []
    for offset in (1, 2, 3):
        other = index ^ offset
        first = segment_row[other * rows]
        last = segment_row[other * rows + rows - 1]
        shares.append(
            jnp.stack([first == own[0], last == own[0], first == own[rows - 1], last == own[rows - 1]]).astype(F32)
        )
    return {
        "cosine": jnp.tile(cosine, (1, 2 * CHUNK // HEAD_DIM)),
        "sine": jnp.tile(jnp.concatenate([-sine, sine], axis=1), (1, CHUNK // HEAD_DIM)),
        "column": own[:, None],
        "row": own[None, :],
        "shares": jnp.stack(shares),
        "maps": [jnp.kron(jnp.eye(4, dtype=F32), feature_map[layer]) for layer in range(feature_map.shape[0])],
    }


def exchange_edges(summary):
    return [swap_head(summary, offset) for offset in (1, 2, 3)]


def added(left, right):
    return (left.astype(F32) + right.astype(F32)).astype(BF16)


def halve(blocks, bit):
    kept = lax.dynamic_index_in_dim(blocks, bit, 1, keepdims=False)
    sent = lax.dynamic_index_in_dim(blocks, 1 - bit, 1, keepdims=False)
    return kept, sent


def adam_update(parameter, gradient, first_moment, second_moment):
    first_moment = BETA_FIRST * first_moment + (1.0 - BETA_FIRST) * gradient
    second_moment = BETA_SECOND * second_moment + (1.0 - BETA_SECOND) * gradient * gradient
    first_hat = first_moment / (1.0 - BETA_FIRST**STEP)
    second_hat = second_moment / (1.0 - BETA_SECOND**STEP)
    return (
        parameter - ADAM_RATE * first_hat / (jnp.sqrt(second_hat) + ADAM_EPSILON),
        first_moment,
        second_moment,
    )


def split_columns(matrix, width):
    rows = matrix.shape[0]
    return jnp.transpose(matrix.reshape(rows, -1, width), (1, 0, 2))


def join_columns(blocks):
    count, rows, width = blocks.shape
    return jnp.transpose(blocks, (1, 0, 2)).reshape(rows, count * width)


def per_device(
    block_input,
    cotangent,
    marked,
    segments,
    feature_map,
    vectors,
    bias_up,
    w_query_key,
    w_value,
    w_out,
    w_up,
    w_down,
    moment_query_key,
    moment_value,
    moment_out,
    moment_up,
    moment_down,
    vector_first,
    vector_second,
    bias_first,
    bias_second,
):
    layers = w_value.shape[0]
    block = w_value.shape[2]
    rows = block_input.shape[0]
    dp_size = lax.axis_size("dp")
    dp_index = lax.axis_index("dp")
    quick = dp_size == 8

    gathered = []
    for layer in range(layers):
        attend_part = jnp.concatenate(
            [w_query_key[layer, :, 0], w_query_key[layer, :, 1], w_value[layer], w_out[layer].T], axis=1
        ).astype(BF16)
        up_part = w_up[layer].astype(BF16)
        down_part = w_down[layer].T.astype(BF16)
        gathered.append(
            (
                gather_weight(attend_part, layer % 2 == 0),
                gather_weight(up_part, True),
                gather_weight(down_part, False),
            )
        )
    bias_slots = [bias_up] + [swap_head(bias_up, offset) for offset in (1, 2, 3)]
    biases = [jnp.stack([item[layer] for item in bias_slots]) for layer in range(layers)]

    moments = (moment_query_key, moment_value, moment_out, moment_up, moment_down)
    old_blocks = []
    for layer in range(layers):
        attend_blocks = jnp.stack(
            [
                moment_query_key[layer, :, 0],
                moment_query_key[layer, :, 1],
                moment_value[layer],
                moment_out[layer].T,
            ]
        )
        hidden_blocks = jnp.concatenate(
            [split_columns(moment_up[layer], block), split_columns(moment_down[layer].T, block)]
        )
        old_blocks.append((attend_blocks.astype(BF16), hidden_blocks.astype(BF16)))

    tables = doc_tables(segments[0], feature_map, rows)
    resid = block_input.astype(F32)
    inputs = []
    states = []
    summaries = []
    for layer in range(layers):
        own = dict(tables, map=tables["maps"][layer])
        inputs.append(resid)
        normed, phi_query, phi_key, value, query, key, summary = project(
            resid, vectors[layer], own, gathered[layer][0]
        )
        state = {
            "normed": normed, "phi_query": phi_query, "phi_key": phi_key, "value": value, "query": query, "key": key
        }
        received = exchange_edges(summary)
        (state["context"], state["inverse"], state["middle"], state["normed_two"], state["slope_keep"],
         state["slope_send"], state["active_keep"], state["active_send"], resid) = mix(
            resid, vectors[layer], biases[layer], state, received, own, gathered[layer]
        )
        states.append(state)
        summaries.append(received)
    activations = resid.astype(BF16)

    if quick:
        payloads = []
        for offset in range(8):
            owner = dp_index ^ offset
            payloads.append(
                jnp.stack(
                    [
                        part
                        for layer in range(layers)
                        for part in (
                            lax.dynamic_index_in_dim(old_blocks[layer][0], owner & 3, 0, keepdims=False),
                            lax.dynamic_index_in_dim(old_blocks[layer][1], owner, 0, keepdims=False),
                        )
                    ]
                )
            )
        owned_moments = jnp.stack(
            [payloads[0]] + [swap_dp(payloads[offset], offset) for offset in range(1, 8)]
        )

    gradient = cotangent.astype(F32) * marked[0][:, None].astype(F32)
    vector_grads = [None] * layers
    bias_grads = [None] * layers
    results = [None] * layers
    raw = [None] * layers
    for layer in reversed(range(layers)):
        own = dict(tables, map=tables["maps"][layer])
        state = states[layer]
        (branch, upper_keep, upper_send, middle_grad, attn, numer, denom, back_summary, vector_two,
         bias_grads[layer]) = back_mix(gradient, vectors[layer], state, own, gathered[layer])
        back = {"numer": numer, "denom": denom, "middle_grad": middle_grad}
        back_received = exchange_edges(back_summary)
        stacked_keep, stacked_send, gradient, vector_one = back_project(
            inputs[layer], vectors[layer], state, back, summaries[layer], back_received, own, gathered[layer][0]
        )
        vector_grads[layer] = (vector_one + vector_two)[:5]
        up_keep, up_send, down_keep, down_send = hidden_grad(
            upper_keep, swap_head(upper_send, 1), state["active_keep"], swap_head(state["active_send"], 1),
            state["normed_two"], swap_head(state["normed_two"], 1), branch, swap_head(branch, 1),
        )
        attend_keep, attend_send = attend_grad(
            stacked_keep, swap_head(stacked_send, 1), state["normed"], swap_head(state["normed"], 1),
            attn, swap_head(attn, 1),
        )
        if not quick:
            attend_sum = added(attend_keep, swap_head(attend_send, 2))
            up_sum = added(up_keep, swap_head(up_send, 2))
            down_sum = added(down_keep, swap_head(down_send, 2))
            raw[layer] = jnp.concatenate([attend_sum, up_sum, down_sum]).reshape(-1, block, attend_sum.shape[1])
            continue
        y_bit, near_bit, far_bit = dp_index & 1, (dp_index >> 1) & 1, dp_index >> 2
        view = (2, 2, block, up_keep.shape[1])
        up_sum = added(up_keep, swap_head(up_send, 2)).reshape(view)
        kept, sent = halve(up_sum, y_bit)
        up_sum = added(kept, swap_dp(sent, 1))
        down_sums = []
        for part in (down_send, down_keep):
            kept, sent = halve(part.reshape(view), y_bit)
            down_sums.append(added(kept, swap_dp(sent, 1)))
        down_sum = added(down_sums[1], swap_head(down_sums[0], 2))
        hidden = jnp.stack([up_sum, down_sum])
        kept, sent = halve(hidden, near_bit)
        hidden = added(kept, swap_dp(sent, 2))
        hidden_own = lax.dynamic_index_in_dim(hidden, far_bit, 0, keepdims=False)
        hidden_other = swap_dp(lax.dynamic_index_in_dim(hidden, 1 - far_bit, 0, keepdims=False), 4)
        attend_sum = added(attend_keep, swap_head(attend_send, 2)).reshape(view)
        kept, sent = halve(attend_sum, y_bit)
        attend_sum = added(kept, swap_dp(sent, 1))[None]
        kept, sent = halve(attend_sum, near_bit)
        attend_own = added(kept, swap_dp(sent, 2))[0]
        attend_other = swap_dp(attend_own, 4)
        sent_back = orthogonalize(
            jnp.stack([attend_own, hidden_own]),
            jnp.stack([attend_other, hidden_other]),
            owned_moments[:, 2 * layer : 2 * layer + 2],
        )
        hidden_back = jnp.stack(
            [sent_back[0, 1]] + [swap_dp(sent_back[offset, 1], offset) for offset in range(1, 8)]
        )
        attend_back = jnp.stack(
            [sent_back[0, 0]] + [swap_dp(sent_back[offset, 0], offset) for offset in range(1, 4)]
        )
        results[layer] = jnp.stack(
            [lax.dynamic_index_in_dim(attend_back, position ^ (dp_index & 3), 0, keepdims=False) for position in range(4)]
            + [lax.dynamic_index_in_dim(hidden_back, position ^ dp_index, 0, keepdims=False) for position in range(8)]
        )
    if not quick:
        count = layers * raw[0].shape[0]
        padded = -(-count // dp_size) * dp_size
        grads = jnp.concatenate(raw)
        grads = jnp.concatenate([grads, jnp.zeros((padded - count,) + grads.shape[1:], grads.dtype)])
        grads = lax.psum_scatter(grads.astype(F32), "dp", scatter_dimension=0, tiled=True)
        old = jnp.concatenate([part for pair in old_blocks for part in pair])
        old = jnp.concatenate([old, jnp.zeros((padded - count,) + old.shape[1:], old.dtype)])
        old = lax.all_to_all(old, "dp", split_axis=0, concat_axis=1, tiled=True)
        back = orthogonalize(grads, jnp.zeros_like(grads), old[None])[0]
        back = lax.all_to_all(back, "dp", split_axis=2, concat_axis=0, tiled=True)
        results = [back[layer * 12 : (layer + 1) * 12] for layer in range(layers)]

    vector_stack = jnp.stack(vector_grads)
    bias_stack = jnp.stack(bias_grads)
    keep, send = bias_stack[:, 0::2], bias_stack[:, 1::2]
    vector_stack, keep = jax.tree.map(
        lambda mine, other: mine + swap_head(other, 1), (vector_stack, keep), (vector_stack, send)
    )
    keep, send = keep[:, 0], keep[:, 1]
    vector_total, bias_total = jax.tree.map(
        lambda mine, other: mine + swap_head(other, 2), (vector_stack, keep), (vector_stack, send)
    )
    if quick:
        packed = jnp.concatenate([vector_total.reshape(-1, vector_total.shape[2]), bias_total])
        for offset in (1, 2, 4):
            packed = packed + swap_dp(packed, offset)
        vector_total = packed[: 5 * layers].reshape(vector_total.shape)
        bias_total = packed[5 * layers :]
    else:
        vector_total, bias_total = lax.psum((vector_total, bias_total), "dp")

    fresh = []
    for which in range(2):
        parts = [result[:, which].astype(F32) for result in results]
        fresh.append(
            (
                jnp.stack([jnp.stack([part[0], part[1]], axis=1) for part in parts]),
                jnp.stack([part[2] for part in parts]),
                jnp.stack([part[3].T for part in parts]),
                jnp.stack([join_columns(part[4:8]) for part in parts]),
                jnp.stack([join_columns(part[8:12]).T for part in parts]),
            )
        )
    next_moments = tuple(MOMENTUM_DECAY * old + grad for old, grad in zip(moments, fresh[0]))
    muon_scale = (w_value.shape[1] * dp_size / block) ** 0.5
    masters = (w_query_key, w_value, w_out, w_up, w_down)
    next_masters = tuple(
        master * (1.0 - MUON_RATE * WEIGHT_DECAY) - MUON_RATE * muon_scale * ortho
        for master, ortho in zip(masters, fresh[1])
    )
    copies = tuple(master.astype(BF16) for master in next_masters)
    vectors_next, vector_first_next, vector_second_next = adam_update(
        vectors, vector_total, vector_first, vector_second
    )
    bias_next, bias_first_next, bias_second_next = adam_update(bias_up, bias_total, bias_first, bias_second)
    return (
        (activations, gradient)
        + next_masters
        + next_moments
        + copies
        + (vectors_next, vector_first_next, vector_second_next, bias_next, bias_first_next, bias_second_next)
    )


def solution(mesh):
    shards = (
        P(None, "dp", None, "head"),
        P(None, "dp", "head"),
        P(None, "head", "dp"),
        P(None, "dp", "head"),
        P(None, "head", "dp"),
    )
    rows = P(("dp", "head"), None)
    placed = (
        (rows, rows, P("dp", "head"), P("dp", None), P(), P(), P(None, "head"))
        + shards
        + shards
        + (P(), P(), P(None, "head"), P(None, "head"))
    )
    return jax.shard_map(
        per_device,
        mesh=mesh,
        in_specs=placed,
        out_specs=(rows, rows) + shards + shards + shards + (P(), P(), P()) + (P(None, "head"),) * 3,
        check_vma=False,
    )
```

```python
from functools import partial

import jax
import jax.numpy as jnp
from jax import lax
from jax.experimental import pallas as pl
from jax.experimental.pallas import tpu as pltpu
from jax.sharding import PartitionSpec as P

HEAD_DIM = 64
FEATS = 32
NS_STEPS = 5
STEP = 10


ORTHO_LINEAR = 3.4445
ORTHO_CUBIC = -4.775
ORTHO_QUINTIC = 2.0315
ORTHO_EPSILON = 1e-07
MOMENTUM_DECAY = 0.95
MUON_RATE = 0.2
WEIGHT_DECAY = 0.1
BETA_FIRST = 0.9
BETA_SECOND = 0.99
ADAM_RATE = 0.2
ADAM_EPSILON = 1e-08
NORM_EPSILON = 1e-05
ATTEND_EPSILON = 1e-06
ROPE_BASE = 10000.0
EXACT = lax.Precision.HIGHEST

F32 = jnp.float32
BF16 = jnp.bfloat16
CHUNK = 4 * HEAD_DIM
FEAT_CHUNK = 4 * FEATS
TOTAL_ROWS = 16
VMEM_BYTES = 56 * 1024 * 1024


def dot_nn(left, right):
    return lax.dot_general(left, right, (((1,), (0,)), ((), ())), preferred_element_type=F32)


def dot_nt(left, right):
    return lax.dot_general(left, right, (((1,), (1,)), ((), ())), preferred_element_type=F32)


def dot_tn(left, right):
    return lax.dot_general(left, right, (((0,), (0,)), ((), ())), preferred_element_type=F32)


def iota(shape, axis):
    return lax.broadcasted_iota(jnp.int32, shape, axis)


def swap_head(values, offset):
    return lax.ppermute(values, "head", [(h, h ^ offset) for h in range(lax.axis_size("head"))])


def swap_dp(values, offset):
    return lax.ppermute(values, "dp", [(d, d ^ offset) for d in range(lax.axis_size("dp"))])


def swap_all(items, swap, offset):
    return [swap(item, offset) for item in items]


def swap_line(parts):
    groups = [[z * 2 + y for z in range(4)] for y in range(2)]
    return lax.all_to_all(parts, "dp", split_axis=0, concat_axis=0, axis_index_groups=groups, tiled=True)


def gather_line(part):
    return swap_line(jnp.broadcast_to(part[None], (4,) + part.shape))


def swap_owners(parts):
    return lax.all_to_all(parts, "dp", split_axis=0, concat_axis=0, tiled=True)


def hold(*values):
    return lax.optimization_barrier(values)


def sources(kind, slot, rows):
    core, across = slot & 1, slot >> 1
    if kind == "whole":
        return [(slot, 0, 1, 0)]
    if "up" in kind:
        return [(slot, 0, 4, 0), (slot, rows // 2, 4, 1)]
    return [(core, across * rows // 2, 4, 0), (2 + core, across * rows // 2, 4, 1)]


def fetch(refs, plan, scratch, sems, base, lanes):
    index = lax.axis_index("dp")
    waits = [[], [], [], []]
    count = base
    for position, (kind, source_lane, lane, width) in enumerate(plan):
        first, last = max(lane, lanes[0]), min(lane + width, lanes[1])
        if first >= last:
            continue
        for slot in range(4):
            for array, row, pieces, y_offset in sources(kind, slot, scratch.shape[1]):
                ref = refs[4 * position + array]
                size = scratch.shape[1] // (2 * pieces) if pieces > 1 else scratch.shape[1]
                for piece in range(pieces):
                    start = 0
                    if pieces > 1:
                        place = 2 * piece + ((index & 1) ^ y_offset)
                        if "near" in kind:
                            place = index ^ (2 * piece + y_offset)
                        start = pl.multiple_of(place * size, 16)
                    copy = pltpu.make_async_copy(
                        ref.at[pl.ds(row + piece * size, size), pl.ds(source_lane + first - lane, last - first)],
                        scratch.at[slot, pl.ds(start, size), pl.ds(first - lanes[0], last - first)],
                        sems.at[count],
                    )
                    copy.start()
                    waits[slot].append(copy)
                    count += 1
    return waits


def ref_count(plan):
    return 4 * len(plan)


def copy_count(plan):
    return sum(4 if run[0] == "whole" else 32 for run in plan)


def take(refs, *plans):
    taken = []
    for plan in plans:
        taken.append(refs[: ref_count(plan)])
        refs = refs[ref_count(plan) :]
    return (*taken, refs)


def arrive(copies):
    for copy in copies:
        copy.wait()


def norm_parts(values):
    row_mean = jnp.mean(values, axis=-1, keepdims=True)
    centred = values - row_mean
    variance = jnp.mean(centred * centred, axis=-1, keepdims=True)
    scale = lax.rsqrt(variance + NORM_EPSILON)
    return centred * scale, scale


def norm_backward(values, gain, incoming):
    unit, scale = norm_parts(values)
    gain_grad = jnp.sum(incoming * unit, axis=0, keepdims=True)
    shift_grad = jnp.sum(incoming, axis=0, keepdims=True)
    inner = incoming * gain
    inner_mean = jnp.mean(inner, axis=-1, keepdims=True)
    along = jnp.mean(inner * unit, axis=-1, keepdims=True)
    return scale * (inner - inner_mean - unit * along), gain_grad, shift_grad


def swap_halves(values):
    width = values.shape[1]
    half = HEAD_DIM // 2
    lower = iota(values.shape, 1) % HEAD_DIM < half
    return jnp.where(lower, pltpu.roll(values, width - half, 1), pltpu.roll(values, half, 1))


def split_low(values):
    high = values.astype(BF16)
    return high, (values - high.astype(F32)).astype(BF16)


def lane_mask(index, per_head, width):
    return (iota((1, width), 1) // per_head == index).astype(BF16)


def turn_tables(cosine, sine):
    part, other = cosine[...], sine[...]
    return (
        jnp.concatenate([part] * (2 * CHUNK // HEAD_DIM), axis=1),
        jnp.concatenate([-other, other] * (CHUNK // HEAD_DIM), axis=1),
    )


def wide_map(feature_map):
    tall = jnp.concatenate([feature_map[...]] * 4, axis=0)
    return jnp.where(feature_ones(), jnp.concatenate([tall] * 4, axis=1), 0.0)


def feature_ones():
    return iota((CHUNK, FEAT_CHUNK), 0) // HEAD_DIM == iota((CHUNK, FEAT_CHUNK), 1) // FEATS


def features(values, map_high, map_low):
    high, low_part = split_low(values)
    square_high, square_low = split_low(0.5 * values * values)
    ones = -feature_ones().astype(BF16)
    left = jnp.concatenate([high, low_part, high, square_high, square_low], axis=1)
    right = jnp.concatenate([map_high, map_high, map_low, ones, ones], axis=0)
    return jnp.exp(dot_nn(left, right)) * FEATS ** (-0.5)


def fold_matrix():
    rows, columns = iota((CHUNK, HEAD_DIM), 0), iota((CHUNK, HEAD_DIM), 1)
    return (rows % HEAD_DIM == columns).astype(BF16)


def spread_matrix():
    rows = iota((2 * HEAD_DIM, 2 * CHUNK), 0)
    columns = iota((2 * HEAD_DIM, 2 * CHUNK), 1)
    return (columns // CHUNK * HEAD_DIM + columns % HEAD_DIM == rows).astype(BF16)


def same_head(feature_rows):
    shape = (feature_rows, 2 * CHUNK)
    return iota(shape, 0) % FEAT_CHUNK // FEATS == iota(shape, 1) % CHUNK // HEAD_DIM


def edge_masks(segment_column):
    first = segment_column[0:1, :]
    last = segment_column[segment_column.shape[0] - 1 :, :]
    in_first = (segment_column == first).astype(F32)
    in_last = (segment_column == last).astype(F32) * (1.0 - in_first)
    return in_first, in_last


def edge_summary(edges, weighted):
    full = dot_tn(edges, weighted)
    full = jnp.where(same_head(2 * FEAT_CHUNK)[:, :CHUNK], full, 0.0).astype(BF16)
    folded = dot_nn(full, fold_matrix())
    return jnp.concatenate([folded[:FEAT_CHUNK], folded[FEAT_CHUNK:]], axis=1).astype(BF16)


def store_totals(summary_out, rows):
    pieces = [piece for row in rows for piece in (row[:, :FEAT_CHUNK], row[:, FEAT_CHUNK:])]
    pieces.append(jnp.zeros((TOTAL_ROWS - len(pieces), FEAT_CHUNK), F32))
    summary_out[summary_out.shape[0] - TOTAL_ROWS :, :] = jnp.concatenate(pieces, axis=0).astype(BF16)


def edges_of(phi, in_first, in_last):
    wide = phi.astype(F32)
    return jnp.concatenate([wide * in_first, wide * in_last], axis=1).astype(BF16)


def open_edges(ref, which):
    feats = ref.shape[0] - TOTAL_ROWS
    totals = ref[feats:, :]
    columns = []
    for chunk in range(feats // FEAT_CHUNK):
        pick = (iota((TOTAL_ROWS, HEAD_DIM), 0) == 2 * chunk + which).astype(BF16)
        columns.append(dot_tn(totals, pick))
    sums = ref[:feats, lanes_of(which, HEAD_DIM)].astype(F32)
    return jnp.concatenate([sums, jnp.concatenate(columns, axis=0)], axis=1)


def combine_edges(received, coefficients):
    totals = [None, None]
    rows = (received[0].shape[0] - TOTAL_ROWS) // 4
    for position, ref in enumerate(received):
        offset = position + 1
        pair = []
        for which in range(2):
            value = open_edges(ref, which)
            pair.append(
                jnp.concatenate(
                    [value[(slot ^ offset) * rows : ((slot ^ offset) + 1) * rows] for slot in range(4)], axis=0
                )
            )
        for which in range(2):
            part = coefficients[position, 2 * which] * pair[0] + coefficients[position, 2 * which + 1] * pair[1]
            totals[which] = part if totals[which] is None else totals[which] + part
    return totals


def spread_edges(totals, chunk):
    rows = slice(chunk * FEAT_CHUNK, (chunk + 1) * FEAT_CHUNK)
    joined = jnp.concatenate([totals[0][rows], totals[1][rows]], axis=0).astype(BF16)
    return jnp.where(same_head(2 * FEAT_CHUNK), dot_nn(joined, spread_matrix()), 0.0).astype(BF16)


def lanes_of(slot, width):
    return slice(slot * width, (slot + 1) * width)


def project_kernel(plan, resid, vectors, cosine_part, sine_part, feature_map, segment_column, *rest):
    weight_refs, rest = take(rest, plan)
    phi_query_out, phi_key_out, value_out, query_out, key_out, summary_out, weight, sems = rest
    waits = fetch(weight_refs, plan, weight, sems, 0, (0, weight.shape[2]))
    cosine, sine = turn_tables(cosine_part, sine_part)
    unit, _ = norm_parts(resid[...])
    normed = (unit * vectors[0:1, :] + vectors[1:2, :]).astype(BF16)
    width = resid.shape[1] // 4
    pieces = [[], [], []]
    for slot in range(4):
        arrive(waits[slot])
        product = dot_nn(normed, weight[slot, :, 0 : 3 * width])
        for which in range(3):
            pieces[which].append(product[:, lanes_of(which, width)])
    queries, key_rows, value_rows = (jnp.concatenate(piece, axis=1) for piece in pieces)
    value_rows = value_rows.astype(BF16)
    value_out[...] = value_rows
    map_high, map_low = split_low(wide_map(feature_map))
    in_first, in_last = edge_masks(segment_column[...])
    totals = []
    for chunk in range(resid.shape[1] // CHUNK):
        lanes = lanes_of(chunk, CHUNK)
        feats = lanes_of(chunk, FEAT_CHUNK)
        turned = []
        for source, scaled_out, phi_out in (
            (queries, query_out, phi_query_out),
            (key_rows, key_out, phi_key_out),
        ):
            part = source[:, lanes]
            scaled = part * cosine + swap_halves(part) * sine
            scaled_out[:, lanes] = scaled
            phi = features(scaled, map_high, map_low).astype(BF16)
            phi_out[:, feats] = phi
            turned.append(phi)
        edges = edges_of(turned[1], in_first, in_last)
        summary_out[feats, :] = edge_summary(edges, value_rows[:, lanes])
        totals.append(jnp.sum(edges.astype(F32), axis=0, keepdims=True))
    store_totals(summary_out, totals)


def mix_kernel(
    plans, resid, vectors, bias, phi_query, phi_key, value, segment_column, segment_row, recv_one, recv_two,
    recv_three, coefficients, *rest
):
    out_refs, up_refs, down_refs, rest = take(rest, *plans)
    (context_out, inverse_out, middle_out, slope_out, active_keep, pack_out, resid_out, out_weight, up_weight,
     down_weight, sems) = rest
    bases = [0, copy_count(plans[0]), copy_count(plans[0]) + copy_count(plans[1])]
    out_waits = fetch(out_refs, plans[0], out_weight, sems, bases[0], (512, 768))
    up_waits = fetch(up_refs, plans[1], up_weight, sems, bases[1], (0, 768))
    down_waits = fetch(down_refs, plans[2], down_weight, sems, bases[2], (0, 768))
    same = (segment_column[...] == segment_row[...]).astype(F32)
    in_first, in_last = edge_masks(segment_column[...])
    totals = combine_edges((recv_one, recv_two, recv_three), coefficients)
    rows = resid.shape[0]
    contexts = []
    for chunk in range(resid.shape[1] // CHUNK):
        lanes = lanes_of(chunk, CHUNK)
        feats = lanes_of(chunk, FEAT_CHUNK)
        query = phi_query[:, feats]
        key = phi_key[:, feats]
        values = value[:, lanes]
        left = []
        right = []
        for head in range(4):
            scores = dot_nt(query * lane_mask(head, FEATS, FEAT_CHUNK), key)
            left.append((scores * same).astype(BF16))
            mask = lane_mask(head, HEAD_DIM, CHUNK)
            right.append(jnp.concatenate([values * mask, jnp.broadcast_to(mask, (rows, CHUNK))], axis=1))
        left.append(edges_of(query, in_first, in_last))
        right.append(spread_edges(totals, chunk))
        both = dot_nn(jnp.concatenate(left, axis=1), jnp.concatenate(right, axis=0))
        inverse = 1.0 / (both[:, CHUNK:] + ATTEND_EPSILON)
        context = both[:, :CHUNK] * inverse
        inverse_out[:, lanes] = inverse
        context_out[:, lanes] = context
        contexts.append(context.astype(BF16))
    context = jnp.concatenate(contexts, axis=1)
    width = resid.shape[1] // 4
    middle = resid[...]
    for slot in range(4):
        arrive(out_waits[slot])
        middle = middle + dot_nt(context[:, lanes_of(slot, width)], out_weight[slot, :, 64:])
    middle_out[...] = middle
    unit, _ = norm_parts(middle)
    normed = (unit * vectors[2:3, :] + vectors[3:4, :]).astype(BF16)
    pack_out[2] = normed
    output = middle + vectors[4:5, :]
    for slot in range(4):
        arrive(up_waits[slot])
        upper = dot_nn(normed, up_weight[slot]) + bias[slot : slot + 1, :]
        below = 0.5 * (1.0 + lax.erf(upper * 2.0**-0.5))
        slope = below + upper * (jnp.exp(-0.5 * upper * upper) * 0.3989422804014327)
        active = (upper * below).astype(BF16)
        slope_out[slot] = slope.astype(BF16)
        if slot % 2 == 0:
            active_keep[slot // 2] = active
        else:
            pack_out[slot // 2] = active
        arrive(down_waits[slot])
        output = output + dot_nt(active, down_weight[slot])
    resid_out[...] = output


def back_mix_kernel(
    plans, grad, vectors, middle, slope, inverse, context, phi_query, segment_column, *rest
):
    out_refs, up_refs, down_refs, rest = take(rest, *plans)
    (upper_keep, pack_out, middle_grad_out, numer_out, denom_out, summary_out, vector_out,
     bias_out, out_weight, up_weight, down_weight, sems) = rest
    bases = [0, copy_count(plans[0]), copy_count(plans[0]) + copy_count(plans[1])]
    down_waits = fetch(down_refs, plans[2], down_weight, sems, bases[2], (0, 768))
    up_waits = fetch(up_refs, plans[1], up_weight, sems, bases[1], (0, 768))
    out_waits = fetch(out_refs, plans[0], out_weight, sems, bases[0], (512, 768))
    grad_out = grad[...]
    branch = grad_out.astype(BF16)
    shift_out = jnp.sum(branch.astype(F32), axis=0, keepdims=True)
    normed_grad = None
    for slot in range(4):
        arrive(down_waits[slot])
        hidden = dot_nn(branch, down_weight[slot])
        upper = (hidden * slope[slot].astype(F32)).astype(BF16)
        if slot % 2 == 0:
            upper_keep[slot // 2] = upper
        else:
            pack_out[slot // 2] = upper
        bias_out[slot : slot + 1, :] = jnp.sum(upper.astype(F32), axis=0, keepdims=True)
        arrive(up_waits[slot])
        part = dot_nt(upper, up_weight[slot])
        normed_grad = part if normed_grad is None else normed_grad + part
    inward, gain_grad, shift_grad = norm_backward(middle[...], vectors[2:3, :], normed_grad)
    middle_grad = grad_out + inward
    middle_grad_out[...] = middle_grad
    attn = middle_grad.astype(BF16)
    pack_out[2] = attn
    zero_row = jnp.zeros_like(shift_out)
    vector_out[...] = jnp.concatenate([zero_row, zero_row, gain_grad, shift_grad, shift_out] + [zero_row] * 3, axis=0)
    pieces = []
    for slot in range(4):
        arrive(out_waits[slot])
        pieces.append(dot_nn(attn, out_weight[slot, :, 64:]))
    context_grad = jnp.concatenate(pieces, axis=1)
    in_first, in_last = edge_masks(segment_column[...])
    head_ones = (iota((CHUNK, CHUNK), 0) // HEAD_DIM == iota((CHUNK, CHUNK), 1) // HEAD_DIM).astype(BF16)
    one_lane = (iota((CHUNK, FEAT_CHUNK), 0) == iota((CHUNK, FEAT_CHUNK), 1) // FEATS * HEAD_DIM).astype(BF16)
    totals = []
    for chunk in range(grad.shape[1] // CHUNK):
        lanes = lanes_of(chunk, CHUNK)
        feats = lanes_of(chunk, FEAT_CHUNK)
        numer = context_grad[:, lanes] * inverse[:, lanes]
        denom = -dot_nn((numer * context[:, lanes]).astype(BF16), head_ones)
        numer = numer.astype(BF16)
        denom = denom.astype(BF16)
        numer_out[:, lanes] = numer
        denom_out[:, lanes] = denom
        edges = edges_of(phi_query[:, feats], in_first, in_last)
        summary_out[feats, :] = edge_summary(edges, numer)
        heads = dot_nn(denom, one_lane)
        weighted = edges.astype(F32) * jnp.concatenate([heads, heads], axis=1)
        totals.append(jnp.sum(weighted, axis=0, keepdims=True))
    store_totals(summary_out, totals)


def back_project_kernel(
    plan, resid, vectors, cosine_part, sine_part, feature_map, segment_column, segment_row, phi_query, phi_key, value,
    query_scaled, key_scaled, numer, denom, context, middle_grad, recv_one, recv_two, recv_three, back_one,
    back_two, back_three, coefficients, *rest
):
    weight_refs, rest = take(rest, plan)
    stacked_keep, pack_out, grad_out, vector_out, weight, sems = rest
    waits = fetch(weight_refs, plan, weight, sems, 0, (0, weight.shape[2]))
    cosine, sine = turn_tables(cosine_part, sine_part)
    unit, _ = norm_parts(resid[...])
    pack_out[2] = (unit * vectors[0:1, :] + vectors[1:2, :]).astype(BF16)
    same = (segment_column[...] == segment_row[...]).astype(F32)
    in_first, in_last = edge_masks(segment_column[...])
    totals = combine_edges((recv_one, recv_two, recv_three), coefficients)
    back_totals = combine_edges((back_one, back_two, back_three), coefficients)
    rows = resid.shape[0]
    map_high, map_low = split_low(wide_map(feature_map))
    spread_high = jnp.concatenate([map_high, feature_ones().astype(BF16)], axis=0)
    spread_low = jnp.concatenate([map_low, jnp.zeros_like(map_low)], axis=0)
    spread_map = jnp.concatenate([spread_high, spread_high, spread_low], axis=1)
    share = jnp.full((rows, CHUNK), 1.0 / HEAD_DIM, BF16)
    grads = [[], [], []]
    for chunk in range(resid.shape[1] // CHUNK):
        lanes = lanes_of(chunk, CHUNK)
        feats = lanes_of(chunk, FEAT_CHUNK)
        query = phi_query[:, feats]
        key = phi_key[:, feats]
        values = value[:, lanes]
        both = jnp.concatenate([numer[:, lanes], denom[:, lanes]], axis=1)
        valued = jnp.concatenate([values, share], axis=1)
        query_left, query_right, key_left, key_right, value_left, value_right = [], [], [], [], [], []
        for head in range(4):
            feat_mask = lane_mask(head, FEATS, FEAT_CHUNK)
            mask = lane_mask(head, HEAD_DIM, CHUNK)
            both_mask = jnp.concatenate([mask, mask], axis=1)
            masked_query = query * feat_mask
            masked_both = both * both_mask
            query_left.append((dot_nt(masked_both, valued) * same).astype(BF16))
            query_right.append(key * feat_mask)
            key_left.append((dot_nt(valued, masked_both) * same).astype(BF16))
            key_right.append(masked_query)
            value_left.append((dot_nt(key, masked_query) * same).astype(BF16))
            value_right.append(masked_both[:, :CHUNK])
        forward_edges = spread_edges(totals, chunk)
        backward_edges = spread_edges(back_totals, chunk)
        query_edges = dot_nt(jnp.concatenate([numer[:, lanes], denom[:, lanes] * share], axis=1), forward_edges)
        key_edges = dot_nt(valued, backward_edges)
        query_edges = query_edges[:, :FEAT_CHUNK] * in_first + query_edges[:, FEAT_CHUNK:] * in_last
        key_edges = key_edges[:, :FEAT_CHUNK] * in_first + key_edges[:, FEAT_CHUNK:] * in_last
        value_left.append(edges_of(key, in_first, in_last))
        value_right.append(backward_edges[:, :CHUNK])
        phi_grads = (
            dot_nn(jnp.concatenate(query_left, axis=1), jnp.concatenate(query_right, axis=0)) + query_edges,
            dot_nn(jnp.concatenate(key_left, axis=1), jnp.concatenate(key_right, axis=0)) + key_edges,
        )
        grads[2].append(dot_nn(jnp.concatenate(value_left, axis=1), jnp.concatenate(value_right, axis=0)))
        for which, phi, scaled in ((0, query, query_scaled), (1, key, key_scaled)):
            high, low_part = split_low(phi_grads[which] * phi.astype(F32))
            wide = dot_nt(jnp.concatenate([high, low_part, high], axis=1), spread_map)
            turned = wide[:, :CHUNK] - scaled[:, lanes] * wide[:, CHUNK:]
            grads[which].append(turned * cosine + swap_halves(turned * sine))
    joined = [jnp.concatenate(item, axis=1).astype(BF16) for item in grads]
    joined.append(context[...].astype(BF16))
    width = resid.shape[1] // 4
    normed_grad = None
    for slot in range(4):
        stacked = jnp.concatenate([item[:, lanes_of(slot, width)] for item in joined], axis=1)
        if slot % 2 == 0:
            stacked_keep[slot // 2] = stacked
        else:
            pack_out[slot // 2] = stacked
        arrive(waits[slot])
        part = dot_nt(stacked[:, : 3 * width], weight[slot, :, 0 : 3 * width])
        normed_grad = part if normed_grad is None else normed_grad + part
    inward, gain_grad, shift_grad = norm_backward(resid[...], vectors[0:1, :], normed_grad)
    below = middle_grad[...] + inward
    grad_out[...] = below
    pack_out[3] = below.astype(BF16)
    zero_row = jnp.zeros_like(gain_grad)
    vector_out[...] = jnp.concatenate([gain_grad, shift_grad] + [zero_row] * 6, axis=0)


def grad_kernel(quick, splits, right_own, right_other, *rest):
    lefts, (up_keep, up_send, down_keep, down_send, whole) = rest[: 2 * len(splits)], rest[2 * len(splits) :]
    y_bit = lax.axis_index("dp") & 1
    size = up_keep.shape[1]
    joined = []
    for position, (_, own_entry, other_entry) in enumerate(splits):
        own, other = lefts[2 * position], lefts[2 * position + 1]
        own = own[...] if own_entry is None else own[own_entry]
        other = other[...] if other_entry is None else other[other_entry]
        joined.append(jnp.concatenate([own, other], axis=0))
    for position, up_out, down_out in ((1, up_send, down_send), (0, up_keep, down_keep)):
        right = jnp.concatenate([right_own[position], right_other[position]], axis=0)
        start = 0
        for (columns, _, _), left in zip(splits, joined):
            whole[start : start + columns] = dot_tn(right[:, start : start + columns], left).astype(BF16)
            start += columns
        for part in range(2):
            up_out[part] = whole[part * size : (part + 1) * size]
        if not quick:
            for part in range(2):
                down_out[part] = whole[(2 + part) * size : (3 + part) * size]
            continue
        for bit, out in ((y_bit, down_keep), (1 - y_bit, down_send)):
            out[position] = whole[pl.ds(pl.multiple_of((2 + bit) * size, size), size), :]


def sum_of(left, right):
    return (left.astype(F32) + right.astype(F32)).astype(BF16)


def merge_first_kernel(up, up_other, down, down_other, up_keep, up_send, down_keep, down_send):
    y_bit = lax.axis_index("dp") & 1
    up_keep[...] = sum_of(up[y_bit], up_other[y_bit])
    up_send[...] = sum_of(up[1 - y_bit], up_other[1 - y_bit])
    down_keep[...] = sum_of(down[0], down_other[0])
    down_send[...] = sum_of(down[1], down_other[1])


def merge_second_kernel(up, up_other, down, down_other, *rest):
    other, out = rest[:-1], rest[-1]
    for blocks in other:
        out[:2] = blocks[...]
    base = 2 * len(other)
    out[base] = sum_of(up[...], up_other[...])
    out[base + 1] = sum_of(down[...], down_other[...])


def update_hidden_kernel(layers, *refs):
    up_pieces, down_pieces, rest = refs[:layers], refs[layers : 2 * layers], refs[2 * layers :]
    up, up_moment, down, down_moment, up_out, up_moment_out, up_copy, down_out, down_moment_out, down_copy = rest
    width = up_pieces[0].shape[2] // 2
    scale = MUON_RATE * (up.shape[2] // width) ** 0.5
    for old, moment, pieces, out, moment_out, copy in (
        (up, up_moment, up_pieces, up_out, up_moment_out, up_copy),
        (down, down_moment, down_pieces, down_out, down_moment_out, down_copy),
    ):
        for layer in range(layers):
            for block in range(4):
                lanes = lanes_of(block, width)
                both = pieces[layer][block].astype(F32)
                moment_out[layer, :, lanes] = MOMENTUM_DECAY * moment[layer, :, lanes] + both[:, :width]
                master = old[layer, :, lanes] * (1.0 - MUON_RATE * WEIGHT_DECAY) - scale * both[:, width:]
                out[layer, :, lanes] = master
                copy[layer, :, lanes] = master.astype(BF16)


def ortho_kernel(place, terms, moment, result, whole):
    pieces, size, _ = moment.shape
    width = whole.shape[1]
    eye = (iota((width, width), 0) == iota((width, width), 1)).astype(F32)

    def exact(left, right, dims=(((1,), (0,)), ((), ()))):
        return lax.dot_general(left, right, dims, precision=EXACT, preferred_element_type=F32)

    grad = terms[0].astype(F32)
    for term in range(1, terms.shape[0]):
        grad = grad + terms[term].astype(F32)
    for piece in range(pieces):
        whole[piece * size : (piece + 1) * size, :] = moment[piece, :, lanes_of(place, width)].astype(F32)
    source = MOMENTUM_DECAY * whole[...].T + grad
    gram = exact(source, source, (((1,), (1,)), ((), ())))
    norm = jnp.sqrt(jnp.sum(gram * eye)) + ORTHO_EPSILON
    gram = gram / (norm * norm)
    chain = None
    for iteration in range(NS_STEPS):
        step = ORTHO_LINEAR * eye + ORTHO_CUBIC * gram + ORTHO_QUINTIC * exact(gram, gram)
        chain = step if iteration == 0 else exact(chain, step)
        if iteration + 1 < NS_STEPS:
            gram = exact(exact(step, gram), step)
    ortho = dot_tn(source.astype(BF16), (chain / norm).astype(BF16))
    for which, value in ((0, grad.T), (1, ortho)):
        for piece in range(pieces):
            result[piece, :, lanes_of(which, width)] = value[piece * size : (piece + 1) * size].astype(BF16)


def vmem(count):
    return [pl.BlockSpec(memory_space=pltpu.VMEM)] * count


def anywhere(count):
    return [pl.BlockSpec(memory_space=pl.ANY)] * count


def scalars():
    return [pl.BlockSpec(memory_space=pltpu.SMEM)]


def shape(dims, dtype=F32):
    return jax.ShapeDtypeStruct(dims, dtype)


def call(kernel, name, in_specs, outs, scratch, flops, moved):
    return pl.pallas_call(
        kernel,
        name=name,
        out_shape=outs,
        in_specs=in_specs,
        out_specs=vmem(len(outs)),
        scratch_shapes=scratch,
        cost_estimate=pl.CostEstimate(flops=int(flops), bytes_accessed=int(moved), transcendentals=0),
        compiler_params=pltpu.CompilerParams(vmem_limit_bytes=VMEM_BYTES),
    )


def flat(weight):
    return [item for run in weight for item in run[0]]


def plan_of(weight):
    return tuple(tuple(run[1:]) for run in weight)


def project(resid, vectors, tables, feature_map, weight):
    rows, width = resid.shape
    plan = plan_of(weight)
    feats = width // HEAD_DIM * FEATS
    outs = [
        shape((rows, feats), BF16),
        shape((rows, feats), BF16),
        shape((rows, width), BF16),
        shape((rows, width)),
        shape((rows, width)),
        shape((feats + TOTAL_ROWS, 2 * HEAD_DIM), BF16),
    ]
    results = call(
        partial(project_kernel, plan),
        "project",
        vmem(6) + anywhere(ref_count(plan)),
        outs,
        [pltpu.VMEM((4, width, 640), BF16), pltpu.SemaphoreType.DMA((copy_count(plan),))],
        2 * rows * width * width * 3 * 1.5,
        8 * width * width,
    )(resid, vectors, tables["cosine"], tables["sine"], feature_map, tables["column"], *flat(weight))
    return dict(zip(("phi_query", "phi_key", "value", "query", "key", "summary"), results))


def mix_scratch(width, plans):
    return [
        pltpu.VMEM((4, width, 256), BF16),
        pltpu.VMEM((4, width, width), BF16),
        pltpu.VMEM((4, width, width), BF16),
        pltpu.SemaphoreType.DMA((sum(copy_count(plan) for plan in plans),)),
    ]


def mix(resid, vectors, bias, state, received, tables, weights):
    rows, width = resid.shape
    plans = [plan_of(weight) for weight in weights]
    refs = [item for weight in weights for item in flat(weight)]
    outs = [
        shape((rows, width)),
        shape((rows, width)),
        shape((rows, width)),
        shape((4, rows, width), BF16),
        shape((2, rows, width), BF16),
        shape((3, rows, width), BF16),
        shape((rows, width)),
    ]
    results = call(
        partial(mix_kernel, plans),
        "mix",
        vmem(11) + scalars() + anywhere(len(refs)),
        outs,
        mix_scratch(width, plans),
        2 * rows * width * width * 12,
        20 * width * width,
    )(
        resid, vectors, bias, state["phi_query"], state["phi_key"], state["value"], tables["column"], tables["row"],
        *received, tables["shares"], *refs,
    )
    return dict(zip(("context", "inverse", "middle", "slope", "active_keep", "mix_pack", "output"), results))


def back_mix(grad, vectors, state, tables, weights):
    rows, width = grad.shape
    plans = [plan_of(weight) for weight in weights]
    refs = [item for weight in weights for item in flat(weight)]
    feats = width // HEAD_DIM * FEATS
    outs = [
        shape((2, rows, width), BF16),
        shape((3, rows, width), BF16),
        shape((rows, width)),
        shape((rows, width), BF16),
        shape((rows, width), BF16),
        shape((feats + TOTAL_ROWS, 2 * HEAD_DIM), BF16),
        shape((8, width)),
        shape((4, width)),
    ]
    results = call(
        partial(back_mix_kernel, plans),
        "back_mix",
        vmem(8) + anywhere(len(refs)),
        outs,
        mix_scratch(width, plans),
        2 * rows * width * width * 11,
        20 * width * width,
    )(
        grad, vectors, state["middle"], state["slope"], state["inverse"], state["context"], state["phi_query"],
        tables["column"], *refs,
    )
    names = ("upper_keep", "back_pack", "middle_grad", "numer", "denom", "back_summary", "vector_two", "bias_grad")
    return dict(zip(names, results))


def back_project(resid, vectors, state, received, back_received, tables, feature_map, weight):
    rows, width = resid.shape
    plan = plan_of(weight)
    outs = [
        shape((2, rows, width), BF16),
        shape((4, rows, width), BF16),
        shape((rows, width)),
        shape((8, width)),
    ]
    results = call(
        partial(back_project_kernel, plan),
        "back_project",
        vmem(22) + scalars() + anywhere(ref_count(plan)),
        outs,
        [pltpu.VMEM((4, width, 640), BF16), pltpu.SemaphoreType.DMA((copy_count(plan),))],
        2 * rows * width * width * 8,
        8 * width * width,
    )(
        resid, vectors, tables["cosine"], tables["sine"], feature_map, tables["column"], tables["row"],
        state["phi_query"], state["phi_key"], state["value"], state["query"], state["key"], state["numer"],
        state["denom"], state["context"], state["middle_grad"], *received, *back_received, tables["shares"],
        *flat(weight),
    )
    return dict(zip(("stacked_keep", "stack_pack", "input_grad", "vector_one"), results))


def matrix_grad(quick, splits, right_own, right_other, *lefts):
    width = right_own.shape[2]
    block = shape((2, width // 4, width), BF16)
    return call(
        partial(grad_kernel, quick, splits), "matrix_grad", vmem(2 + len(lefts)), [block] * 4,
        [pltpu.VMEM((width, width), BF16)], 2 * 512 * width * width * 2, 8 * width * width,
    )(right_own, right_other, *lefts)


def down_grad(quick, state, mix_other, branch_own, branch_other, entries):
    splits = ((state["mix_pack"].shape[2], *entries),)
    return matrix_grad(quick, splits, state["active_keep"], mix_other, branch_own, branch_other)


def up_grad(quick, state, back_other, mix_other):
    splits = ((state["mix_pack"].shape[2], 2, 2),)
    return matrix_grad(quick, splits, state["upper_keep"], back_other, state["mix_pack"], mix_other)


def attend_grad(quick, state, stack_other, back_other):
    width = state["mix_pack"].shape[2]
    splits = ((width // 4 * 3, 2, 2), (width // 4, 2, 2))
    return matrix_grad(
        quick, splits, state["stacked_keep"], stack_other, state["stack_pack"], stack_other, state["back_pack"],
        back_other,
    )


def merge(kernel, outs, *operands):
    return call(kernel, "merge", vmem(len(operands)), outs, [], 1, 1)(*operands)


def merge_first(own, others):
    out = shape(own[0].shape[1:], BF16)
    return merge(merge_first_kernel, [out] * 4, own[0], others[0], own[2], others[1])


def merge_second(own, others, *other_blocks):
    out = shape((2 + 2 * len(other_blocks),) + own[0].shape, BF16)
    return merge(merge_second_kernel, [out], own[0], others[0], own[2], others[1], *other_blocks)[0]


def send_first(own):
    return swap_head(own[1], 2), swap_dp(own[3], 1)


def send_second(own):
    return swap_dp(own[1], 1), swap_head(own[3], 2)


def orthogonalize(place, terms, moment):
    pieces, size, _ = moment.shape
    width = terms.shape[1]
    return call(
        partial(ortho_kernel, place), "orthogonalize", vmem(2), [shape((pieces, size, 2 * width), BF16)],
        [pltpu.VMEM((pieces * size, width), F32)], 2 * 6 * 20 * width**3, 8 * width * pieces * size,
    )(terms, moment)[0]


def update_hidden(up_pieces, down_pieces, up, up_moment, down, down_moment):
    outs = [shape(up.shape), shape(up.shape), shape(up.shape, BF16)] * 2
    layers = up.shape[0]
    return call(
        partial(update_hidden_kernel, layers), "update_hidden", vmem(2 * layers + 4), outs, [], 8 * up.size,
        26 * up.size,
    )(*up_pieces, *down_pieces, up, up_moment, down, down_moment)


def doc_tables(segment_row, rows):
    index = lax.axis_index("head")
    own = lax.dynamic_slice_in_dim(segment_row, index * rows, rows, 0)
    starts = jnp.sum((segment_row[None, :] < own[:, None]).astype(jnp.int32), axis=1, dtype=jnp.int32)
    offsets = (index * rows + jnp.arange(rows, dtype=jnp.int32) - starts).astype(F32)
    half = HEAD_DIM // 2
    frequency = ROPE_BASE ** (-jnp.arange(half, dtype=F32) / half)
    angles = offsets[:, None] * frequency[None, :]
    scale = HEAD_DIM ** (-0.25)
    edges = segment_row.reshape(-1, rows)[:, :: rows - 1]
    others = jnp.stack([lax.dynamic_index_in_dim(edges, index ^ offset, 0, keepdims=False) for offset in (1, 2, 3)])
    mine = jnp.stack([own[0], own[rows - 1]])
    shares = (others[:, None, :] == mine[None, :, None]).astype(F32).reshape(3, 4)
    return {
        "cosine": jnp.cos(angles) * scale,
        "sine": jnp.sin(angles) * scale,
        "column": own[:, None],
        "row": own[None, :],
        "shares": shares,
    }


def cross_edges(summary, near):
    return swap_head(summary, 2), swap_head(near, 2)


def exchange_edges(summary):
    near = swap_head(summary, 1)
    return near, *cross_edges(summary, near)


def other_slots(values):
    return [swap_head(values, offset) for offset in (1, 2, 3)]


def adam_update(parameter, gradient, first_moment, second_moment):
    first_moment = BETA_FIRST * first_moment + (1.0 - BETA_FIRST) * gradient
    second_moment = BETA_SECOND * second_moment + (1.0 - BETA_SECOND) * gradient * gradient
    first_hat = first_moment / (1.0 - BETA_FIRST**STEP)
    second_hat = second_moment / (1.0 - BETA_SECOND**STEP)
    return (
        parameter - ADAM_RATE * first_hat / (jnp.sqrt(second_hat) + ADAM_EPSILON),
        first_moment,
        second_moment,
    )


def split_columns(matrix, width):
    rows = matrix.shape[0]
    return jnp.transpose(matrix.reshape(rows, -1, width), (1, 0, 2))


def join_columns(blocks):
    count, rows, width = blocks.shape
    return jnp.transpose(blocks, (1, 0, 2)).reshape(rows, count * width)


def attend_shard(query_key, value, out):
    return jnp.concatenate([query_key[:, 0], query_key[:, 1], value, out.T], axis=1).astype(BF16)


def old_blocks(layer, moments, block):
    query_key, value, out, up, down = (moment[layer] for moment in moments)
    return (
        jnp.stack([query_key[:, 0], query_key[:, 1], value, out.T]).astype(BF16),
        jnp.concatenate([split_columns(up, block), split_columns(down.T, block)]).astype(BF16),
    )


def line_parts(line, cuts):
    return [line[:, :, first:last].reshape(-1, last - first) for first, last in cuts]


def core_vectors(vector_grads, bias_grads):
    vectors = jnp.concatenate(vector_grads)
    biases = jnp.stack(bias_grads)
    keep, send = biases[:, 0::2], biases[:, 1::2]
    size = vectors.shape[0]
    sent = swap_head(jnp.concatenate([vectors, send.reshape(-1, vectors.shape[1])]), 1)
    biases = keep + sent[size:].reshape(keep.shape)
    return jnp.concatenate([vectors + sent[:size], biases[:, 1]]), biases[:, 0]


def across_vectors(packed, bias_keep):
    size = packed.shape[0] - bias_keep.shape[0]
    return jnp.concatenate([packed[:size], bias_keep]) + swap_head(packed, 2)


def hold_weight(weight, *values):
    arrays, *values = hold([run[0] for run in weight], *values)
    return [(items, *run[1:]) for items, run in zip(arrays, weight)], *values


def hold_runs(lines, received, *runs):
    arrays, lines, received = hold([run[0] for run in runs], lines, received)
    return lines, received, *[(items, *run[1:]) for items, run in zip(arrays, runs)]


def per_device(
    block_input,
    cotangent,
    marked,
    segments,
    feature_map,
    vectors,
    bias_up,
    w_query_key,
    w_value,
    w_out,
    w_up,
    w_down,
    moment_query_key,
    moment_value,
    moment_out,
    moment_up,
    moment_down,
    vector_first,
    vector_second,
    bias_first,
    bias_second,
):
    layers = w_value.shape[0]
    block = w_value.shape[2]
    rows, width = block_input.shape
    dp_size = lax.axis_size("dp")
    dp_index = lax.axis_index("dp")
    quick = dp_size == 8 and layers == 2
    masters = (w_query_key, w_value, w_out, w_up, w_down)
    moments = (moment_query_key, moment_value, moment_out, moment_up, moment_down)
    muon_scale = (w_value.shape[1] * dp_size / block) ** 0.5

    def attend_of(layer):
        return attend_shard(w_query_key[layer], w_value[layer], w_out[layer])

    def hidden_of(layer):
        return jnp.concatenate([w_up[layer], w_down[layer].T], axis=1).astype(BF16)

    tables = doc_tables(segments[0], rows)
    resid = block_input.astype(F32)
    bias_slots = [bias_up] + other_slots(bias_up)
    biases = [jnp.stack([item[layer] for item in bias_slots]) for layer in range(layers)]
    gradient = cotangent.astype(F32) * marked[0][:, None].astype(F32)
    states = [None] * layers

    def run_project(layer, resid, weight):
        states[layer] = project(resid, vectors[layer], tables, feature_map[layer], weight)
        states[layer]["input"] = resid

    def run_mix(layer, received, weights):
        state = states[layer]
        state["received"] = received
        state.update(mix(state["input"], vectors[layer], biases[layer], state, received, tables, weights))
        return state["output"]

    def run_back_mix(layer, gradient, weights):
        states[layer].update(back_mix(gradient, vectors[layer], states[layer], tables, weights))

    def run_back_project(layer, back_received, weight):
        state = states[layer]
        state.update(
            back_project(
                state["input"], vectors[layer], state, state["received"], back_received, tables, feature_map[layer],
                weight,
            )
        )
        return state["input_grad"]

    if quick:
        half = width // 2
        first = attend_of(0)
        hidden = hidden_of(0)
        second = jnp.concatenate([attend_of(1), hidden_of(1)], axis=1)
        line = [first] + [swap_dp(first, offset) for offset in (2, 4, 6)]

        line, hidden = hold(line, hidden)
        up_line, down_line = (jnp.concatenate([item[:, cut] for item in line]) for cut in (slice(half), slice(half, width)))
        up_y, down_x = swap_dp(up_line, 1), swap_head(down_line, 2)
        hidden_line = gather_line(hidden)

        up_line, down_line, up_y, down_x = hold(up_line, down_line, up_y, down_x)
        up, down = jnp.concatenate([up_line, up_y]), jnp.concatenate([down_line, down_x])
        up_other, down_other = swap_head(up, 2), swap_dp(down, 1)

        up, down, up_other, down_other, resid, tables, biases = hold(
            up, down, up_other, down_other, resid, tables, biases
        )
        cores = swap_all([up, up_other, down, down_other], swap_head, 1)
        weight_one = [
            ((up, cores[0], up_other, cores[1]), "up near", 0, 0, half),
            ((down, cores[2], down_other, cores[3]), "down near", 0, half, half),
        ]
        weight_one, hidden_line, second = hold_weight(weight_one, hidden_line, second)
        up_line, down_line = line_parts(hidden_line, ((0, width), (width, 2 * width)))
        up_y, down_x = swap_dp(up_line, 1), swap_head(down_line, 2)
        second_line = gather_line(second)
        run_project(0, resid, weight_one)
        near = swap_head(states[0]["summary"], 1)

        up_line, down_line, up_y, down_x, near, moments = hold(up_line, down_line, up_y, down_x, near, moments)
        up, down = jnp.concatenate([up_line, up_y]), jnp.concatenate([down_line, down_x])
        up_other, down_other = swap_head(up, 2), swap_dp(down, 1)
        both = cross_edges(states[0]["summary"], near)
        cores = swap_all([up, down], swap_head, 1)
        blocks = [old_blocks(layer, moments, block) for layer in (1, 0)]
        (attend_one, hidden_one), (attend_zero, hidden_zero) = blocks
        payload = jnp.concatenate(
            [
                jnp.concatenate([hidden_one[4:], hidden_one[:4]]),
                jnp.concatenate([attend_one, hidden_zero[4:]]),
            ],
            axis=2,
        )
        payload_late = jnp.concatenate([hidden_zero[:4], attend_zero])

        branch = gradient.astype(BF16)
        branch_other = swap_head(branch, 1)

        cores, up_other, down_other, received, payload, payload_late, second_line, branch_other = hold(
            cores, up_other, down_other, (near, *both), payload, payload_late, second_line, branch_other
        )
        cores += swap_all([up_other, down_other], swap_head, 1)
        weights = [
            (
                weight_one,
                [((up, cores[0], up_other, cores[2]), "up", 0, 0, width)],
                [((down, cores[1], down_other, cores[3]), "down", 0, 0, width)],
            )
        ]
        cuts = ((0, half), (half, width), (width, 2 * width), (2 * width, 3 * width))
        lines = line_parts(second_line, cuts)

        lines, received, weights[0][1][0], weights[0][2][0] = hold_runs(
            lines, received, weights[0][1][0], weights[0][2][0]
        )
        crossed = [swap_dp(lines[0], 1), swap_head(lines[1], 2), swap_dp(lines[2], 1), swap_head(lines[3], 2)]
        resid = run_mix(0, received, weights[0])

        lines, crossed, resid = hold(lines, crossed, resid)
        up, down, up_late, down_late = (jnp.concatenate(pair) for pair in zip(lines, crossed))
        up_other, down_other = swap_head(up, 2), swap_dp(down, 1)
        up_late_other, down_late_other = swap_head(up_late, 2), swap_dp(down_late, 1)

        up, down, up_other, down_other = hold(up, down, up_other, down_other)
        cores = swap_all([up, down, up_other, down_other], swap_head, 1)
        weight_one = [
            ((up, cores[0], up_other, cores[2]), "up", 0, 0, half),
            ((down, cores[1], down_other, cores[3]), "down", 0, half, half),
        ]
        run_project(1, resid, weight_one)
        late_cores = swap_all([up_late, down_late], swap_head, 1)
        near = swap_head(states[1]["summary"], 1)

        both = cross_edges(states[1]["summary"], near)
        received, late_cores, up_late_other, down_late_other, payload = hold(
            (near, *both), late_cores, up_late_other, down_late_other, payload
        )
        late_cores += swap_all([up_late_other, down_late_other], swap_head, 1)
        weights.append(
            (
                weight_one,
                [((up_late, late_cores[0], up_late_other, late_cores[2]), "up", 0, 0, width)],
                [((down_late, late_cores[1], down_late_other, late_cores[3]), "down", 0, 0, width)],
            )
        )
        moment = swap_owners(payload)
        activations = run_mix(1, received, weights[1])

        moment, mix_pack, activations = hold(moment, states[1]["mix_pack"], activations)
        mix_other = swap_head(mix_pack, 1)
        down_one = down_grad(quick, states[1], mix_other, branch, branch_other, (None, None))

        down_one, gradient = hold(down_one, gradient)
        down_others = send_first(down_one)
        run_back_mix(1, gradient, weights[1])

        down_others, summary, back_pack = hold(down_others, states[1]["back_summary"], states[1]["back_pack"])
        near, back_other = swap_all([summary, back_pack], swap_head, 1)
        down_one = merge_first(down_one, down_others)
        near, back_other, down_one = hold(near, back_other, down_one)
        both = cross_edges(summary, near)
        down_others = send_second(down_one)
        up_one = up_grad(quick, states[1], back_other, mix_other)

        back_received, up_one, down_others = hold((near, *both), up_one, down_others)
        up_others = send_first(up_one)
        moment_late = swap_owners(payload_late)
        gradient = run_back_project(1, back_received, weights[1][0])

        up_others, gradient, stack_pack, mix_pack, moment_late = hold(
            up_others, gradient, states[1]["stack_pack"], states[0]["mix_pack"], moment_late
        )
        stack_other, mix_other = swap_all([stack_pack, mix_pack], swap_head, 1)
        up_one = merge_first(up_one, up_others)
        stack_other, mix_other, up_one = hold(stack_other, mix_other, up_one)
        up_others = send_second(up_one)
        down_blocks = merge_second(down_one, down_others)
        attend_one = attend_grad(quick, states[1], stack_other, back_other)

        attend_one, up_others, gradient = hold(attend_one, up_others, gradient)
        attend_others = send_first(attend_one)
        pair_one = swap_line(merge_second(up_one, up_others, down_blocks))
        run_back_mix(0, gradient, weights[0])

        attend_others, summary, back_pack = hold(attend_others, states[0]["back_summary"], states[0]["back_pack"])
        near, back_other = swap_all([summary, back_pack], swap_head, 1)
        attend_one = merge_first(attend_one, attend_others)
        near, back_other, attend_one = hold(near, back_other, attend_one)
        both = cross_edges(summary, near)
        attend_others = send_second(attend_one)
        down_zero = down_grad(quick, states[0], mix_other, stack_pack, stack_other, (3, 3))

        back_received, down_zero, attend_others = hold((near, *both), down_zero, attend_others)
        down_others = send_first(down_zero)
        gradient = run_back_project(0, back_received, weights[0][0])

        down_others, stack_pack, pair_one = hold(down_others, states[0]["stack_pack"], pair_one)
        stack_other = swap_head(stack_pack, 1)
        up_zero = up_grad(quick, states[0], back_other, mix_other)
        down_zero = merge_first(down_zero, down_others)
        up_zero, down_zero, stack_other = hold(up_zero, down_zero, stack_other)
        down_others = send_second(down_zero)
        up_others = send_first(up_zero)
        attend_blocks = merge_second(attend_one, attend_others)
        attend_zero = attend_grad(quick, states[0], stack_other, back_other)

        attend_zero, down_others = hold(attend_zero, down_others)
        attend_others = send_first(attend_zero)
        pair_two = merge_second(down_zero, down_others, attend_blocks)
        pair_two, pair_one = hold(pair_two, pair_one)
        pair_two = swap_line(pair_two)
        back_one = orthogonalize(0, pair_one, moment)

        up_others, back_one = hold(up_others, back_one)
        up_zero = merge_first(up_zero, up_others)
        up_others = send_second(up_zero)
        vector_grads = [(state["vector_one"] + state["vector_two"])[:5] for state in states]
        vector_pack, bias_keep = core_vectors(vector_grads, [state["bias_grad"] for state in states])

        attend_others, vector_pack = hold(attend_others, vector_pack)
        attend_zero = merge_first(attend_zero, attend_others)
        attend_others = send_second(attend_zero)
        packed = across_vectors(vector_pack, bias_keep)

        up_others, packed, pair_two = hold(up_others, packed, pair_two)
        pieces_one = swap_owners(back_one)
        up_blocks = merge_second(up_zero, up_others)
        packed = packed + swap_dp(packed, 1)

        attend_others, up_blocks, pieces_one = hold(attend_others, up_blocks, pieces_one)
        pair_three = merge_second(attend_zero, attend_others, up_blocks)
        pair_three, pair_two = hold(pair_three, pair_two)
        pair_three = swap_line(pair_three)
        back_two = orthogonalize(1, pair_two, moment)

        pair_three, back_two, packed = hold(pair_three, back_two, packed)
        pieces_two = swap_owners(back_two)
        back_three = orthogonalize(0, pair_three, moment_late)

        pieces_two, back_three, packed = hold(pieces_two, back_three, packed)
        pieces_three = swap_owners(back_three)
        for offset in (2, 4):
            packed = packed + swap_dp(packed, offset)
        hidden_pieces = (pieces_three[:4], pieces_one[4:]), (pieces_two[4:], pieces_one[:4])
        attend_pieces = pieces_three[4:], pieces_two[:4]
    else:
        weights = []
        for layer in range(layers):
            parts = []
            for part in (attend_of(layer), w_up[layer].astype(BF16), w_down[layer].T.astype(BF16)):
                whole = lax.all_gather(part, "dp", axis=0, tiled=True)
                parts.append([([whole] + other_slots(whole), "whole", 0, 0, width)])
            weights.append(tuple(parts))
        for layer in range(layers):
            run_project(layer, resid, weights[layer][0])
            resid = run_mix(layer, exchange_edges(states[layer]["summary"]), weights[layer])
        activations = resid
        raw = []
        for layer in reversed(range(layers)):
            state = states[layer]
            branch = gradient.astype(BF16)
            run_back_mix(layer, gradient, weights[layer])
            gradient = run_back_project(layer, exchange_edges(state["back_summary"]), weights[layer][0])
            back_other, mix_other, stack_other, branch_other = swap_all(
                [state["back_pack"], state["mix_pack"], state["stack_pack"], branch], swap_head, 1
            )
            for own in (
                attend_grad(quick, state, stack_other, back_other),
                up_grad(quick, state, back_other, mix_other),
                down_grad(quick, state, mix_other, branch, branch_other, (None, None)),
            ):
                for keep, send in ((own[0], own[1]), (own[2], own[3])):
                    raw.append(keep.astype(F32) + swap_head(send, 2).astype(F32))
        count = layers * 12
        padded = -(-count // dp_size) * dp_size
        grads = jnp.concatenate(raw)
        grads = jnp.concatenate([grads, jnp.zeros((padded - count,) + grads.shape[1:], F32)])
        grads = lax.psum_scatter(grads, "dp", scatter_dimension=0, tiled=True)
        old = [part for layer in reversed(range(layers)) for part in old_blocks(layer, moments, block)]
        old = jnp.concatenate(old)
        old = jnp.concatenate([old, jnp.zeros((padded - count,) + old.shape[1:], old.dtype)])
        old = lax.all_to_all(old, "dp", split_axis=0, concat_axis=1, tiled=True)
        owned = padded // dp_size
        back = jnp.concatenate(
            [orthogonalize(0, grads[place : place + 1], old[place : place + 1]) for place in range(owned)]
        )
        back = jnp.stack([back[..., :block], back[..., block:]], axis=1)
        back = lax.all_to_all(back, "dp", split_axis=2, concat_axis=0, tiled=True)
        back = jnp.concatenate([back[:, 0], back[:, 1]], axis=2)
        ordered = [back[12 * place : 12 * (place + 1)] for place in reversed(range(layers))]
        attend_pieces = [part[:4] for part in ordered]
        hidden_pieces = [part[4:8] for part in ordered], [part[8:] for part in ordered]
        vector_grads = [(state["vector_one"] + state["vector_two"])[:5] for state in states]
        packed = across_vectors(*core_vectors(vector_grads, [state["bias_grad"] for state in states]))
        packed = lax.psum(packed, "dp")

    vector_total, bias_total = packed[: 5 * layers].reshape(vectors.shape), packed[5 * layers :]
    turned = [jnp.transpose(item, (0, 2, 1)) for item in (w_down, moment_down)]
    updated = list(update_hidden(*hidden_pieces, w_up, moment_up, *turned))
    updated[3:] = [jnp.transpose(item, (0, 2, 1)) for item in updated[3:]]
    fresh = []
    for which in range(2):
        parts = [pieces[:, :, lanes_of(which, block)].astype(F32) for pieces in attend_pieces]
        fresh.append(
            (
                jnp.stack([jnp.stack([part[0], part[1]], axis=1) for part in parts]),
                jnp.stack([part[2] for part in parts]),
                jnp.stack([part[3].T for part in parts]),
            )
        )
    next_moments = tuple(MOMENTUM_DECAY * old + grad for old, grad in zip(moments, fresh[0]))
    next_masters = tuple(
        master * (1.0 - MUON_RATE * WEIGHT_DECAY) - MUON_RATE * muon_scale * ortho
        for master, ortho in zip(masters, fresh[1])
    )
    copies = tuple(master.astype(BF16) for master in next_masters)
    vectors_next, vector_first_next, vector_second_next = adam_update(
        vectors, vector_total, vector_first, vector_second
    )
    bias_next, bias_first_next, bias_second_next = adam_update(bias_up, bias_total, bias_first, bias_second)
    return (
        (activations.astype(BF16), gradient)
        + (*next_masters, updated[0], updated[3])
        + (*next_moments, updated[1], updated[4])
        + (*copies, updated[2], updated[5])
        + (vectors_next, vector_first_next, vector_second_next, bias_next, bias_first_next, bias_second_next)
    )


def solution(mesh):
    shards = (
        P(None, "dp", None, "head"),
        P(None, "dp", "head"),
        P(None, "head", "dp"),
        P(None, "dp", "head"),
        P(None, "head", "dp"),
    )
    rows = P(("dp", "head"), None)
    placed = (
        (rows, rows, P("dp", "head"), P("dp", None), P(), P(), P(None, "head"))
        + shards
        + shards
        + (P(), P(), P(None, "head"), P(None, "head"))
    )
    return jax.shard_map(
        per_device,
        mesh=mesh,
        in_specs=placed,
        out_specs=(rows, rows) + shards + shards + shards + (P(), P(), P()) + (P(None, "head"),) * 3,
        check_vma=False,
    )
```

```python
from functools import partial

import jax
import jax.numpy as jnp
from jax import lax
from jax.experimental import pallas as pl
from jax.experimental.pallas import tpu as pltpu
from jax.sharding import PartitionSpec as P

HEAD_DIM = 64
FEATS = 32
NS_STEPS = 5
STEP = 10


ORTHO_LINEAR = 3.4445
ORTHO_CUBIC = -4.775
ORTHO_QUINTIC = 2.0315
ORTHO_EPSILON = 1e-07
MOMENTUM_DECAY = 0.95
MUON_RATE = 0.2
WEIGHT_DECAY = 0.1
BETA_FIRST = 0.9
BETA_SECOND = 0.99
ADAM_RATE = 0.2
ADAM_EPSILON = 1e-08
NORM_EPSILON = 1e-05
ATTEND_EPSILON = 1e-06
ROPE_BASE = 10000.0
EXACT = lax.Precision.HIGHEST

F32 = jnp.float32
BF16 = jnp.bfloat16
CHUNK = 4 * HEAD_DIM
FEAT_CHUNK = 4 * FEATS
TOTAL_ROWS = 16
VMEM_BYTES = 56 * 1024 * 1024


def dot_nn(left, right):
    return lax.dot_general(left, right, (((1,), (0,)), ((), ())), preferred_element_type=F32)


def dot_nt(left, right):
    return lax.dot_general(left, right, (((1,), (1,)), ((), ())), preferred_element_type=F32)


def dot_tn(left, right):
    return lax.dot_general(left, right, (((0,), (0,)), ((), ())), preferred_element_type=F32)


def iota(shape, axis):
    return lax.broadcasted_iota(jnp.int32, shape, axis)


def swap_head(values, offset):
    return lax.ppermute(values, "head", [(h, h ^ offset) for h in range(lax.axis_size("head"))])


def swap_dp(values, offset):
    return lax.ppermute(values, "dp", [(d, d ^ offset) for d in range(lax.axis_size("dp"))])


def swap_all(items, swap, offset):
    return [swap(item, offset) for item in items]


def swap_line(parts):
    groups = [[z * 2 + y for z in range(4)] for y in range(2)]
    return lax.all_to_all(parts, "dp", split_axis=0, concat_axis=0, axis_index_groups=groups, tiled=True)


def four_times(part):
    return jnp.broadcast_to(part[None], (4,) + part.shape)


def swap_owners(parts):
    return lax.all_to_all(parts, "dp", split_axis=0, concat_axis=0, tiled=True)


def hold(*values):
    return lax.optimization_barrier(values)


def sources(kind, slot):
    core, across = slot & 1, slot >> 1
    if kind == "whole":
        return [(slot, None, None)]
    if "up" in kind:
        return [(slot, 0, 0), (slot, 1, 1)]
    return [(core, across, 0), (2 + core, across, 1)]


def fetch(refs, plan, scratch, sems, base, lanes):
    index = lax.axis_index("dp")
    waits = [[], [], [], []]
    count = base
    for position, (kind, source_lane, lane, width) in enumerate(plan):
        first, last = max(lane, lanes[0]), min(lane + width, lanes[1])
        if first >= last:
            continue
        taken = pl.ds(source_lane + first - lane, last - first)
        given = pl.ds(first - lanes[0], last - first)
        for slot in range(4):
            for array, entry, y_offset in sources(kind, slot):
                ref = refs[4 * position + array]
                if kind == "whole":
                    pairs = [(ref.at[:, :, :, taken], scratch.at[slot, :, :, :, given])]
                elif "near" in kind:
                    pairs = [
                        (
                            ref.at[entry, offset, :, taken],
                            scratch.at[slot, (index >> 1) ^ offset, (index & 1) ^ y_offset, :, given],
                        )
                        for offset in range(4)
                    ]
                else:
                    pairs = [(ref.at[entry, :, :, taken], scratch.at[slot, :, (index & 1) ^ y_offset, :, given])]
                for source, target in pairs:
                    copy = pltpu.make_async_copy(source, target, sems.at[count])
                    copy.start()
                    waits[slot].append(copy)
                    count += 1
    return waits


def matrix(scratch, slot, first, last):
    value = scratch[slot]
    return value.reshape(-1, value.shape[-1])[:, first:last]


def ref_count(plan):
    return 4 * len(plan)


def copy_count(plan):
    return sum(4 if run[0] == "whole" else 32 if "near" in run[0] else 8 for run in plan)


def take(refs, *plans):
    taken = []
    for plan in plans:
        taken.append(refs[: ref_count(plan)])
        refs = refs[ref_count(plan) :]
    return (*taken, refs)


def arrive(copies):
    for copy in copies:
        copy.wait()


def norm_parts(values):
    row_mean = jnp.mean(values, axis=-1, keepdims=True)
    centred = values - row_mean
    variance = jnp.mean(centred * centred, axis=-1, keepdims=True)
    scale = lax.rsqrt(variance + NORM_EPSILON)
    return centred * scale, scale


def norm_backward(values, gain, incoming):
    unit, scale = norm_parts(values)
    gain_grad = jnp.sum(incoming * unit, axis=0, keepdims=True)
    shift_grad = jnp.sum(incoming, axis=0, keepdims=True)
    inner = incoming * gain
    inner_mean = jnp.mean(inner, axis=-1, keepdims=True)
    along = jnp.mean(inner * unit, axis=-1, keepdims=True)
    return scale * (inner - inner_mean - unit * along), gain_grad, shift_grad


def swap_halves(values):
    width = values.shape[1]
    half = HEAD_DIM // 2
    lower = iota(values.shape, 1) % HEAD_DIM < half
    return jnp.where(lower, pltpu.roll(values, width - half, 1), pltpu.roll(values, half, 1))


def split_low(values):
    high = values.astype(BF16)
    return high, (values - high.astype(F32)).astype(BF16)


def lane_mask(index, per_head, width):
    return (iota((1, width), 1) // per_head == index).astype(BF16)


def turn_tables(cosine, sine):
    part, other = cosine[...], sine[...]
    return (
        jnp.concatenate([part] * (2 * CHUNK // HEAD_DIM), axis=1),
        jnp.concatenate([-other, other] * (CHUNK // HEAD_DIM), axis=1),
    )


def wide_map(feature_map):
    tall = jnp.concatenate([feature_map[...]] * 4, axis=0)
    return jnp.where(feature_ones(), jnp.concatenate([tall] * 4, axis=1), 0.0)


def feature_ones():
    return iota((CHUNK, FEAT_CHUNK), 0) // HEAD_DIM == iota((CHUNK, FEAT_CHUNK), 1) // FEATS


def features(values, map_high, map_low):
    high, low_part = split_low(values)
    square_high, square_low = split_low(0.5 * values * values)
    ones = -feature_ones().astype(BF16)
    left = jnp.concatenate([high, low_part, high, square_high, square_low], axis=1)
    right = jnp.concatenate([map_high, map_high, map_low, ones, ones], axis=0)
    return jnp.exp(dot_nn(left, right)) * FEATS ** (-0.5)


def fold_matrix():
    rows, columns = iota((CHUNK, HEAD_DIM), 0), iota((CHUNK, HEAD_DIM), 1)
    return (rows % HEAD_DIM == columns).astype(BF16)


def spread_matrix():
    rows = iota((2 * HEAD_DIM, 2 * CHUNK), 0)
    columns = iota((2 * HEAD_DIM, 2 * CHUNK), 1)
    return (columns // CHUNK * HEAD_DIM + columns % HEAD_DIM == rows).astype(BF16)


def same_head(feature_rows):
    shape = (feature_rows, 2 * CHUNK)
    return iota(shape, 0) % FEAT_CHUNK // FEATS == iota(shape, 1) % CHUNK // HEAD_DIM


def column_of(segment_row):
    return jnp.broadcast_to(segment_row[...], (8, segment_row.shape[1])).T[:, 0:1]


def edge_masks(segment_column):
    first = segment_column[0:1, :]
    last = segment_column[segment_column.shape[0] - 1 :, :]
    in_first = (segment_column == first).astype(F32)
    in_last = (segment_column == last).astype(F32) * (1.0 - in_first)
    return in_first, in_last


def edge_summary(edges, weighted):
    full = dot_tn(edges, weighted)
    full = jnp.where(same_head(2 * FEAT_CHUNK)[:, :CHUNK], full, 0.0).astype(BF16)
    folded = dot_nn(full, fold_matrix())
    return jnp.concatenate([folded[:FEAT_CHUNK], folded[FEAT_CHUNK:]], axis=1).astype(BF16)


def store_totals(summary_out, rows):
    pieces = [piece for row in rows for piece in (row[:, :FEAT_CHUNK], row[:, FEAT_CHUNK:])]
    pieces.append(jnp.zeros((TOTAL_ROWS - len(pieces), FEAT_CHUNK), F32))
    summary_out[summary_out.shape[0] - TOTAL_ROWS :, :] = jnp.concatenate(pieces, axis=0).astype(BF16)


def edges_of(phi, in_first, in_last):
    wide = phi.astype(F32)
    return jnp.concatenate([wide * in_first, wide * in_last], axis=1).astype(BF16)


def open_edges(ref, which):
    feats = ref.shape[0] - TOTAL_ROWS
    totals = ref[feats:, :]
    columns = []
    for chunk in range(feats // FEAT_CHUNK):
        pick = (iota((TOTAL_ROWS, HEAD_DIM), 0) == 2 * chunk + which).astype(BF16)
        columns.append(dot_tn(totals, pick))
    sums = ref[:feats, lanes_of(which, HEAD_DIM)].astype(F32)
    return jnp.concatenate([sums, jnp.concatenate(columns, axis=0)], axis=1)


def combine_edges(received, coefficients):
    totals = [None, None]
    rows = (received[0].shape[0] - TOTAL_ROWS) // 4
    for position, ref in enumerate(received):
        offset = position + 1
        pair = []
        for which in range(2):
            value = open_edges(ref, which)
            pair.append(
                jnp.concatenate(
                    [value[(slot ^ offset) * rows : ((slot ^ offset) + 1) * rows] for slot in range(4)], axis=0
                )
            )
        for which in range(2):
            part = coefficients[position, 2 * which] * pair[0] + coefficients[position, 2 * which + 1] * pair[1]
            totals[which] = part if totals[which] is None else totals[which] + part
    return totals


def spread_edges(totals, chunk):
    rows = slice(chunk * FEAT_CHUNK, (chunk + 1) * FEAT_CHUNK)
    joined = jnp.concatenate([totals[0][rows], totals[1][rows]], axis=0).astype(BF16)
    return jnp.where(same_head(2 * FEAT_CHUNK), dot_nn(joined, spread_matrix()), 0.0).astype(BF16)


def lanes_of(slot, width):
    return slice(slot * width, (slot + 1) * width)


def project_kernel(plan, resid, vectors, cosine_part, sine_part, feature_map, segment_row, *rest):
    weight_refs, rest = take(rest, plan)
    phi_query_out, phi_key_out, value_out, query_out, key_out, summary_out, weight, sems = rest
    waits = fetch(weight_refs, plan, weight, sems, 0, (0, weight.shape[4]))
    cosine, sine = turn_tables(cosine_part, sine_part)
    unit, _ = norm_parts(resid[...])
    normed = (unit * vectors[0:1, :] + vectors[1:2, :]).astype(BF16)
    width = resid.shape[1] // 4
    pieces = [[], [], []]
    for slot in range(4):
        arrive(waits[slot])
        product = dot_nn(normed, matrix(weight, slot, 0, 3 * width))
        for which in range(3):
            pieces[which].append(product[:, lanes_of(which, width)])
    queries, key_rows, value_rows = (jnp.concatenate(piece, axis=1) for piece in pieces)
    value_rows = value_rows.astype(BF16)
    value_out[...] = value_rows
    map_high, map_low = split_low(wide_map(feature_map))
    in_first, in_last = edge_masks(column_of(segment_row))
    totals = []
    for chunk in range(resid.shape[1] // CHUNK):
        lanes = lanes_of(chunk, CHUNK)
        feats = lanes_of(chunk, FEAT_CHUNK)
        turned = []
        for source, scaled_out, phi_out in (
            (queries, query_out, phi_query_out),
            (key_rows, key_out, phi_key_out),
        ):
            part = source[:, lanes]
            scaled = part * cosine + swap_halves(part) * sine
            scaled_out[:, lanes] = scaled
            phi = features(scaled, map_high, map_low).astype(BF16)
            phi_out[:, feats] = phi
            turned.append(phi)
        edges = edges_of(turned[1], in_first, in_last)
        summary_out[feats, :] = edge_summary(edges, value_rows[:, lanes])
        totals.append(jnp.sum(edges.astype(F32), axis=0, keepdims=True))
    store_totals(summary_out, totals)


def mix_kernel(
    plans, resid, vectors, bias, phi_query, phi_key, value, segment_row, recv_one, recv_two,
    recv_three, coefficients, *rest
):
    out_refs, up_refs, down_refs, rest = take(rest, *plans)
    (context_out, inverse_out, middle_out, slope_out, active_keep, pack_out, resid_out, out_weight, up_weight,
     down_weight, sems) = rest
    bases = [0, copy_count(plans[0]), copy_count(plans[0]) + copy_count(plans[1])]
    out_waits = fetch(out_refs, plans[0], out_weight, sems, bases[0], (512, 768))
    up_waits = fetch(up_refs, plans[1], up_weight, sems, bases[1], (0, 768))
    down_waits = fetch(down_refs, plans[2], down_weight, sems, bases[2], (0, 768))
    segment_column = column_of(segment_row)
    same = (segment_column == segment_row[...]).astype(F32)
    in_first, in_last = edge_masks(segment_column)
    totals = combine_edges((recv_one, recv_two, recv_three), coefficients)
    rows = resid.shape[0]
    contexts = []
    for chunk in range(resid.shape[1] // CHUNK):
        lanes = lanes_of(chunk, CHUNK)
        feats = lanes_of(chunk, FEAT_CHUNK)
        query = phi_query[:, feats]
        key = phi_key[:, feats]
        values = value[:, lanes]
        left = []
        right = []
        for head in range(4):
            scores = dot_nt(query * lane_mask(head, FEATS, FEAT_CHUNK), key)
            left.append((scores * same).astype(BF16))
            mask = lane_mask(head, HEAD_DIM, CHUNK)
            right.append(jnp.concatenate([values * mask, jnp.broadcast_to(mask, (rows, CHUNK))], axis=1))
        left.append(edges_of(query, in_first, in_last))
        right.append(spread_edges(totals, chunk))
        both = dot_nn(jnp.concatenate(left, axis=1), jnp.concatenate(right, axis=0))
        inverse = 1.0 / (both[:, CHUNK:] + ATTEND_EPSILON)
        context = both[:, :CHUNK] * inverse
        inverse_out[:, lanes] = inverse
        context_out[:, lanes] = context
        contexts.append(context.astype(BF16))
    context = jnp.concatenate(contexts, axis=1)
    width = resid.shape[1] // 4
    middle = resid[...]
    for slot in range(4):
        arrive(out_waits[slot])
        middle = middle + dot_nt(context[:, lanes_of(slot, width)], matrix(out_weight, slot, 64, 256))
    middle_out[...] = middle
    unit, _ = norm_parts(middle)
    normed = (unit * vectors[2:3, :] + vectors[3:4, :]).astype(BF16)
    pack_out[2] = normed
    output = middle + vectors[4:5, :]
    for slot in range(4):
        arrive(up_waits[slot])
        upper = dot_nn(normed, matrix(up_weight, slot, 0, 768)) + bias[slot : slot + 1, :]
        below = 0.5 * (1.0 + lax.erf(upper * 2.0**-0.5))
        slope = below + upper * (jnp.exp(-0.5 * upper * upper) * 0.3989422804014327)
        active = (upper * below).astype(BF16)
        slope_out[slot] = slope.astype(BF16)
        if slot % 2 == 0:
            active_keep[slot // 2] = active
        else:
            pack_out[slot // 2] = active
        arrive(down_waits[slot])
        output = output + dot_nt(active, matrix(down_weight, slot, 0, 768))
    resid_out[...] = output


def back_mix_kernel(
    plans, grad, vectors, middle, slope, inverse, context, phi_query, segment_row, *rest
):
    out_refs, up_refs, down_refs, rest = take(rest, *plans)
    (upper_keep, pack_out, middle_grad_out, numer_out, denom_out, summary_out, vector_out,
     bias_out, out_weight, up_weight, down_weight, sems) = rest
    bases = [0, copy_count(plans[0]), copy_count(plans[0]) + copy_count(plans[1])]
    down_waits = fetch(down_refs, plans[2], down_weight, sems, bases[2], (0, 768))
    up_waits = fetch(up_refs, plans[1], up_weight, sems, bases[1], (0, 768))
    out_waits = fetch(out_refs, plans[0], out_weight, sems, bases[0], (512, 768))
    grad_out = grad[...]
    branch = grad_out.astype(BF16)
    shift_out = jnp.sum(branch.astype(F32), axis=0, keepdims=True)
    normed_grad = None
    for slot in range(4):
        arrive(down_waits[slot])
        hidden = dot_nn(branch, matrix(down_weight, slot, 0, 768))
        upper = (hidden * slope[slot].astype(F32)).astype(BF16)
        if slot % 2 == 0:
            upper_keep[slot // 2] = upper
        else:
            pack_out[slot // 2] = upper
        bias_out[slot : slot + 1, :] = jnp.sum(upper.astype(F32), axis=0, keepdims=True)
        arrive(up_waits[slot])
        part = dot_nt(upper, matrix(up_weight, slot, 0, 768))
        normed_grad = part if normed_grad is None else normed_grad + part
    inward, gain_grad, shift_grad = norm_backward(middle[...], vectors[2:3, :], normed_grad)
    middle_grad = grad_out + inward
    middle_grad_out[...] = middle_grad
    attn = middle_grad.astype(BF16)
    pack_out[2] = attn
    zero_row = jnp.zeros_like(shift_out)
    vector_out[...] = jnp.concatenate([zero_row, zero_row, gain_grad, shift_grad, shift_out] + [zero_row] * 3, axis=0)
    pieces = []
    for slot in range(4):
        arrive(out_waits[slot])
        pieces.append(dot_nn(attn, matrix(out_weight, slot, 64, 256)))
    context_grad = jnp.concatenate(pieces, axis=1)
    in_first, in_last = edge_masks(column_of(segment_row))
    head_ones = (iota((CHUNK, CHUNK), 0) // HEAD_DIM == iota((CHUNK, CHUNK), 1) // HEAD_DIM).astype(BF16)
    one_lane = (iota((CHUNK, FEAT_CHUNK), 0) == iota((CHUNK, FEAT_CHUNK), 1) // FEATS * HEAD_DIM).astype(BF16)
    totals = []
    for chunk in range(grad.shape[1] // CHUNK):
        lanes = lanes_of(chunk, CHUNK)
        feats = lanes_of(chunk, FEAT_CHUNK)
        numer = context_grad[:, lanes] * inverse[:, lanes]
        denom = -dot_nn((numer * context[:, lanes]).astype(BF16), head_ones)
        numer = numer.astype(BF16)
        denom = denom.astype(BF16)
        numer_out[:, lanes] = numer
        denom_out[:, lanes] = denom
        edges = edges_of(phi_query[:, feats], in_first, in_last)
        summary_out[feats, :] = edge_summary(edges, numer)
        heads = dot_nn(denom, one_lane)
        weighted = edges.astype(F32) * jnp.concatenate([heads, heads], axis=1)
        totals.append(jnp.sum(weighted, axis=0, keepdims=True))
    store_totals(summary_out, totals)


def back_project_kernel(
    plan, resid, vectors, cosine_part, sine_part, feature_map, segment_row, phi_query, phi_key, value,
    query_scaled, key_scaled, numer, denom, context, middle_grad, recv_one, recv_two, recv_three, back_one,
    back_two, back_three, coefficients, *rest
):
    weight_refs, rest = take(rest, plan)
    stacked_keep, pack_out, grad_out, vector_out, weight, sems = rest
    waits = fetch(weight_refs, plan, weight, sems, 0, (0, weight.shape[4]))
    cosine, sine = turn_tables(cosine_part, sine_part)
    unit, _ = norm_parts(resid[...])
    pack_out[2] = (unit * vectors[0:1, :] + vectors[1:2, :]).astype(BF16)
    segment_column = column_of(segment_row)
    same = (segment_column == segment_row[...]).astype(F32)
    in_first, in_last = edge_masks(segment_column)
    totals = combine_edges((recv_one, recv_two, recv_three), coefficients)
    back_totals = combine_edges((back_one, back_two, back_three), coefficients)
    rows = resid.shape[0]
    map_high, map_low = split_low(wide_map(feature_map))
    spread_high = jnp.concatenate([map_high, feature_ones().astype(BF16)], axis=0)
    spread_low = jnp.concatenate([map_low, jnp.zeros_like(map_low)], axis=0)
    spread_map = jnp.concatenate([spread_high, spread_high, spread_low], axis=1)
    share = jnp.full((rows, CHUNK), 1.0 / HEAD_DIM, BF16)
    grads = [[], [], []]
    for chunk in range(resid.shape[1] // CHUNK):
        lanes = lanes_of(chunk, CHUNK)
        feats = lanes_of(chunk, FEAT_CHUNK)
        query = phi_query[:, feats]
        key = phi_key[:, feats]
        values = value[:, lanes]
        both = jnp.concatenate([numer[:, lanes], denom[:, lanes]], axis=1)
        valued = jnp.concatenate([values, share], axis=1)
        query_left, query_right, key_left, key_right, value_left, value_right = [], [], [], [], [], []
        for head in range(4):
            feat_mask = lane_mask(head, FEATS, FEAT_CHUNK)
            mask = lane_mask(head, HEAD_DIM, CHUNK)
            both_mask = jnp.concatenate([mask, mask], axis=1)
            masked_query = query * feat_mask
            masked_both = both * both_mask
            query_left.append((dot_nt(masked_both, valued) * same).astype(BF16))
            query_right.append(key * feat_mask)
            key_left.append((dot_nt(valued, masked_both) * same).astype(BF16))
            key_right.append(masked_query)
            value_left.append((dot_nt(key, masked_query) * same).astype(BF16))
            value_right.append(masked_both[:, :CHUNK])
        forward_edges = spread_edges(totals, chunk)
        backward_edges = spread_edges(back_totals, chunk)
        query_edges = dot_nt(jnp.concatenate([numer[:, lanes], denom[:, lanes] * share], axis=1), forward_edges)
        key_edges = dot_nt(valued, backward_edges)
        query_edges = query_edges[:, :FEAT_CHUNK] * in_first + query_edges[:, FEAT_CHUNK:] * in_last
        key_edges = key_edges[:, :FEAT_CHUNK] * in_first + key_edges[:, FEAT_CHUNK:] * in_last
        value_left.append(edges_of(key, in_first, in_last))
        value_right.append(backward_edges[:, :CHUNK])
        phi_grads = (
            dot_nn(jnp.concatenate(query_left, axis=1), jnp.concatenate(query_right, axis=0)) + query_edges,
            dot_nn(jnp.concatenate(key_left, axis=1), jnp.concatenate(key_right, axis=0)) + key_edges,
        )
        grads[2].append(dot_nn(jnp.concatenate(value_left, axis=1), jnp.concatenate(value_right, axis=0)))
        for which, phi, scaled in ((0, query, query_scaled), (1, key, key_scaled)):
            high, low_part = split_low(phi_grads[which] * phi.astype(F32))
            wide = dot_nt(jnp.concatenate([high, low_part, high], axis=1), spread_map)
            turned = wide[:, :CHUNK] - scaled[:, lanes] * wide[:, CHUNK:]
            grads[which].append(turned * cosine + swap_halves(turned * sine))
    joined = [jnp.concatenate(item, axis=1).astype(BF16) for item in grads]
    joined.append(context[...].astype(BF16))
    width = resid.shape[1] // 4
    normed_grad = None
    for slot in range(4):
        stacked = jnp.concatenate([item[:, lanes_of(slot, width)] for item in joined], axis=1)
        if slot % 2 == 0:
            stacked_keep[slot // 2] = stacked
        else:
            pack_out[slot // 2] = stacked
        arrive(waits[slot])
        part = dot_nt(stacked[:, : 3 * width], matrix(weight, slot, 0, 3 * width))
        normed_grad = part if normed_grad is None else normed_grad + part
    inward, gain_grad, shift_grad = norm_backward(resid[...], vectors[0:1, :], normed_grad)
    below = middle_grad[...] + inward
    grad_out[...] = below
    pack_out[3] = below.astype(BF16)
    zero_row = jnp.zeros_like(gain_grad)
    vector_out[...] = jnp.concatenate([gain_grad, shift_grad] + [zero_row] * 6, axis=0)


def grad_kernel(quick, splits, right_own, right_other, *rest):
    lefts, (up_keep, up_send, down_keep, down_send, whole) = rest[: 2 * len(splits)], rest[2 * len(splits) :]
    y_bit = lax.axis_index("dp") & 1
    size = up_keep.shape[1]
    joined = []
    for position, (_, own_entry, other_entry) in enumerate(splits):
        own, other = lefts[2 * position], lefts[2 * position + 1]
        own = own[...] if own_entry is None else own[own_entry]
        other = other[...] if other_entry is None else other[other_entry]
        joined.append(jnp.concatenate([own, other], axis=0))
    for position, up_out, down_out in ((1, up_send, down_send), (0, up_keep, down_keep)):
        right = jnp.concatenate([right_own[position], right_other[position]], axis=0)
        start = 0
        for (columns, _, _), left in zip(splits, joined):
            whole[start : start + columns] = dot_tn(right[:, start : start + columns], left).astype(BF16)
            start += columns
        for part in range(2):
            up_out[part] = whole[part * size : (part + 1) * size]
        if not quick:
            for part in range(2):
                down_out[part] = whole[(2 + part) * size : (3 + part) * size]
            continue
        for bit, out in ((y_bit, down_keep), (1 - y_bit, down_send)):
            out[position] = whole[pl.ds(pl.multiple_of((2 + bit) * size, size), size), :]


def sum_of(left, right):
    return (left.astype(F32) + right.astype(F32)).astype(BF16)


def merge_first_kernel(up, up_other, down, down_other, up_keep, up_send, down_keep, down_send):
    y_bit = lax.axis_index("dp") & 1
    up_keep[...] = sum_of(up[y_bit], up_other[y_bit])
    up_send[...] = sum_of(up[1 - y_bit], up_other[1 - y_bit])
    down_keep[...] = sum_of(down[0], down_other[0])
    down_send[...] = sum_of(down[1], down_other[1])


def merge_second_kernel(up, up_other, down, down_other, *rest):
    other, out = rest[:-1], rest[-1]
    for blocks in other:
        out[:2] = blocks[...]
    base = 2 * len(other)
    out[base] = sum_of(up[...], up_other[...])
    out[base + 1] = sum_of(down[...], down_other[...])


def update_kernel(ratio, items, aliased, pieces, *refs):
    width = pieces.shape[2] // 2
    scale = MUON_RATE * ratio**0.5
    olds, news = refs[: 2 * len(items)], refs[2 * len(items) + aliased :]
    for position, (name, base) in enumerate(items):
        old, moment = olds[2 * position : 2 * position + 2]
        new, new_moment, copy = news[3 * position : 3 * position + 3]
        rows = old.shape[2] if name == "out" else old.shape[1]
        for block in range({"query_key": 2, "value": 1, "out": 1}.get(name, 4)):
            both = pieces[base + block, 0:rows].astype(F32)
            if name == "out":
                both = both.T
                grad, ortho = both[:width], both[width:]
            else:
                grad, ortho = both[:, :width], both[:, width:]
            if name == "query_key":
                place = (0, slice(None), block)
            elif name in ("value", "out"):
                place = (0,)
            else:
                place = (0, slice(None), lanes_of(block, width))
            new_moment[place] = MOMENTUM_DECAY * moment[place] + grad
            master = old[place] * (1.0 - MUON_RATE * WEIGHT_DECAY) - scale * ortho
            new[place] = master
            copy[place] = master.astype(BF16)


def ortho_kernel(place, terms, moment, *rest):
    extra, (result, whole) = rest[:-2], rest[-2:]
    pieces, size, _ = moment.shape
    width = whole.shape[1]
    eye = (iota((width, width), 0) == iota((width, width), 1)).astype(F32)

    def exact(left, right, dims=(((1,), (0,)), ((), ()))):
        return lax.dot_general(left, right, dims, precision=EXACT, preferred_element_type=F32)

    grad = terms[0].astype(F32)
    for term in range(1, terms.shape[0]):
        grad = grad + terms[term].astype(F32)
    for piece in range(pieces):
        whole[piece * size : (piece + 1) * size, :] = moment[piece, :, lanes_of(place, width)].astype(F32)
    source = MOMENTUM_DECAY * whole[...].T + grad
    gram = exact(source, source, (((1,), (1,)), ((), ())))
    norm = jnp.sqrt(jnp.sum(gram * eye)) + ORTHO_EPSILON
    gram = gram / (norm * norm)
    chain = None
    for iteration in range(NS_STEPS):
        step = ORTHO_LINEAR * eye + ORTHO_CUBIC * gram + ORTHO_QUINTIC * exact(gram, gram)
        chain = step if iteration == 0 else exact(chain, step)
        if iteration + 1 < NS_STEPS:
            gram = exact(exact(step, gram), step)
    ortho = dot_tn(source.astype(BF16), (chain / norm).astype(BF16))
    for which, value in ((0, grad.T), (1, ortho)):
        for piece in range(pieces):
            result[piece, 0:size, lanes_of(which, width)] = value[piece * size : (piece + 1) * size].astype(BF16)
    for rows in extra:
        half = rows.shape[1] // 2
        spare = result.shape[1] - size
        more = [rows[:, :half], rows[:, half:], jnp.zeros((spare - 2 * rows.shape[0], half), F32)]
        more = jnp.concatenate(more, axis=0).astype(BF16)
        for piece in range(pieces):
            result[piece, size:, :] = more


def vmem(count):
    return [pl.BlockSpec(memory_space=pltpu.VMEM)] * count


def anywhere(count):
    return [pl.BlockSpec(memory_space=pl.ANY)] * count


def scalars():
    return [pl.BlockSpec(memory_space=pltpu.SMEM)]


def shape(dims, dtype=F32):
    return jax.ShapeDtypeStruct(dims, dtype)


def call(kernel, name, in_specs, outs, scratch, flops, moved):
    return pl.pallas_call(
        kernel,
        name=name,
        out_shape=outs,
        in_specs=in_specs,
        out_specs=vmem(len(outs)),
        scratch_shapes=scratch,
        cost_estimate=pl.CostEstimate(flops=int(flops), bytes_accessed=int(moved), transcendentals=0),
        compiler_params=pltpu.CompilerParams(vmem_limit_bytes=VMEM_BYTES),
    )


def weight_scratch(width, lanes):
    return pltpu.VMEM((4, 4, 2, width // 8, lanes), BF16)


def flat(weight):
    return [item for run in weight for item in run[0]]


def plan_of(weight):
    return tuple(tuple(run[1:]) for run in weight)


def project(resid, vectors, tables, feature_map, weight):
    rows, width = resid.shape
    plan = plan_of(weight)
    feats = width // HEAD_DIM * FEATS
    outs = [
        shape((rows, feats), BF16),
        shape((rows, feats), BF16),
        shape((rows, width), BF16),
        shape((rows, width)),
        shape((rows, width)),
        shape((feats + TOTAL_ROWS, 2 * HEAD_DIM), BF16),
    ]
    results = call(
        partial(project_kernel, plan),
        "project",
        vmem(6) + anywhere(ref_count(plan)),
        outs,
        [weight_scratch(width, 640), pltpu.SemaphoreType.DMA((copy_count(plan),))],
        2 * rows * width * width * 3 * 1.5,
        8 * width * width,
    )(resid, vectors, tables["cosine"], tables["sine"], feature_map, tables["row"], *flat(weight))
    return dict(zip(("phi_query", "phi_key", "value", "query", "key", "summary"), results))


def mix_scratch(width, plans):
    return [
        weight_scratch(width, 256),
        weight_scratch(width, width),
        weight_scratch(width, width),
        pltpu.SemaphoreType.DMA((sum(copy_count(plan) for plan in plans),)),
    ]


def mix(resid, vectors, bias, state, received, tables, weights):
    rows, width = resid.shape
    plans = [plan_of(weight) for weight in weights]
    refs = [item for weight in weights for item in flat(weight)]
    outs = [
        shape((rows, width)),
        shape((rows, width)),
        shape((rows, width)),
        shape((4, rows, width), BF16),
        shape((2, rows, width), BF16),
        shape((3, rows, width), BF16),
        shape((rows, width)),
    ]
    results = call(
        partial(mix_kernel, plans),
        "mix",
        vmem(10) + scalars() + anywhere(len(refs)),
        outs,
        mix_scratch(width, plans),
        2 * rows * width * width * 12,
        20 * width * width,
    )(
        resid, vectors, bias, state["phi_query"], state["phi_key"], state["value"], tables["row"],
        *received, tables["shares"], *refs,
    )
    return dict(zip(("context", "inverse", "middle", "slope", "active_keep", "mix_pack", "output"), results))


def back_mix(grad, vectors, state, tables, weights):
    rows, width = grad.shape
    plans = [plan_of(weight) for weight in weights]
    refs = [item for weight in weights for item in flat(weight)]
    feats = width // HEAD_DIM * FEATS
    outs = [
        shape((2, rows, width), BF16),
        shape((3, rows, width), BF16),
        shape((rows, width)),
        shape((rows, width), BF16),
        shape((rows, width), BF16),
        shape((feats + TOTAL_ROWS, 2 * HEAD_DIM), BF16),
        shape((8, width)),
        shape((4, width)),
    ]
    results = call(
        partial(back_mix_kernel, plans),
        "back_mix",
        vmem(8) + anywhere(len(refs)),
        outs,
        mix_scratch(width, plans),
        2 * rows * width * width * 11,
        20 * width * width,
    )(
        grad, vectors, state["middle"], state["slope"], state["inverse"], state["context"], state["phi_query"],
        tables["row"], *refs,
    )
    names = ("upper_keep", "back_pack", "middle_grad", "numer", "denom", "back_summary", "vector_two", "bias_grad")
    return dict(zip(names, results))


def back_project(resid, vectors, state, received, back_received, tables, feature_map, weight):
    rows, width = resid.shape
    plan = plan_of(weight)
    outs = [
        shape((2, rows, width), BF16),
        shape((4, rows, width), BF16),
        shape((rows, width)),
        shape((8, width)),
    ]
    results = call(
        partial(back_project_kernel, plan),
        "back_project",
        vmem(21) + scalars() + anywhere(ref_count(plan)),
        outs,
        [weight_scratch(width, 640), pltpu.SemaphoreType.DMA((copy_count(plan),))],
        2 * rows * width * width * 8,
        8 * width * width,
    )(
        resid, vectors, tables["cosine"], tables["sine"], feature_map, tables["row"],
        state["phi_query"], state["phi_key"], state["value"], state["query"], state["key"], state["numer"],
        state["denom"], state["context"], state["middle_grad"], *received, *back_received, tables["shares"],
        *flat(weight),
    )
    return dict(zip(("stacked_keep", "stack_pack", "input_grad", "vector_one"), results))


def matrix_grad(quick, splits, right_own, right_other, *lefts):
    width = right_own.shape[2]
    block = shape((2, width // 4, width), BF16)
    return call(
        partial(grad_kernel, quick, splits), "matrix_grad", vmem(2 + len(lefts)), [block] * 4,
        [pltpu.VMEM((width, width), BF16)], 2 * 512 * width * width * 2, 8 * width * width,
    )(right_own, right_other, *lefts)


def down_grad(quick, state, mix_other, branch_own, branch_other, entries):
    splits = ((state["mix_pack"].shape[2], *entries),)
    return matrix_grad(quick, splits, state["active_keep"], mix_other, branch_own, branch_other)


def up_grad(quick, state, back_other, mix_other):
    splits = ((state["mix_pack"].shape[2], 2, 2),)
    return matrix_grad(quick, splits, state["upper_keep"], back_other, state["mix_pack"], mix_other)


def attend_grad(quick, state, stack_other, back_other):
    width = state["mix_pack"].shape[2]
    splits = ((width // 4 * 3, 2, 2), (width // 4, 2, 2))
    return matrix_grad(
        quick, splits, state["stacked_keep"], stack_other, state["stack_pack"], stack_other, state["back_pack"],
        back_other,
    )


def merge(kernel, outs, *operands):
    return call(kernel, "merge", vmem(len(operands)), outs, [], 1, 1)(*operands)


def merge_first(own, others):
    out = shape(own[0].shape[1:], BF16)
    return merge(merge_first_kernel, [out] * 4, own[0], others[0], own[2], others[1])


def merge_second(own, others, *other_blocks):
    out = shape((2 + 2 * len(other_blocks),) + own[0].shape, BF16)
    return merge(merge_second_kernel, [out], own[0], others[0], own[2], others[1], *other_blocks)[0]


def send_first(own):
    return swap_head(own[1], 2), swap_dp(own[3], 1)


def send_second(own):
    return swap_dp(own[1], 1), swap_head(own[3], 2)


def orthogonalize(place, terms, moment, *extra):
    pieces, size, _ = moment.shape
    width = terms.shape[1]
    spare = 32 if extra else 0
    return call(
        partial(ortho_kernel, place), "orthogonalize", vmem(2 + len(extra)),
        [shape((pieces, size + spare, 2 * width), BF16)], [pltpu.VMEM((pieces * size, width), F32)], 1, 1,
    )(terms, moment, *extra)[0]


def update(ratio, pieces, items, olds, news):
    def part_of(array, layer):
        dims = array.shape[1:]
        return pl.BlockSpec((1, *dims), lambda step: (layer,) + (0,) * len(dims))

    in_specs, operands, out_specs, outs, before = vmem(1), [pieces], [], [], []
    for name, layer, _ in items:
        for array in olds[name]:
            in_specs.append(part_of(array, layer))
            operands.append(array)
    for name, layer, _ in items:
        for position, like in enumerate((olds[name][0], olds[name][0], olds[name][0])):
            if name in news:
                before.append((news[name][position], len(outs)))
            outs.append(shape(like.shape, BF16 if position == 2 else F32))
            out_specs.append(part_of(like, layer))
    aliases = {len(operands) + position: out for position, (_, out) in enumerate(before)}
    results = pl.pallas_call(
        partial(update_kernel, ratio, [(name, base) for name, _, base in items], len(before)),
        name="update",
        grid=(1,),
        out_shape=outs,
        in_specs=in_specs + anywhere(len(before)),
        out_specs=out_specs,
        input_output_aliases=aliases,
        compiler_params=pltpu.CompilerParams(vmem_limit_bytes=VMEM_BYTES),
    )(*operands, *(array for array, _ in before))
    return {name: results[3 * place : 3 * place + 3] for place, (name, _, _) in enumerate(items)}


def doc_tables(segment_row, rows):
    index = lax.axis_index("head")
    own = lax.dynamic_slice_in_dim(segment_row, index * rows, rows, 0)
    starts = jnp.sum((segment_row[None, :] < own[:, None]).astype(jnp.int32), axis=1, dtype=jnp.int32)
    offsets = (index * rows + jnp.arange(rows, dtype=jnp.int32) - starts).astype(F32)
    half = HEAD_DIM // 2
    frequency = ROPE_BASE ** (-jnp.arange(half, dtype=F32) / half)
    angles = offsets[:, None] * frequency[None, :]
    scale = HEAD_DIM ** (-0.25)
    edges = segment_row.reshape(-1, rows)[:, :: rows - 1]
    others = jnp.stack([lax.dynamic_index_in_dim(edges, index ^ offset, 0, keepdims=False) for offset in (1, 2, 3)])
    mine = jnp.stack([own[0], own[rows - 1]])
    shares = (others[:, None, :] == mine[None, :, None]).astype(F32).reshape(3, 4)
    return {
        "cosine": jnp.cos(angles) * scale,
        "sine": jnp.sin(angles) * scale,
        "row": own[None, :].astype(F32),
        "shares": shares,
    }


def cross_edges(summary, near):
    return swap_head(summary, 2), swap_head(near, 2)


def exchange_edges(summary):
    near = swap_head(summary, 1)
    return near, *cross_edges(summary, near)


def other_slots(values):
    return [swap_head(values, offset) for offset in (1, 2, 3)]


def adam_update(parameter, gradient, first_moment, second_moment):
    first_moment = BETA_FIRST * first_moment + (1.0 - BETA_FIRST) * gradient
    second_moment = BETA_SECOND * second_moment + (1.0 - BETA_SECOND) * gradient * gradient
    first_hat = first_moment / (1.0 - BETA_FIRST**STEP)
    second_hat = second_moment / (1.0 - BETA_SECOND**STEP)
    return (
        parameter - ADAM_RATE * first_hat / (jnp.sqrt(second_hat) + ADAM_EPSILON),
        first_moment,
        second_moment,
    )


def split_columns(matrix, width):
    rows = matrix.shape[0]
    return jnp.transpose(matrix.reshape(rows, -1, width), (1, 0, 2))


def join_columns(blocks):
    count, rows, width = blocks.shape
    return jnp.transpose(blocks, (1, 0, 2)).reshape(rows, count * width)


def attend_shard(query_key, value, out):
    return jnp.concatenate([query_key[:, 0], query_key[:, 1], value, out.T], axis=1).astype(BF16)


def old_blocks(layer, moments, block):
    query_key, value, out, up, down = (moment[layer] for moment in moments)
    return (
        jnp.stack([query_key[:, 0], query_key[:, 1], value, out.T]).astype(BF16),
        jnp.concatenate([split_columns(up, block), split_columns(down.T, block)]).astype(BF16),
    )


def line_parts(line, cuts):
    return [line[:, :, first:last] for first, last in cuts]


def core_vectors(vector_grads, bias_grads):
    vectors = jnp.concatenate(vector_grads)
    biases = jnp.stack(bias_grads)
    width = vectors.shape[1]
    keep, send = biases[:, 0::2].reshape(-1, width), biases[:, 1::2].reshape(-1, width)
    return jnp.concatenate([vectors, keep]), jnp.concatenate([vectors, send])


def across_vectors(total, layers):
    size = total.shape[0] - 2 * layers
    vectors, biases = total[:size], total[size:]
    return jnp.concatenate([vectors, biases[0::2]]), jnp.concatenate([vectors, biases[1::2]])


def per_device(
    block_input,
    cotangent,
    marked,
    segments,
    feature_map,
    vectors,
    bias_up,
    w_query_key,
    w_value,
    w_out,
    w_up,
    w_down,
    moment_query_key,
    moment_value,
    moment_out,
    moment_up,
    moment_down,
    vector_first,
    vector_second,
    bias_first,
    bias_second,
):
    layers = w_value.shape[0]
    block = w_value.shape[2]
    rows, width = block_input.shape
    dp_size = lax.axis_size("dp")
    dp_index = lax.axis_index("dp")
    quick = dp_size == 8 and layers == 2
    moments = (moment_query_key, moment_value, moment_out, moment_up, moment_down)

    def attend_of(layer):
        return attend_shard(w_query_key[layer], w_value[layer], w_out[layer])

    def hidden_of(layer):
        return jnp.concatenate([w_up[layer], w_down[layer].T], axis=1).astype(BF16)

    tables = doc_tables(segments[0], rows)
    resid = block_input.astype(F32)
    bias_slots = [bias_up] + other_slots(bias_up)
    biases = [jnp.stack([item[layer] for item in bias_slots]) for layer in range(layers)]
    gradient = cotangent.astype(F32) * marked[0][:, None].astype(F32)
    states = [None] * layers

    def run_project(layer, resid, weight):
        states[layer] = project(resid, vectors[layer], tables, feature_map[layer], weight)
        states[layer]["input"] = resid

    def run_mix(layer, received, weights):
        state = states[layer]
        state["received"] = received
        state.update(mix(state["input"], vectors[layer], biases[layer], state, received, tables, weights))
        return state["output"]

    def run_back_mix(layer, gradient, weights):
        states[layer].update(back_mix(gradient, vectors[layer], states[layer], tables, weights))

    def run_back_project(layer, back_received, weight):
        state = states[layer]
        state.update(
            back_project(
                state["input"], vectors[layer], state, state["received"], back_received, tables, feature_map[layer],
                weight,
            )
        )
        return state["input_grad"]

    if quick:
        half = width // 2
        first = attend_of(0)
        hidden, second_attend, second_hidden = (
            four_times(part) for part in (hidden_of(0), attend_of(1), hidden_of(1))
        )
        line = [first] + [swap_dp(first, offset) for offset in (2, 4, 6)]

        line, hidden = hold(line, hidden)
        up_line, down_line = (jnp.stack([item[:, cut] for item in line]) for cut in (slice(half), slice(half, width)))
        up_y, down_x = swap_dp(up_line, 1), swap_head(down_line, 2)
        hidden_line = swap_line(hidden)

        up_line, down_line, up_y, down_x = hold(up_line, down_line, up_y, down_x)
        up, down = jnp.stack([up_line, up_y]), jnp.stack([down_line, down_x])
        up_other, down_other = swap_head(up, 2), swap_dp(down, 1)

        up, down, up_other, down_other, resid, tables, biases, second_attend = hold(
            up, down, up_other, down_other, resid, tables, biases, second_attend
        )
        cores = swap_all([up, up_other, down, down_other], swap_head, 1)
        cores, hidden_line, second_attend = hold(cores, hidden_line, second_attend)
        weight_one = [
            ((up, cores[0], up_other, cores[1]), "up near", 0, 0, half),
            ((down, cores[2], down_other, cores[3]), "down near", 0, half, half),
        ]
        up_line, down_line = line_parts(hidden_line, ((0, width), (width, 2 * width)))
        up_y, down_x = swap_dp(up_line, 1), swap_head(down_line, 2)
        attend_line = swap_line(second_attend)
        run_project(0, resid, weight_one)
        near = swap_head(states[0]["summary"], 1)

        up_line, down_line, up_y, down_x, near, attend_line, second_hidden, moments, gradient = hold(
            up_line, down_line, up_y, down_x, near, attend_line, second_hidden, moments, gradient
        )
        second_line = swap_line(second_hidden)
        up, down = jnp.stack([up_line, up_y]), jnp.stack([down_line, down_x])
        up_other, down_other = swap_head(up, 2), swap_dp(down, 1)
        both = cross_edges(states[0]["summary"], near)
        cores = swap_all([up, down], swap_head, 1)
        blocks = [old_blocks(layer, moments, block) for layer in (1, 0)]
        (attend_one, hidden_one), (attend_zero, hidden_zero) = blocks
        payload = jnp.concatenate(
            [
                jnp.concatenate([hidden_one[4:], hidden_one[:4]]),
                jnp.concatenate([attend_one, hidden_zero[4:]]),
            ],
            axis=2,
        )
        payload_late = jnp.concatenate([hidden_zero[:4], attend_zero])

        branch = gradient.astype(BF16)
        branch_other = swap_head(branch, 1)

        cores, up_other, down_other, received, payload, payload_late, second_line, branch_other = hold(
            cores, up_other, down_other, (near, *both), payload, payload_late, second_line, branch_other
        )
        cores += swap_all([up_other, down_other], swap_head, 1)
        lines = line_parts(attend_line, ((0, half), (half, width)))
        lines += line_parts(second_line, ((0, width), (width, 2 * width)))

        lines, received, cores = hold(lines, received, cores)
        weights = [
            (
                weight_one,
                [((up, cores[0], up_other, cores[2]), "up", 0, 0, width)],
                [((down, cores[1], down_other, cores[3]), "down", 0, 0, width)],
            )
        ]
        crossed = [swap_dp(lines[0], 1), swap_head(lines[1], 2), swap_dp(lines[2], 1), swap_head(lines[3], 2)]
        resid = run_mix(0, received, weights[0])

        lines, crossed, resid = hold(lines, crossed, resid)
        up, down, up_late, down_late = (jnp.stack(pair) for pair in zip(lines, crossed))
        up_other, down_other = swap_head(up, 2), swap_dp(down, 1)
        up_late_other, down_late_other = swap_head(up_late, 2), swap_dp(down_late, 1)

        up, down, up_other, down_other = hold(up, down, up_other, down_other)
        cores = swap_all([up, down, up_other, down_other], swap_head, 1)
        late_cores = swap_all([up_late, down_late], swap_head, 1)
        cores, late_cores, resid = hold(cores, late_cores, resid)
        weight_one = [
            ((up, cores[0], up_other, cores[2]), "up", 0, 0, half),
            ((down, cores[1], down_other, cores[3]), "down", 0, half, half),
        ]
        run_project(1, resid, weight_one)

        summary = states[1]["summary"]
        near = swap_head(summary, 1)
        both = cross_edges(summary, near)
        received, up_late_other, down_late_other, payload = hold(
            (near, *both), up_late_other, down_late_other, payload
        )
        late_cores += swap_all([up_late_other, down_late_other], swap_head, 1)
        weights.append(
            (
                weight_one,
                [((up_late, late_cores[0], up_late_other, late_cores[2]), "up", 0, 0, width)],
                [((down_late, late_cores[1], down_late_other, late_cores[3]), "down", 0, 0, width)],
            )
        )
        moment = swap_owners(payload)
        activations = run_mix(1, received, weights[1])

        moment, mix_pack, activations = hold(moment, states[1]["mix_pack"], activations)
        mix_other = swap_head(mix_pack, 1)
        down_one = down_grad(quick, states[1], mix_other, branch, branch_other, (None, None))

        down_one, gradient = hold(down_one, gradient)
        down_others = send_first(down_one)
        run_back_mix(1, gradient, weights[1])

        down_others, summary, back_pack = hold(down_others, states[1]["back_summary"], states[1]["back_pack"])
        near, back_other = swap_all([summary, back_pack], swap_head, 1)
        down_one = merge_first(down_one, down_others)
        near, back_other, down_one = hold(near, back_other, down_one)
        both = cross_edges(summary, near)
        down_others = send_second(down_one)
        up_one = up_grad(quick, states[1], back_other, mix_other)

        back_received, up_one, down_others = hold((near, *both), up_one, down_others)
        up_others = send_first(up_one)
        moment_late = swap_owners(payload_late)
        gradient = run_back_project(1, back_received, weights[1][0])

        up_others, gradient, stack_pack, mix_pack, moment_late = hold(
            up_others, gradient, states[1]["stack_pack"], states[0]["mix_pack"], moment_late
        )
        stack_other, mix_other = swap_all([stack_pack, mix_pack], swap_head, 1)
        up_one = merge_first(up_one, up_others)
        stack_other, mix_other, up_one = hold(stack_other, mix_other, up_one)
        up_others = send_second(up_one)
        down_blocks = merge_second(down_one, down_others)
        attend_one = attend_grad(quick, states[1], stack_other, back_other)

        attend_one, up_others, gradient = hold(attend_one, up_others, gradient)
        attend_others = send_first(attend_one)
        pair_one = swap_line(merge_second(up_one, up_others, down_blocks))
        run_back_mix(0, gradient, weights[0])

        attend_others, summary, back_pack = hold(attend_others, states[0]["back_summary"], states[0]["back_pack"])
        near, back_other = swap_all([summary, back_pack], swap_head, 1)
        attend_one = merge_first(attend_one, attend_others)
        near, back_other, attend_one = hold(near, back_other, attend_one)
        both = cross_edges(summary, near)
        attend_others = send_second(attend_one)
        down_zero = down_grad(quick, states[0], mix_other, stack_pack, stack_other, (3, 3))

        back_received, down_zero, attend_others = hold((near, *both), down_zero, attend_others)
        down_others = send_first(down_zero)
        gradient = run_back_project(0, back_received, weights[0][0])

        down_others, stack_pack, pair_one = hold(down_others, states[0]["stack_pack"], pair_one)
        stack_other = swap_head(stack_pack, 1)
        vector_grads = [(state["vector_one"] + state["vector_two"])[:5] for state in states]
        kept, sent = core_vectors(vector_grads, [state["bias_grad"] for state in states])
        came = swap_head(sent, 1)
        up_zero = up_grad(quick, states[0], back_other, mix_other)
        down_zero = merge_first(down_zero, down_others)
        up_zero, down_zero, stack_other, one, one_others, came = hold(
            up_zero, down_zero, stack_other, attend_one, attend_others, came
        )
        down_others = send_second(down_zero)
        up_others = send_first(up_zero)
        attend_blocks = merge_second(one, one_others)
        kept, sent = across_vectors(kept + came, layers)
        came = swap_head(sent, 2)
        attend_zero = attend_grad(quick, states[0], stack_other, back_other)

        attend_zero, down_others, came = hold(attend_zero, down_others, came)
        attend_others = send_first(attend_zero)
        pair_two = swap_line(merge_second(down_zero, down_others, attend_blocks))
        back_one = orthogonalize(0, pair_one, moment, kept + came)

        up_others, back_one = hold(up_others, back_one)
        up_zero = merge_first(up_zero, up_others)
        up_kept = up_zero[0], up_zero[2]
        up_others = send_second(up_zero)

        attend_others, pair_two, back_one, up_kept = hold(attend_others, pair_two, back_one, up_kept)
        attend_zero = merge_first(attend_zero, attend_others)
        attend_kept = attend_zero[0], attend_zero[2]
        attend_others = send_second(attend_zero)
        pieces_one = swap_owners(back_one)
        back_two = orthogonalize(1, pair_two, moment)

        attend_others, up_others, back_two = hold(attend_others, up_others, back_two)
        up_blocks = merge_second((up_kept[0], None, up_kept[1]), up_others)
        pair_three = merge_second((attend_kept[0], None, attend_kept[1]), attend_others, up_blocks)
        pair_three, pieces_one = hold(pair_three, pieces_one)
        pair_three = swap_line(pair_three)

        pair_three, back_two = hold(pair_three, back_two)
        pieces_two = swap_owners(back_two)
        back_three = orthogonalize(0, pair_three, moment_late)

        pieces_two, back_three = hold(pieces_two, back_three)
        pieces_three = swap_owners(back_three)
        packed = jnp.sum(pieces_one[:, moments[1].shape[1] :].astype(F32), axis=0)
        packed = packed[: 2 * kept.shape[0]]
        packed = jnp.concatenate([packed[: kept.shape[0]], packed[kept.shape[0] :]], axis=1)
        plan = [
            (pieces_one, [("up", 1, 4), ("down", 1, 0)]),
            (pieces_two, [("down", 0, 4), ("query_key", 1, 0), ("value", 1, 2), ("out", 1, 3)]),
            (pieces_three, [("up", 0, 0), ("query_key", 0, 4), ("value", 0, 6), ("out", 0, 7)]),
        ]
    else:
        weights = []
        for layer in range(layers):
            parts = []
            for part in (attend_of(layer), w_up[layer].astype(BF16), w_down[layer].T.astype(BF16)):
                whole = lax.all_gather(part, "dp", axis=0, tiled=True).reshape(4, 2, width // 8, -1)
                parts.append([([whole] + other_slots(whole), "whole", 0, 0, width)])
            weights.append(tuple(parts))
        for layer in range(layers):
            run_project(layer, resid, weights[layer][0])
            resid = run_mix(layer, exchange_edges(states[layer]["summary"]), weights[layer])
        activations = resid
        raw = []
        for layer in reversed(range(layers)):
            state = states[layer]
            branch = gradient.astype(BF16)
            run_back_mix(layer, gradient, weights[layer])
            gradient = run_back_project(layer, exchange_edges(state["back_summary"]), weights[layer][0])
            back_other, mix_other, stack_other, branch_other = swap_all(
                [state["back_pack"], state["mix_pack"], state["stack_pack"], branch], swap_head, 1
            )
            for own in (
                attend_grad(quick, state, stack_other, back_other),
                up_grad(quick, state, back_other, mix_other),
                down_grad(quick, state, mix_other, branch, branch_other, (None, None)),
            ):
                for keep, send in ((own[0], own[1]), (own[2], own[3])):
                    raw.append(keep.astype(F32) + swap_head(send, 2).astype(F32))
        count = layers * 12
        padded = -(-count // dp_size) * dp_size
        grads = jnp.concatenate(raw)
        grads = jnp.concatenate([grads, jnp.zeros((padded - count,) + grads.shape[1:], F32)])
        grads = lax.psum_scatter(grads, "dp", scatter_dimension=0, tiled=True)
        old = [part for layer in reversed(range(layers)) for part in old_blocks(layer, moments, block)]
        old = jnp.concatenate(old)
        old = jnp.concatenate([old, jnp.zeros((padded - count,) + old.shape[1:], old.dtype)])
        old = lax.all_to_all(old, "dp", split_axis=0, concat_axis=1, tiled=True)
        owned = padded // dp_size
        back = jnp.concatenate(
            [orthogonalize(0, grads[place : place + 1], old[place : place + 1]) for place in range(owned)]
        )
        back = jnp.stack([back[..., :block], back[..., block:]], axis=1)
        back = lax.all_to_all(back, "dp", split_axis=2, concat_axis=0, tiled=True)
        back = jnp.concatenate([back[:, 0], back[:, 1]], axis=2)
        ordered = [back[12 * place : 12 * (place + 1)] for place in reversed(range(layers))]
        plan = [
            (part, [("query_key", layer, 0), ("value", layer, 2), ("out", layer, 3), ("up", layer, 4), ("down", layer, 8)])
            for layer, part in enumerate(ordered)
        ]
        vector_grads = [(state["vector_one"] + state["vector_two"])[:5] for state in states]
        kept, sent = core_vectors(vector_grads, [state["bias_grad"] for state in states])
        kept, sent = across_vectors(kept + swap_head(sent, 1), layers)
        packed = lax.psum(kept + swap_head(sent, 2), "dp")

    vector_total, bias_total = packed[: 5 * layers].reshape(vectors.shape), packed[5 * layers :]
    olds = {
        "query_key": (w_query_key, moment_query_key),
        "value": (w_value, moment_value),
        "out": (w_out, moment_out),
        "up": (w_up, moment_up),
        "down": tuple(jnp.transpose(item, (0, 2, 1)) for item in (w_down, moment_down)),
    }
    news = {}
    for pieces, items in plan:
        news.update(update(width // block, pieces, items, olds, news))
    news["down"] = [jnp.transpose(item, (0, 2, 1)) for item in news["down"]]
    next_masters, next_moments, copies = zip(*(news[name] for name in ("query_key", "value", "out", "up", "down")))
    vectors_next, vector_first_next, vector_second_next = adam_update(
        vectors, vector_total, vector_first, vector_second
    )
    bias_next, bias_first_next, bias_second_next = adam_update(bias_up, bias_total, bias_first, bias_second)
    return (
        (activations.astype(BF16), gradient)
        + next_masters
        + next_moments
        + copies
        + (vectors_next, vector_first_next, vector_second_next, bias_next, bias_first_next, bias_second_next)
    )


def solution(mesh):
    shards = (
        P(None, "dp", None, "head"),
        P(None, "dp", "head"),
        P(None, "head", "dp"),
        P(None, "dp", "head"),
        P(None, "head", "dp"),
    )
    rows = P(("dp", "head"), None)
    placed = (
        (rows, rows, P("dp", "head"), P("dp", None), P(), P(), P(None, "head"))
        + shards
        + shards
        + (P(), P(), P(None, "head"), P(None, "head"))
    )
    return jax.shard_map(
        per_device,
        mesh=mesh,
        in_specs=placed,
        out_specs=(rows, rows) + shards + shards + shards + (P(), P(), P()) + (P(None, "head"),) * 3,
        check_vma=False,
    )
```

```python
from functools import partial
from types import SimpleNamespace

import jax
import jax.numpy as jnp
from jax import lax
from jax.experimental import pallas as pl
from jax.experimental.pallas import tpu as pltpu
from jax.sharding import PartitionSpec as P

HEAD_DIM = 64
FEATS = 32
NS_STEPS = 5
STEP = 10


ORTHO_LINEAR = 3.4445
ORTHO_CUBIC = -4.775
ORTHO_QUINTIC = 2.0315
ORTHO_EPSILON = 1e-07
MOMENTUM_DECAY = 0.95
MUON_RATE = 0.2
WEIGHT_DECAY = 0.1
BETA_FIRST = 0.9
BETA_SECOND = 0.99
ADAM_RATE = 0.2
ADAM_EPSILON = 1e-08
NORM_EPSILON = 1e-05
ATTEND_EPSILON = 1e-06
ROPE_BASE = 10000.0
EXACT = lax.Precision.HIGHEST

F32 = jnp.float32
BF16 = jnp.bfloat16
CHUNK = 4 * HEAD_DIM
FEAT_CHUNK = 4 * FEATS
TOTAL_ROWS = 16
VMEM_BYTES = 56 * 1024 * 1024


def dot_nn(left, right):
    return lax.dot_general(left, right, (((1,), (0,)), ((), ())), preferred_element_type=F32)


def dot_nt(left, right):
    return lax.dot_general(left, right, (((1,), (1,)), ((), ())), preferred_element_type=F32)


def dot_tn(left, right):
    return lax.dot_general(left, right, (((0,), (0,)), ((), ())), preferred_element_type=F32)


def iota(shape, axis):
    return lax.broadcasted_iota(jnp.int32, shape, axis)


def swap_head(values, offset):
    return lax.ppermute(values, "head", [(h, h ^ offset) for h in range(lax.axis_size("head"))])


def swap_dp(values, offset):
    return lax.ppermute(values, "dp", [(d, d ^ offset) for d in range(lax.axis_size("dp"))])


def swap_all(items, swap, offset):
    return [swap(item, offset) for item in items]


def swap_line(parts):
    groups = [[z * 2 + y for z in range(4)] for y in range(2)]
    return lax.all_to_all(parts, "dp", split_axis=0, concat_axis=0, axis_index_groups=groups, tiled=True)


def four_times(part):
    return jnp.broadcast_to(part[None], (4,) + part.shape)


def swap_owners(parts):
    return lax.all_to_all(parts, "dp", split_axis=0, concat_axis=0, tiled=True)


def hold(*values):
    return lax.optimization_barrier(values)


def sources(kind, slot):
    core, across = slot & 1, slot >> 1
    if kind == "whole":
        return [(slot, None, None)]
    if "up" in kind:
        return [(slot, 0, 0), (slot, 1, 1)]
    return [(core, across, 0), (2 + core, across, 1)]


def fetch(refs, plan, scratch, sems, base, lanes):
    index = lax.axis_index("dp")
    waits = [[], [], [], []]
    count = base
    for position, (kind, source_lane, lane, width) in enumerate(plan):
        first, last = max(lane, lanes[0]), min(lane + width, lanes[1])
        if first >= last:
            continue
        taken = pl.ds(source_lane + first - lane, last - first)
        given = pl.ds(first - lanes[0], last - first)
        for slot in range(4):
            for array, entry, y_offset in sources(kind, slot):
                ref = refs[4 * position + array]
                if kind == "whole":
                    pairs = [(ref.at[:, :, :, taken], scratch.at[slot, :, :, :, given])]
                elif "near" in kind:
                    pairs = [
                        (
                            ref.at[entry, offset, :, taken],
                            scratch.at[slot, (index >> 1) ^ offset, (index & 1) ^ y_offset, :, given],
                        )
                        for offset in range(4)
                    ]
                else:
                    pairs = [(ref.at[entry, :, :, taken], scratch.at[slot, :, (index & 1) ^ y_offset, :, given])]
                for source, target in pairs:
                    copy = pltpu.make_async_copy(source, target, sems.at[count])
                    copy.start()
                    waits[slot].append(copy)
                    count += 1
    return waits


def matrix(scratch, slot, first, last):
    value = scratch[slot]
    return value.reshape(-1, value.shape[-1])[:, first:last]


def ref_count(plan):
    return 4 * len(plan)


def copy_count(plan):
    return sum(4 if run[0] == "whole" else 32 if "near" in run[0] else 8 for run in plan)


def take(refs, *plans):
    taken = []
    for plan in plans:
        taken.append(refs[: ref_count(plan)])
        refs = refs[ref_count(plan) :]
    return (*taken, refs)


def arrive(copies):
    for copy in copies:
        copy.wait()


def norm_parts(values):
    row_mean = jnp.mean(values, axis=-1, keepdims=True)
    centred = values - row_mean
    variance = jnp.mean(centred * centred, axis=-1, keepdims=True)
    scale = lax.rsqrt(variance + NORM_EPSILON)
    return centred * scale, scale


def norm_backward(values, gain, incoming):
    unit, scale = norm_parts(values)
    gain_grad = jnp.sum(incoming * unit, axis=0, keepdims=True)
    shift_grad = jnp.sum(incoming, axis=0, keepdims=True)
    inner = incoming * gain
    inner_mean = jnp.mean(inner, axis=-1, keepdims=True)
    along = jnp.mean(inner * unit, axis=-1, keepdims=True)
    return scale * (inner - inner_mean - unit * along), gain_grad, shift_grad


def swap_halves(values):
    width = values.shape[1]
    half = HEAD_DIM // 2
    lower = iota(values.shape, 1) % HEAD_DIM < half
    return jnp.where(lower, pltpu.roll(values, width - half, 1), pltpu.roll(values, half, 1))


def split_low(values):
    high = values.astype(BF16)
    return high, (values - high.astype(F32)).astype(BF16)


def lane_mask(index, per_head, width):
    return (iota((1, width), 1) // per_head == index).astype(BF16)


def turn_tables(cosine, sine):
    part, other = cosine[...], sine[...]
    return (
        jnp.concatenate([part] * (2 * CHUNK // HEAD_DIM), axis=1),
        jnp.concatenate([-other, other] * (CHUNK // HEAD_DIM), axis=1),
    )


def wide_map(feature_map):
    tall = jnp.concatenate([feature_map[...]] * 4, axis=0)
    return jnp.where(feature_ones(), jnp.concatenate([tall] * 4, axis=1), 0.0)


def feature_ones():
    return iota((CHUNK, FEAT_CHUNK), 0) // HEAD_DIM == iota((CHUNK, FEAT_CHUNK), 1) // FEATS


def features(values, map_high, map_low):
    high, low_part = split_low(values)
    square_high, square_low = split_low(0.5 * values * values)
    ones = -feature_ones().astype(BF16)
    left = jnp.concatenate([high, low_part, high, square_high, square_low], axis=1)
    right = jnp.concatenate([map_high, map_high, map_low, ones, ones], axis=0)
    return jnp.exp(dot_nn(left, right)) * FEATS ** (-0.5)


def fold_matrix():
    rows, columns = iota((CHUNK, HEAD_DIM), 0), iota((CHUNK, HEAD_DIM), 1)
    return (rows % HEAD_DIM == columns).astype(BF16)


def spread_matrix():
    rows = iota((2 * HEAD_DIM, 2 * CHUNK), 0)
    columns = iota((2 * HEAD_DIM, 2 * CHUNK), 1)
    return (columns // CHUNK * HEAD_DIM + columns % HEAD_DIM == rows).astype(BF16)


def same_head(feature_rows):
    shape = (feature_rows, 2 * CHUNK)
    return iota(shape, 0) % FEAT_CHUNK // FEATS == iota(shape, 1) % CHUNK // HEAD_DIM


def column_of(segment_row):
    return jnp.broadcast_to(segment_row[...], (8, segment_row.shape[1])).T[:, 0:1]


def edge_masks(segment_column):
    first = segment_column[0:1, :]
    last = segment_column[segment_column.shape[0] - 1 :, :]
    in_first = (segment_column == first).astype(F32)
    in_last = (segment_column == last).astype(F32) * (1.0 - in_first)
    return in_first, in_last


def edge_summary(edges, weighted):
    full = dot_tn(edges, weighted)
    full = jnp.where(same_head(2 * FEAT_CHUNK)[:, :CHUNK], full, 0.0).astype(BF16)
    folded = dot_nn(full, fold_matrix())
    return jnp.concatenate([folded[:FEAT_CHUNK], folded[FEAT_CHUNK:]], axis=1).astype(BF16)


def store_totals(summary_out, rows):
    pieces = [piece for row in rows for piece in (row[:, :FEAT_CHUNK], row[:, FEAT_CHUNK:])]
    pieces.append(jnp.zeros((TOTAL_ROWS - len(pieces), FEAT_CHUNK), F32))
    summary_out[summary_out.shape[0] - TOTAL_ROWS :, :] = jnp.concatenate(pieces, axis=0).astype(BF16)


def edges_of(phi, in_first, in_last):
    wide = phi.astype(F32)
    return jnp.concatenate([wide * in_first, wide * in_last], axis=1).astype(BF16)


def open_edges(ref, which):
    feats = ref.shape[0] - TOTAL_ROWS
    totals = ref[feats:, :]
    columns = []
    for chunk in range(feats // FEAT_CHUNK):
        pick = (iota((TOTAL_ROWS, HEAD_DIM), 0) == 2 * chunk + which).astype(BF16)
        columns.append(dot_tn(totals, pick))
    sums = ref[:feats, lanes_of(which, HEAD_DIM)].astype(F32)
    return jnp.concatenate([sums, jnp.concatenate(columns, axis=0)], axis=1)


def combine_edges(received, coefficients):
    totals = [None, None]
    rows = (received[0].shape[0] - TOTAL_ROWS) // 4
    for position, ref in enumerate(received):
        offset = position + 1
        pair = []
        for which in range(2):
            value = open_edges(ref, which)
            pair.append(
                jnp.concatenate(
                    [value[(slot ^ offset) * rows : ((slot ^ offset) + 1) * rows] for slot in range(4)], axis=0
                )
            )
        for which in range(2):
            part = coefficients[position, 2 * which] * pair[0] + coefficients[position, 2 * which + 1] * pair[1]
            totals[which] = part if totals[which] is None else totals[which] + part
    return totals


def spread_edges(totals, chunk):
    rows = slice(chunk * FEAT_CHUNK, (chunk + 1) * FEAT_CHUNK)
    joined = jnp.concatenate([totals[0][rows], totals[1][rows]], axis=0).astype(BF16)
    return jnp.where(same_head(2 * FEAT_CHUNK), dot_nn(joined, spread_matrix()), 0.0).astype(BF16)


def lanes_of(slot, width):
    return slice(slot * width, (slot + 1) * width)


def project_kernel(plan, resid, vectors, cosine_part, sine_part, feature_map, segment_row, *rest):
    weight_refs, rest = take(rest, plan)
    phi_query_out, phi_key_out, value_out, query_out, key_out, summary_out, weight, sems = rest
    waits = fetch(weight_refs, plan, weight, sems, 0, (0, weight.shape[4]))
    cosine, sine = turn_tables(cosine_part, sine_part)
    unit, _ = norm_parts(resid[...])
    normed = (unit * vectors[0:1, :] + vectors[1:2, :]).astype(BF16)
    width = resid.shape[1] // 4
    pieces = [[], [], []]
    for slot in range(4):
        arrive(waits[slot])
        product = dot_nn(normed, matrix(weight, slot, 0, 3 * width))
        for which in range(3):
            pieces[which].append(product[:, lanes_of(which, width)])
    queries, key_rows, value_rows = (jnp.concatenate(piece, axis=1) for piece in pieces)
    value_rows = value_rows.astype(BF16)
    value_out[...] = value_rows
    map_high, map_low = split_low(wide_map(feature_map))
    in_first, in_last = edge_masks(column_of(segment_row))
    totals = []
    for chunk in range(resid.shape[1] // CHUNK):
        lanes = lanes_of(chunk, CHUNK)
        feats = lanes_of(chunk, FEAT_CHUNK)
        turned = []
        for source, scaled_out, phi_out in (
            (queries, query_out, phi_query_out),
            (key_rows, key_out, phi_key_out),
        ):
            part = source[:, lanes]
            scaled = part * cosine + swap_halves(part) * sine
            scaled_out[:, lanes] = scaled
            phi = features(scaled, map_high, map_low).astype(BF16)
            phi_out[:, feats] = phi
            turned.append(phi)
        edges = edges_of(turned[1], in_first, in_last)
        summary_out[feats, :] = edge_summary(edges, value_rows[:, lanes])
        totals.append(jnp.sum(edges.astype(F32), axis=0, keepdims=True))
    store_totals(summary_out, totals)


def mix_kernel(
    plans, resid, vectors, bias, phi_query, phi_key, value, segment_row, recv_one, recv_two,
    recv_three, coefficients, *rest
):
    out_refs, up_refs, down_refs, rest = take(rest, *plans)
    (context_out, inverse_out, middle_out, slope_out, active_keep, pack_out, resid_out, out_weight, up_weight,
     down_weight, sems) = rest
    bases = [0, copy_count(plans[0]), copy_count(plans[0]) + copy_count(plans[1])]
    out_waits = fetch(out_refs, plans[0], out_weight, sems, bases[0], (512, 768))
    up_waits = fetch(up_refs, plans[1], up_weight, sems, bases[1], (0, 768))
    down_waits = fetch(down_refs, plans[2], down_weight, sems, bases[2], (0, 768))
    segment_column = column_of(segment_row)
    same = (segment_column == segment_row[...]).astype(F32)
    in_first, in_last = edge_masks(segment_column)
    totals = combine_edges((recv_one, recv_two, recv_three), coefficients)
    rows = resid.shape[0]
    contexts = []
    for chunk in range(resid.shape[1] // CHUNK):
        lanes = lanes_of(chunk, CHUNK)
        feats = lanes_of(chunk, FEAT_CHUNK)
        query = phi_query[:, feats]
        key = phi_key[:, feats]
        values = value[:, lanes]
        left = []
        right = []
        for head in range(4):
            scores = dot_nt(query * lane_mask(head, FEATS, FEAT_CHUNK), key)
            left.append((scores * same).astype(BF16))
            mask = lane_mask(head, HEAD_DIM, CHUNK)
            right.append(jnp.concatenate([values * mask, jnp.broadcast_to(mask, (rows, CHUNK))], axis=1))
        left.append(edges_of(query, in_first, in_last))
        right.append(spread_edges(totals, chunk))
        both = dot_nn(jnp.concatenate(left, axis=1), jnp.concatenate(right, axis=0))
        inverse = 1.0 / (both[:, CHUNK:] + ATTEND_EPSILON)
        context = both[:, :CHUNK] * inverse
        inverse_out[:, lanes] = inverse
        context_out[:, lanes] = context
        contexts.append(context.astype(BF16))
    context = jnp.concatenate(contexts, axis=1)
    width = resid.shape[1] // 4
    middle = resid[...]
    for slot in range(4):
        arrive(out_waits[slot])
        middle = middle + dot_nt(context[:, lanes_of(slot, width)], matrix(out_weight, slot, 64, 256))
    middle_out[...] = middle
    unit, _ = norm_parts(middle)
    normed = (unit * vectors[2:3, :] + vectors[3:4, :]).astype(BF16)
    pack_out[2] = normed
    output = middle + vectors[4:5, :]
    for slot in range(4):
        arrive(up_waits[slot])
        upper = dot_nn(normed, matrix(up_weight, slot, 0, 768)) + bias[slot : slot + 1, :]
        below = 0.5 * (1.0 + lax.erf(upper * 2.0**-0.5))
        slope = below + upper * (jnp.exp(-0.5 * upper * upper) * 0.3989422804014327)
        active = (upper * below).astype(BF16)
        slope_out[slot] = slope.astype(BF16)
        if slot % 2 == 0:
            active_keep[slot // 2] = active
        else:
            pack_out[slot // 2] = active
        arrive(down_waits[slot])
        output = output + dot_nt(active, matrix(down_weight, slot, 0, 768))
    resid_out[...] = output


def back_mix_kernel(
    plans, grad, vectors, middle, slope, inverse, context, phi_query, segment_row, *rest
):
    out_refs, up_refs, down_refs, rest = take(rest, *plans)
    (upper_keep, pack_out, middle_grad_out, numer_out, denom_out, summary_out, vector_out,
     bias_out, out_weight, up_weight, down_weight, sems) = rest
    bases = [0, copy_count(plans[0]), copy_count(plans[0]) + copy_count(plans[1])]
    down_waits = fetch(down_refs, plans[2], down_weight, sems, bases[2], (0, 768))
    up_waits = fetch(up_refs, plans[1], up_weight, sems, bases[1], (0, 768))
    out_waits = fetch(out_refs, plans[0], out_weight, sems, bases[0], (512, 768))
    grad_out = grad[...]
    branch = grad_out.astype(BF16)
    shift_out = jnp.sum(branch.astype(F32), axis=0, keepdims=True)
    normed_grad = None
    for slot in range(4):
        arrive(down_waits[slot])
        hidden = dot_nn(branch, matrix(down_weight, slot, 0, 768))
        upper = (hidden * slope[slot].astype(F32)).astype(BF16)
        if slot % 2 == 0:
            upper_keep[slot // 2] = upper
        else:
            pack_out[slot // 2] = upper
        bias_out[slot : slot + 1, :] = jnp.sum(upper.astype(F32), axis=0, keepdims=True)
        arrive(up_waits[slot])
        part = dot_nt(upper, matrix(up_weight, slot, 0, 768))
        normed_grad = part if normed_grad is None else normed_grad + part
    inward, gain_grad, shift_grad = norm_backward(middle[...], vectors[2:3, :], normed_grad)
    middle_grad = grad_out + inward
    middle_grad_out[...] = middle_grad
    attn = middle_grad.astype(BF16)
    pack_out[2] = attn
    zero_row = jnp.zeros_like(shift_out)
    vector_out[...] = jnp.concatenate([zero_row, zero_row, gain_grad, shift_grad, shift_out] + [zero_row] * 3, axis=0)
    pieces = []
    for slot in range(4):
        arrive(out_waits[slot])
        pieces.append(dot_nn(attn, matrix(out_weight, slot, 64, 256)))
    context_grad = jnp.concatenate(pieces, axis=1)
    in_first, in_last = edge_masks(column_of(segment_row))
    head_ones = (iota((CHUNK, CHUNK), 0) // HEAD_DIM == iota((CHUNK, CHUNK), 1) // HEAD_DIM).astype(BF16)
    one_lane = (iota((CHUNK, FEAT_CHUNK), 0) == iota((CHUNK, FEAT_CHUNK), 1) // FEATS * HEAD_DIM).astype(BF16)
    totals = []
    for chunk in range(grad.shape[1] // CHUNK):
        lanes = lanes_of(chunk, CHUNK)
        feats = lanes_of(chunk, FEAT_CHUNK)
        numer = context_grad[:, lanes] * inverse[:, lanes]
        denom = -dot_nn((numer * context[:, lanes]).astype(BF16), head_ones)
        numer = numer.astype(BF16)
        denom = denom.astype(BF16)
        numer_out[:, lanes] = numer
        denom_out[:, lanes] = denom
        edges = edges_of(phi_query[:, feats], in_first, in_last)
        summary_out[feats, :] = edge_summary(edges, numer)
        heads = dot_nn(denom, one_lane)
        weighted = edges.astype(F32) * jnp.concatenate([heads, heads], axis=1)
        totals.append(jnp.sum(weighted, axis=0, keepdims=True))
    store_totals(summary_out, totals)


def back_project_kernel(
    plan, resid, vectors, cosine_part, sine_part, feature_map, segment_row, phi_query, phi_key, value,
    query_scaled, key_scaled, numer, denom, context, middle_grad, recv_one, recv_two, recv_three, back_one,
    back_two, back_three, coefficients, *rest
):
    weight_refs, rest = take(rest, plan)
    stacked_keep, pack_out, grad_out, vector_out, weight, sems = rest
    waits = fetch(weight_refs, plan, weight, sems, 0, (0, weight.shape[4]))
    cosine, sine = turn_tables(cosine_part, sine_part)
    unit, _ = norm_parts(resid[...])
    pack_out[2] = (unit * vectors[0:1, :] + vectors[1:2, :]).astype(BF16)
    segment_column = column_of(segment_row)
    same = (segment_column == segment_row[...]).astype(F32)
    in_first, in_last = edge_masks(segment_column)
    totals = combine_edges((recv_one, recv_two, recv_three), coefficients)
    back_totals = combine_edges((back_one, back_two, back_three), coefficients)
    rows = resid.shape[0]
    map_high, map_low = split_low(wide_map(feature_map))
    spread_high = jnp.concatenate([map_high, feature_ones().astype(BF16)], axis=0)
    spread_low = jnp.concatenate([map_low, jnp.zeros_like(map_low)], axis=0)
    spread_map = jnp.concatenate([spread_high, spread_high, spread_low], axis=1)
    share = jnp.full((rows, CHUNK), 1.0 / HEAD_DIM, BF16)
    grads = [[], [], []]
    for chunk in range(resid.shape[1] // CHUNK):
        lanes = lanes_of(chunk, CHUNK)
        feats = lanes_of(chunk, FEAT_CHUNK)
        query = phi_query[:, feats]
        key = phi_key[:, feats]
        values = value[:, lanes]
        both = jnp.concatenate([numer[:, lanes], denom[:, lanes]], axis=1)
        valued = jnp.concatenate([values, share], axis=1)
        query_left, query_right, key_left, key_right, value_left, value_right = [], [], [], [], [], []
        for head in range(4):
            feat_mask = lane_mask(head, FEATS, FEAT_CHUNK)
            mask = lane_mask(head, HEAD_DIM, CHUNK)
            both_mask = jnp.concatenate([mask, mask], axis=1)
            masked_query = query * feat_mask
            masked_both = both * both_mask
            query_left.append((dot_nt(masked_both, valued) * same).astype(BF16))
            query_right.append(key * feat_mask)
            key_left.append((dot_nt(valued, masked_both) * same).astype(BF16))
            key_right.append(masked_query)
            value_left.append((dot_nt(key, masked_query) * same).astype(BF16))
            value_right.append(masked_both[:, :CHUNK])
        forward_edges = spread_edges(totals, chunk)
        backward_edges = spread_edges(back_totals, chunk)
        query_edges = dot_nt(jnp.concatenate([numer[:, lanes], denom[:, lanes] * share], axis=1), forward_edges)
        key_edges = dot_nt(valued, backward_edges)
        query_edges = query_edges[:, :FEAT_CHUNK] * in_first + query_edges[:, FEAT_CHUNK:] * in_last
        key_edges = key_edges[:, :FEAT_CHUNK] * in_first + key_edges[:, FEAT_CHUNK:] * in_last
        value_left.append(edges_of(key, in_first, in_last))
        value_right.append(backward_edges[:, :CHUNK])
        phi_grads = (
            dot_nn(jnp.concatenate(query_left, axis=1), jnp.concatenate(query_right, axis=0)) + query_edges,
            dot_nn(jnp.concatenate(key_left, axis=1), jnp.concatenate(key_right, axis=0)) + key_edges,
        )
        grads[2].append(dot_nn(jnp.concatenate(value_left, axis=1), jnp.concatenate(value_right, axis=0)))
        for which, phi, scaled in ((0, query, query_scaled), (1, key, key_scaled)):
            high, low_part = split_low(phi_grads[which] * phi.astype(F32))
            wide = dot_nt(jnp.concatenate([high, low_part, high], axis=1), spread_map)
            turned = wide[:, :CHUNK] - scaled[:, lanes] * wide[:, CHUNK:]
            grads[which].append(turned * cosine + swap_halves(turned * sine))
    joined = [jnp.concatenate(item, axis=1).astype(BF16) for item in grads]
    joined.append(context[...].astype(BF16))
    width = resid.shape[1] // 4
    normed_grad = None
    for slot in range(4):
        stacked = jnp.concatenate([item[:, lanes_of(slot, width)] for item in joined], axis=1)
        if slot % 2 == 0:
            stacked_keep[slot // 2] = stacked
        else:
            pack_out[slot // 2] = stacked
        arrive(waits[slot])
        part = dot_nt(stacked[:, : 3 * width], matrix(weight, slot, 0, 3 * width))
        normed_grad = part if normed_grad is None else normed_grad + part
    inward, gain_grad, shift_grad = norm_backward(resid[...], vectors[0:1, :], normed_grad)
    below = middle_grad[...] + inward
    grad_out[...] = below
    pack_out[3] = below.astype(BF16)
    zero_row = jnp.zeros_like(gain_grad)
    vector_out[...] = jnp.concatenate([gain_grad, shift_grad] + [zero_row] * 6, axis=0)


def grad_kernel(quick, splits, right_own, right_other, *rest):
    lefts, (up_keep, up_send, down_keep, down_send, whole) = rest[: 2 * len(splits)], rest[2 * len(splits) :]
    y_bit = lax.axis_index("dp") & 1
    size = up_keep.shape[1]
    joined = []
    for position, (_, own_entry, other_entry) in enumerate(splits):
        own, other = lefts[2 * position], lefts[2 * position + 1]
        own = own[...] if own_entry is None else own[own_entry]
        other = other[...] if other_entry is None else other[other_entry]
        joined.append(jnp.concatenate([own, other], axis=0))
    for position, up_out, down_out in ((1, up_send, down_send), (0, up_keep, down_keep)):
        right = jnp.concatenate([right_own[position], right_other[position]], axis=0)
        start = 0
        for (columns, _, _), left in zip(splits, joined):
            whole[start : start + columns] = dot_tn(right[:, start : start + columns], left).astype(BF16)
            start += columns
        for part in range(2):
            up_out[part] = whole[part * size : (part + 1) * size]
        if not quick:
            for part in range(2):
                down_out[part] = whole[(2 + part) * size : (3 + part) * size]
            continue
        for bit, out in ((y_bit, down_keep), (1 - y_bit, down_send)):
            out[position] = whole[pl.ds(pl.multiple_of((2 + bit) * size, size), size), :]


def sum_of(left, right):
    return (left.astype(F32) + right.astype(F32)).astype(BF16)


def merge_first_kernel(up, up_other, down, down_other, up_keep, up_send, down_keep, down_send):
    y_bit = lax.axis_index("dp") & 1
    up_keep[...] = sum_of(up[y_bit], up_other[y_bit])
    up_send[...] = sum_of(up[1 - y_bit], up_other[1 - y_bit])
    down_keep[...] = sum_of(down[0], down_other[0])
    down_send[...] = sum_of(down[1], down_other[1])


def merge_second_kernel(up, up_other, down, down_other, *rest):
    other, out = rest[:-1], rest[-1]
    for blocks in other:
        out[:2] = blocks[...]
    base = 2 * len(other)
    out[base] = sum_of(up[...], up_other[...])
    out[base + 1] = sum_of(down[...], down_other[...])


def update_kernel(ratio, items, aliased, pieces, *refs):
    width = pieces.shape[2] // 2
    scale = MUON_RATE * ratio**0.5
    olds, news = refs[: 2 * len(items)], refs[2 * len(items) + aliased :]
    for position, (name, base) in enumerate(items):
        old, moment = olds[2 * position : 2 * position + 2]
        new, new_moment, copy = news[3 * position : 3 * position + 3]
        rows = old.shape[2] if name == "out" else old.shape[1]
        for block in range({"query_key": 2, "value": 1, "out": 1}.get(name, 4)):
            both = pieces[base + block, 0:rows].astype(F32)
            if name == "out":
                both = both.T
                grad, ortho = both[:width], both[width:]
            else:
                grad, ortho = both[:, :width], both[:, width:]
            if name == "query_key":
                place = (0, slice(None), block)
            elif name in ("value", "out"):
                place = (0,)
            else:
                place = (0, slice(None), lanes_of(block, width))
            new_moment[place] = MOMENTUM_DECAY * moment[place] + grad
            master = old[place] * (1.0 - MUON_RATE * WEIGHT_DECAY) - scale * ortho
            new[place] = master
            copy[place] = master.astype(BF16)


def ortho_kernel(place, count, moment, *rest):
    terms, extra, (result, whole) = rest[:count], rest[count:-2], rest[-2:]
    pieces, size, _ = moment.shape
    width = whole.shape[1]
    eye = (iota((width, width), 0) == iota((width, width), 1)).astype(F32)

    def exact(left, right, dims=(((1,), (0,)), ((), ()))):
        return lax.dot_general(left, right, dims, precision=EXACT, preferred_element_type=F32)

    pieces_of = [part[term].astype(F32) for part in terms for term in range(part.shape[0])]
    grad = pieces_of[0]
    for term in pieces_of[1:]:
        grad = grad + term
    for piece in range(pieces):
        whole[piece * size : (piece + 1) * size, :] = moment[piece, :, lanes_of(place, width)].astype(F32)
    source = MOMENTUM_DECAY * whole[...].T + grad
    gram = exact(source, source, (((1,), (1,)), ((), ())))
    norm = jnp.sqrt(jnp.sum(gram * eye)) + ORTHO_EPSILON
    gram = gram / (norm * norm)
    chain = None
    for iteration in range(NS_STEPS):
        step = ORTHO_LINEAR * eye + ORTHO_CUBIC * gram + ORTHO_QUINTIC * exact(gram, gram)
        chain = step if iteration == 0 else exact(chain, step)
        if iteration + 1 < NS_STEPS:
            gram = exact(exact(step, gram), step)
    ortho = dot_tn(source.astype(BF16), (chain / norm).astype(BF16))
    for which, value in ((0, grad.T), (1, ortho)):
        for piece in range(pieces):
            result[piece, 0:size, lanes_of(which, width)] = value[piece * size : (piece + 1) * size].astype(BF16)
    for rows in extra:
        half = rows.shape[1] // 2
        spare = result.shape[1] - size
        more = [rows[:, :half], rows[:, half:], jnp.zeros((spare - 2 * rows.shape[0], half), F32)]
        more = jnp.concatenate(more, axis=0).astype(BF16)
        for piece in range(pieces):
            result[piece, size:, :] = more


def vmem(count):
    return [pl.BlockSpec(memory_space=pltpu.VMEM)] * count


def anywhere(count):
    return [pl.BlockSpec(memory_space=pl.ANY)] * count


def scalars():
    return [pl.BlockSpec(memory_space=pltpu.SMEM)]


def shape(dims, dtype=F32):
    return jax.ShapeDtypeStruct(dims, dtype)


def call(kernel, name, in_specs, outs, scratch, flops, moved):
    return pl.pallas_call(
        kernel,
        name=name,
        out_shape=outs,
        in_specs=in_specs,
        out_specs=vmem(len(outs)),
        scratch_shapes=scratch,
        cost_estimate=pl.CostEstimate(flops=int(flops), bytes_accessed=int(moved), transcendentals=0),
        compiler_params=pltpu.CompilerParams(vmem_limit_bytes=VMEM_BYTES),
    )


def weight_scratch(width, lanes):
    return pltpu.VMEM((4, 4, 2, width // 8, lanes), BF16)


def flat(weight):
    return [item for run in weight for item in run[0]]


def plan_of(weight):
    return tuple(tuple(run[1:]) for run in weight)


def project(resid, vectors, tables, feature_map, weight):
    rows, width = resid.shape
    plan = plan_of(weight)
    feats = width // HEAD_DIM * FEATS
    outs = [
        shape((rows, feats), BF16),
        shape((rows, feats), BF16),
        shape((rows, width), BF16),
        shape((rows, width)),
        shape((rows, width)),
        shape((feats + TOTAL_ROWS, 2 * HEAD_DIM), BF16),
    ]
    results = call(
        partial(project_kernel, plan),
        "project",
        vmem(6) + anywhere(ref_count(plan)),
        outs,
        [weight_scratch(width, 640), pltpu.SemaphoreType.DMA((copy_count(plan),))],
        2 * rows * width * width * 3 * 1.5,
        8 * width * width,
    )(resid, vectors, tables.cosine, tables.sine, feature_map, tables.row, *flat(weight))
    state = SimpleNamespace(input=resid)
    state.phi_query, state.phi_key, state.value, state.query, state.key, state.summary = results
    return state


def mix_scratch(width, plans):
    return [
        weight_scratch(width, 256),
        weight_scratch(width, width),
        weight_scratch(width, width),
        pltpu.SemaphoreType.DMA((sum(copy_count(plan) for plan in plans),)),
    ]


def mix(resid, vectors, bias, state, received, tables, weights):
    rows, width = resid.shape
    plans = [plan_of(weight) for weight in weights]
    refs = [item for weight in weights for item in flat(weight)]
    outs = [
        shape((rows, width)),
        shape((rows, width)),
        shape((rows, width)),
        shape((4, rows, width), BF16),
        shape((2, rows, width), BF16),
        shape((3, rows, width), BF16),
        shape((rows, width)),
    ]
    results = call(
        partial(mix_kernel, plans),
        "mix",
        vmem(10) + scalars() + anywhere(len(refs)),
        outs,
        mix_scratch(width, plans),
        2 * rows * width * width * 12,
        20 * width * width,
    )(
        resid, vectors, bias, state.phi_query, state.phi_key, state.value, tables.row,
        *received, tables.shares, *refs,
    )
    (state.context, state.inverse, state.middle, state.slope, state.active_keep, state.mix_pack,
     state.output) = results


def back_mix(grad, vectors, state, tables, weights):
    rows, width = grad.shape
    plans = [plan_of(weight) for weight in weights]
    refs = [item for weight in weights for item in flat(weight)]
    feats = width // HEAD_DIM * FEATS
    outs = [
        shape((2, rows, width), BF16),
        shape((3, rows, width), BF16),
        shape((rows, width)),
        shape((rows, width), BF16),
        shape((rows, width), BF16),
        shape((feats + TOTAL_ROWS, 2 * HEAD_DIM), BF16),
        shape((8, width)),
        shape((4, width)),
    ]
    results = call(
        partial(back_mix_kernel, plans),
        "back_mix",
        vmem(8) + anywhere(len(refs)),
        outs,
        mix_scratch(width, plans),
        2 * rows * width * width * 11,
        20 * width * width,
    )(
        grad, vectors, state.middle, state.slope, state.inverse, state.context, state.phi_query,
        tables.row, *refs,
    )
    (state.upper_keep, state.back_pack, state.middle_grad, state.numer, state.denom, state.back_summary,
     state.vector_two, state.bias_grad) = results


def back_project(resid, vectors, state, received, back_received, tables, feature_map, weight):
    rows, width = resid.shape
    plan = plan_of(weight)
    outs = [
        shape((2, rows, width), BF16),
        shape((4, rows, width), BF16),
        shape((rows, width)),
        shape((8, width)),
    ]
    results = call(
        partial(back_project_kernel, plan),
        "back_project",
        vmem(21) + scalars() + anywhere(ref_count(plan)),
        outs,
        [weight_scratch(width, 640), pltpu.SemaphoreType.DMA((copy_count(plan),))],
        2 * rows * width * width * 8,
        8 * width * width,
    )(
        resid, vectors, tables.cosine, tables.sine, feature_map, tables.row,
        state.phi_query, state.phi_key, state.value, state.query, state.key, state.numer,
        state.denom, state.context, state.middle_grad, *received, *back_received, tables.shares,
        *flat(weight),
    )
    state.stacked_keep, state.stack_pack, state.input_grad, state.vector_one = results


def matrix_grad(quick, splits, right_own, right_other, *lefts):
    width = right_own.shape[2]
    block = shape((2, width // 4, width), BF16)
    return call(
        partial(grad_kernel, quick, splits), "matrix_grad", vmem(2 + len(lefts)), [block] * 4,
        [pltpu.VMEM((width, width), BF16)], 2 * 512 * width * width * 2, 8 * width * width,
    )(right_own, right_other, *lefts)


def down_grad(quick, state, mix_other, branch_own, branch_other, entries):
    splits = ((state.mix_pack.shape[2], *entries),)
    return matrix_grad(quick, splits, state.active_keep, mix_other, branch_own, branch_other)


def up_grad(quick, state, back_other, mix_other):
    splits = ((state.mix_pack.shape[2], 2, 2),)
    return matrix_grad(quick, splits, state.upper_keep, back_other, state.mix_pack, mix_other)


def attend_grad(quick, state, stack_other, back_other):
    width = state.mix_pack.shape[2]
    splits = ((width // 4 * 3, 2, 2), (width // 4, 2, 2))
    return matrix_grad(
        quick, splits, state.stacked_keep, stack_other, state.stack_pack, stack_other, state.back_pack,
        back_other,
    )


def merge(kernel, outs, *operands):
    return call(kernel, "merge", vmem(len(operands)), outs, [], 1, 1)(*operands)


def merge_first(own, others):
    out = shape(own[0].shape[1:], BF16)
    return merge(merge_first_kernel, [out] * 4, own[0], others[0], own[2], others[1])


def merge_second(own, others, *other_blocks):
    out = shape((2 + 2 * len(other_blocks),) + own[0].shape, BF16)
    return merge(merge_second_kernel, [out], own[0], others[0], own[2], others[1], *other_blocks)[0]


def send_first(own):
    return swap_head(own[1], 2), swap_dp(own[3], 1)


def send_second(own):
    return swap_dp(own[1], 1), swap_head(own[3], 2)


def orthogonalize(place, terms, moment, *extra):
    pieces, size, _ = moment.shape
    terms = terms if isinstance(terms, tuple) else (terms,)
    width = terms[0].shape[1]
    spare = 32 if extra else 0
    return call(
        partial(ortho_kernel, place, len(terms)), "ortho", vmem(1 + len(terms) + len(extra)),
        [shape((pieces, size + spare, 2 * width), BF16)], [pltpu.VMEM((pieces * size, width), F32)], 1, 1,
    )(moment, *terms, *extra)[0]


def update(ratio, pieces, items, olds, news):
    def part_of(array, layer):
        dims = array.shape[1:]
        return pl.BlockSpec((1, *dims), lambda step: (layer,) + (0,) * len(dims))

    in_specs, operands, out_specs, outs, before = vmem(1), [pieces], [], [], []
    for name, layer, _ in items:
        for array in olds[name]:
            in_specs.append(part_of(array, layer))
            operands.append(array)
    for name, layer, _ in items:
        for position, like in enumerate((olds[name][0], olds[name][0], olds[name][0])):
            if name in news:
                before.append((news[name][position], len(outs)))
            outs.append(shape(like.shape, BF16 if position == 2 else F32))
            out_specs.append(part_of(like, layer))
    aliases = {len(operands) + position: out for position, (_, out) in enumerate(before)}
    results = pl.pallas_call(
        partial(update_kernel, ratio, [(name, base) for name, _, base in items], len(before)),
        name="update",
        grid=(1,),
        out_shape=outs,
        in_specs=in_specs + anywhere(len(before)),
        out_specs=out_specs,
        input_output_aliases=aliases,
        compiler_params=pltpu.CompilerParams(vmem_limit_bytes=VMEM_BYTES),
    )(*operands, *(array for array, _ in before))
    return {name: results[3 * place : 3 * place + 3] for place, (name, _, _) in enumerate(items)}


def doc_tables(segment_row, rows):
    index = lax.axis_index("head")
    own = lax.dynamic_slice_in_dim(segment_row, index * rows, rows, 0)
    starts = jnp.sum((segment_row[None, :] < own[:, None]).astype(jnp.int32), axis=1, dtype=jnp.int32)
    offsets = (index * rows + jnp.arange(rows, dtype=jnp.int32) - starts).astype(F32)
    half = HEAD_DIM // 2
    frequency = ROPE_BASE ** (-jnp.arange(half, dtype=F32) / half)
    angles = offsets[:, None] * frequency[None, :]
    scale = HEAD_DIM ** (-0.25)
    edges = segment_row.reshape(-1, rows)[:, :: rows - 1]
    others = jnp.stack([lax.dynamic_index_in_dim(edges, index ^ offset, 0, keepdims=False) for offset in (1, 2, 3)])
    mine = jnp.stack([own[0], own[rows - 1]])
    shares = (others[:, None, :] == mine[None, :, None]).astype(F32).reshape(3, 4)
    return SimpleNamespace(
        cosine=jnp.cos(angles) * scale, sine=jnp.sin(angles) * scale, row=own[None, :].astype(F32), shares=shares
    )


def cross_edges(summary, near):
    return swap_head(summary, 2), swap_head(near, 2)


def exchange_edges(summary):
    near = swap_head(summary, 1)
    return near, *cross_edges(summary, near)


def other_slots(values):
    return [swap_head(values, offset) for offset in (1, 2, 3)]


def adam_update(parameter, gradient, first_moment, second_moment):
    first_moment = BETA_FIRST * first_moment + (1.0 - BETA_FIRST) * gradient
    second_moment = BETA_SECOND * second_moment + (1.0 - BETA_SECOND) * gradient * gradient
    first_hat = first_moment / (1.0 - BETA_FIRST**STEP)
    second_hat = second_moment / (1.0 - BETA_SECOND**STEP)
    return (
        parameter - ADAM_RATE * first_hat / (jnp.sqrt(second_hat) + ADAM_EPSILON),
        first_moment,
        second_moment,
    )


def split_columns(matrix, width):
    rows = matrix.shape[0]
    return jnp.transpose(matrix.reshape(rows, -1, width), (1, 0, 2))


def join_columns(blocks):
    count, rows, width = blocks.shape
    return jnp.transpose(blocks, (1, 0, 2)).reshape(rows, count * width)


def attend_shard(query_key, value, out):
    return jnp.concatenate([query_key[:, 0], query_key[:, 1], value, out.T], axis=1).astype(BF16)


def old_blocks(layer, moments, block):
    query_key, value, out, up, down = (moment[layer] for moment in moments)
    return (
        jnp.stack([query_key[:, 0], query_key[:, 1], value, out.T]).astype(BF16),
        jnp.concatenate([split_columns(up, block), split_columns(down.T, block)]).astype(BF16),
    )


def line_parts(line, cuts):
    return [line[:, :, first:last] for first, last in cuts]


def core_vectors(vector_grads, bias_grads):
    vectors = jnp.concatenate(vector_grads)
    biases = jnp.stack(bias_grads)
    width = vectors.shape[1]
    keep, send = biases[:, 0::2].reshape(-1, width), biases[:, 1::2].reshape(-1, width)
    return jnp.concatenate([vectors, keep]), jnp.concatenate([vectors, send])


def across_vectors(total, layers):
    size = total.shape[0] - 2 * layers
    vectors, biases = total[:size], total[size:]
    return jnp.concatenate([vectors, biases[0::2]]), jnp.concatenate([vectors, biases[1::2]])


def per_device(
    block_input,
    cotangent,
    marked,
    segments,
    feature_map,
    vectors,
    bias_up,
    w_query_key,
    w_value,
    w_out,
    w_up,
    w_down,
    moment_query_key,
    moment_value,
    moment_out,
    moment_up,
    moment_down,
    vector_first,
    vector_second,
    bias_first,
    bias_second,
):
    layers = w_value.shape[0]
    block = w_value.shape[2]
    rows, width = block_input.shape
    dp_size = lax.axis_size("dp")
    dp_index = lax.axis_index("dp")
    quick = dp_size == 8 and layers == 2
    moments = (moment_query_key, moment_value, moment_out, moment_up, moment_down)

    def attend_of(layer):
        return attend_shard(w_query_key[layer], w_value[layer], w_out[layer])

    def hidden_of(layer):
        return jnp.concatenate([w_up[layer], w_down[layer].T], axis=1).astype(BF16)

    tables = doc_tables(segments[0], rows)
    resid = block_input.astype(F32)
    biases = []
    gradient = cotangent.astype(F32) * marked[0][:, None].astype(F32)
    states = [None] * layers

    def spread_biases(bias_up):
        slots = [bias_up] + other_slots(bias_up)
        biases.extend(jnp.stack([item[layer] for item in slots]) for layer in range(layers))

    def run_project(layer, resid, weight):
        states[layer] = project(resid, vectors[layer], tables, feature_map[layer], weight)

    def run_mix(layer, received, weights):
        state = states[layer]
        state.received = received
        mix(state.input, vectors[layer], biases[layer], state, received, tables, weights)
        return state.output

    def run_back_mix(layer, gradient, weights):
        back_mix(gradient, vectors[layer], states[layer], tables, weights)

    def run_back_project(layer, back_received, weight):
        state = states[layer]
        back_project(
            state.input, vectors[layer], state, state.received, back_received, tables, feature_map[layer], weight
        )
        return state.input_grad

    if quick:
        half = width // 2
        first = attend_of(0)
        hidden, second_attend, second_hidden = (
            four_times(part) for part in (hidden_of(0), attend_of(1), hidden_of(1))
        )
        line = [first] + [swap_dp(first, offset) for offset in (2, 4, 6)]

        blocks = [old_blocks(layer, moments, block) for layer in (1, 0)]
        (attend_one, hidden_one), (attend_zero, hidden_zero) = blocks
        payload = jnp.concatenate(
            [
                jnp.concatenate([hidden_one[4:], hidden_one[:4]]),
                jnp.concatenate([attend_one, hidden_zero[4:]]),
            ],
            axis=2,
        )
        line, hidden, payload = hold(line, hidden, payload)
        up_line, down_line = (jnp.stack([item[:, cut] for item in line]) for cut in (slice(half), slice(half, width)))
        up_y, down_x = swap_dp(up_line, 1), swap_head(down_line, 2)
        hidden_line = swap_line(hidden)

        up_line, down_line, up_y, down_x = hold(up_line, down_line, up_y, down_x)
        up, down = jnp.stack([up_line, up_y]), jnp.stack([down_line, down_x])
        up_other, down_other = swap_head(up, 2), swap_dp(down, 1)

        up, down, up_other, down_other, resid, held, second_attend = hold(
            up, down, up_other, down_other, resid, vars(tables), second_attend
        )
        vars(tables).update(held)
        cores = swap_all([up, up_other, down, down_other], swap_head, 1)
        cores, hidden_line, second_attend = hold(cores, hidden_line, second_attend)
        weight_one = [
            ((up, cores[0], up_other, cores[1]), "up near", 0, 0, half),
            ((down, cores[2], down_other, cores[3]), "down near", 0, half, half),
        ]
        up_line, down_line = line_parts(hidden_line, ((0, width), (width, 2 * width)))
        up_y, down_x = swap_dp(up_line, 1), swap_head(down_line, 2)
        attend_line = swap_line(second_attend)
        run_project(0, resid, weight_one)
        near = swap_head(states[0].summary, 1)

        up_line, down_line, up_y, down_x, near, attend_line, second_hidden, moments, gradient, late_bias = hold(
            up_line, down_line, up_y, down_x, near, attend_line, second_hidden, moments, gradient, bias_up
        )
        second_line = swap_line(second_hidden)
        spread_biases(late_bias)
        up, down = jnp.stack([up_line, up_y]), jnp.stack([down_line, down_x])
        up_other, down_other = swap_head(up, 2), swap_dp(down, 1)
        both = cross_edges(states[0].summary, near)
        cores = swap_all([up, down], swap_head, 1)
        attend_zero, hidden_zero = old_blocks(0, moments, block)
        payload_late = jnp.concatenate([hidden_zero[:4], attend_zero])

        branch = gradient.astype(BF16)
        branch_other = swap_head(branch, 1)

        cores, up_other, down_other, received, payload_late, branch_other = hold(
            cores, up_other, down_other, (near, *both), payload_late, branch_other
        )
        cores += swap_all([up_other, down_other], swap_head, 1)
        attend_up, attend_down = line_parts(attend_line, ((0, half), (half, width)))
        attend_y, attend_x = swap_dp(attend_up, 1), swap_head(attend_down, 2)
        cores, attend_y, attend_x, second_line, received = hold(cores, attend_y, attend_x, second_line, received)
        weights = [
            (
                weight_one,
                [((up, cores[0], up_other, cores[2]), "up", 0, 0, width)],
                [((down, cores[1], down_other, cores[3]), "down", 0, 0, width)],
            )
        ]
        up, down = jnp.stack([attend_up, attend_y]), jnp.stack([attend_down, attend_x])
        up_other, down_other = swap_head(up, 2), swap_dp(down, 1)
        up_line, down_line = line_parts(second_line, ((0, width), (width, 2 * width)))
        up_y, down_x = swap_dp(up_line, 1), swap_head(down_line, 2)
        resid = run_mix(0, received, weights[0])

        up_other, down_other, up_y, down_x, resid = hold(up_other, down_other, up_y, down_x, resid)
        up_late, down_late = jnp.stack([up_line, up_y]), jnp.stack([down_line, down_x])
        up_late_other, down_late_other = swap_head(up_late, 2), swap_dp(down_late, 1)
        cores = swap_all([up, down, up_other, down_other], swap_head, 1)
        late_cores = swap_all([up_late, down_late], swap_head, 1)
        cores, late_cores, resid = hold(cores, late_cores, resid)
        weight_one = [
            ((up, cores[0], up_other, cores[2]), "up", 0, 0, half),
            ((down, cores[1], down_other, cores[3]), "down", 0, half, half),
        ]
        run_project(1, resid, weight_one)

        summary = states[1].summary
        near = swap_head(summary, 1)
        both = cross_edges(summary, near)
        received, up_late_other, down_late_other, payload = hold(
            (near, *both), up_late_other, down_late_other, payload
        )
        late_cores += swap_all([up_late_other, down_late_other], swap_head, 1)
        weights.append(
            (
                weight_one,
                [((up_late, late_cores[0], up_late_other, late_cores[2]), "up", 0, 0, width)],
                [((down_late, late_cores[1], down_late_other, late_cores[3]), "down", 0, 0, width)],
            )
        )
        moment = swap_owners(payload)
        activations = run_mix(1, received, weights[1])

        moment, mix_pack, activations = hold(moment, states[1].mix_pack, activations)
        mix_other = swap_head(mix_pack, 1)
        down_one = down_grad(quick, states[1], mix_other, branch, branch_other, (None, None))

        down_one, gradient = hold(down_one, gradient)
        down_others = send_first(down_one)
        run_back_mix(1, gradient, weights[1])

        down_others, summary, back_pack = hold(down_others, states[1].back_summary, states[1].back_pack)
        near, back_other = swap_all([summary, back_pack], swap_head, 1)
        down_one = merge_first(down_one, down_others)
        near, back_other, down_one = hold(near, back_other, down_one)
        both = cross_edges(summary, near)
        down_others = send_second(down_one)
        up_one = up_grad(quick, states[1], back_other, mix_other)

        back_received, up_one, down_others = hold((near, *both), up_one, down_others)
        up_others = send_first(up_one)
        moment_late = swap_owners(payload_late)
        gradient = run_back_project(1, back_received, weights[1][0])

        up_others, gradient, stack_pack, mix_pack, moment_late = hold(
            up_others, gradient, states[1].stack_pack, states[0].mix_pack, moment_late
        )
        stack_other, mix_other = swap_all([stack_pack, mix_pack], swap_head, 1)
        up_one = merge_first(up_one, up_others)
        stack_other, mix_other, up_one = hold(stack_other, mix_other, up_one)
        up_others = send_second(up_one)
        down_blocks = merge_second(down_one, down_others)
        attend_one = attend_grad(quick, states[1], stack_other, back_other)

        attend_one, up_others, gradient = hold(attend_one, up_others, gradient)
        attend_others = send_first(attend_one)
        pair_one = swap_line(merge_second(up_one, up_others, down_blocks))
        run_back_mix(0, gradient, weights[0])

        attend_others, summary, back_pack = hold(attend_others, states[0].back_summary, states[0].back_pack)
        near, back_other = swap_all([summary, back_pack], swap_head, 1)
        attend_one = merge_first(attend_one, attend_others)
        near, back_other, attend_one = hold(near, back_other, attend_one)
        both = cross_edges(summary, near)
        attend_others = send_second(attend_one)
        down_zero = down_grad(quick, states[0], mix_other, stack_pack, stack_other, (3, 3))

        back_received, down_zero, attend_others = hold((near, *both), down_zero, attend_others)
        down_others = send_first(down_zero)
        gradient = run_back_project(0, back_received, weights[0][0])

        down_others, stack_pack, pair_one = hold(down_others, states[0].stack_pack, pair_one)
        stack_other = swap_head(stack_pack, 1)
        vector_grads = [(state.vector_one + state.vector_two)[:5] for state in states]
        kept, sent = core_vectors(vector_grads, [state.bias_grad for state in states])
        came = swap_head(sent, 1)
        up_zero = up_grad(quick, states[0], back_other, mix_other)
        down_zero = merge_first(down_zero, down_others)
        up_zero, down_zero, stack_other, one, one_others, came = hold(
            up_zero, down_zero, stack_other, attend_one, attend_others, came
        )
        down_others = send_second(down_zero)
        up_others = send_first(up_zero)
        attend_blocks = merge_second(one, one_others)
        kept, sent = across_vectors(kept + came, layers)
        came = swap_head(sent, 2)
        attend_zero = attend_grad(quick, states[0], stack_other, back_other)

        attend_zero, down_others, came = hold(attend_zero, down_others, came)
        attend_others = send_first(attend_zero)
        pair_two = swap_line(merge_second(down_zero, down_others, attend_blocks))
        back_one = orthogonalize(0, pair_one, moment, kept + came)

        up_others, back_one = hold(up_others, back_one)
        up_zero = merge_first(up_zero, up_others)
        up_kept = up_zero[0], up_zero[2]
        up_others = send_second(up_zero)

        attend_others, pair_two, back_one, up_kept = hold(attend_others, pair_two, back_one, up_kept)
        attend_zero = merge_first(attend_zero, attend_others)
        attend_kept = attend_zero[0], attend_zero[2]
        attend_others = send_second(attend_zero)
        pieces_one = swap_owners(back_one)
        back_two = orthogonalize(1, pair_two, moment)

        attend_others, up_others, back_two = hold(attend_others, up_others, back_two)
        up_blocks = merge_second((up_kept[0], None, up_kept[1]), up_others)
        pair_three = merge_second((attend_kept[0], None, attend_kept[1]), attend_others, up_blocks)
        pair_three, pieces_one = hold(pair_three, pieces_one)
        pair_three = swap_line(pair_three)

        pair_three, back_two = hold(pair_three, back_two)
        pieces_two = swap_owners(back_two)
        back_three = orthogonalize(0, pair_three, moment_late)

        pieces_two, back_three = hold(pieces_two, back_three)
        pieces_three = swap_owners(back_three)
        packed = jnp.sum(pieces_one[:, moments[1].shape[1] :].astype(F32), axis=0)
        packed = packed[: 2 * kept.shape[0]]
        packed = jnp.concatenate([packed[: kept.shape[0]], packed[kept.shape[0] :]], axis=1)
        plan = [
            (pieces_one, [("up", 1, 4), ("down", 1, 0)]),
            (pieces_two, [("down", 0, 4), ("query_key", 1, 0), ("value", 1, 2), ("out", 1, 3)]),
            (pieces_three, [("up", 0, 0), ("query_key", 0, 4), ("value", 0, 6), ("out", 0, 7)]),
        ]
    else:
        spread_biases(bias_up)
        weights = []
        for layer in range(layers):
            parts = []
            for part in (attend_of(layer), w_up[layer].astype(BF16), w_down[layer].T.astype(BF16)):
                whole = lax.all_gather(part, "dp", axis=0, tiled=True).reshape(4, 2, width // 8, -1)
                parts.append([([whole] + other_slots(whole), "whole", 0, 0, width)])
            weights.append(tuple(parts))
        for layer in range(layers):
            run_project(layer, resid, weights[layer][0])
            resid = run_mix(layer, exchange_edges(states[layer].summary), weights[layer])
        activations = resid
        raw = []
        for layer in reversed(range(layers)):
            state = states[layer]
            branch = gradient.astype(BF16)
            run_back_mix(layer, gradient, weights[layer])
            gradient = run_back_project(layer, exchange_edges(state.back_summary), weights[layer][0])
            back_other, mix_other, stack_other, branch_other = swap_all(
                [state.back_pack, state.mix_pack, state.stack_pack, branch], swap_head, 1
            )
            for own in (
                attend_grad(quick, state, stack_other, back_other),
                up_grad(quick, state, back_other, mix_other),
                down_grad(quick, state, mix_other, branch, branch_other, (None, None)),
            ):
                for keep, send in ((own[0], own[1]), (own[2], own[3])):
                    raw.append(keep.astype(F32) + swap_head(send, 2).astype(F32))
        count = layers * 12
        padded = -(-count // dp_size) * dp_size
        grads = jnp.concatenate(raw)
        grads = jnp.concatenate([grads, jnp.zeros((padded - count,) + grads.shape[1:], F32)])
        grads = lax.psum_scatter(grads, "dp", scatter_dimension=0, tiled=True)
        old = [part for layer in reversed(range(layers)) for part in old_blocks(layer, moments, block)]
        old = jnp.concatenate(old)
        old = jnp.concatenate([old, jnp.zeros((padded - count,) + old.shape[1:], old.dtype)])
        old = lax.all_to_all(old, "dp", split_axis=0, concat_axis=1, tiled=True)
        owned = padded // dp_size
        back = jnp.concatenate(
            [orthogonalize(0, grads[place : place + 1], old[place : place + 1]) for place in range(owned)]
        )
        back = jnp.stack([back[..., :block], back[..., block:]], axis=1)
        back = lax.all_to_all(back, "dp", split_axis=2, concat_axis=0, tiled=True)
        back = jnp.concatenate([back[:, 0], back[:, 1]], axis=2)
        ordered = [back[12 * place : 12 * (place + 1)] for place in reversed(range(layers))]
        plan = [
            (part, [("query_key", layer, 0), ("value", layer, 2), ("out", layer, 3), ("up", layer, 4), ("down", layer, 8)])
            for layer, part in enumerate(ordered)
        ]
        vector_grads = [(state.vector_one + state.vector_two)[:5] for state in states]
        kept, sent = core_vectors(vector_grads, [state.bias_grad for state in states])
        kept, sent = across_vectors(kept + swap_head(sent, 1), layers)
        packed = lax.psum(kept + swap_head(sent, 2), "dp")

    vector_total, bias_total = packed[: 5 * layers].reshape(vectors.shape), packed[5 * layers :]
    olds = {
        "query_key": (w_query_key, moment_query_key),
        "value": (w_value, moment_value),
        "out": (w_out, moment_out),
        "up": (w_up, moment_up),
        "down": tuple(jnp.transpose(item, (0, 2, 1)) for item in (w_down, moment_down)),
    }
    news = {}
    for pieces, items in plan:
        news.update(update(width // block, pieces, items, olds, news))
    news["down"] = [jnp.transpose(item, (0, 2, 1)) for item in news["down"]]
    next_masters, next_moments, copies = zip(*(news[name] for name in ("query_key", "value", "out", "up", "down")))
    vectors_next, vector_first_next, vector_second_next = adam_update(
        vectors, vector_total, vector_first, vector_second
    )
    bias_next, bias_first_next, bias_second_next = adam_update(bias_up, bias_total, bias_first, bias_second)
    return (
        (activations.astype(BF16), gradient)
        + next_masters
        + next_moments
        + copies
        + (vectors_next, vector_first_next, vector_second_next, bias_next, bias_first_next, bias_second_next)
    )


def solution(mesh):
    shards = (
        P(None, "dp", None, "head"),
        P(None, "dp", "head"),
        P(None, "head", "dp"),
        P(None, "dp", "head"),
        P(None, "head", "dp"),
    )
    rows = P(("dp", "head"), None)
    placed = (
        (rows, rows, P("dp", "head"), P("dp", None), P(), P(), P(None, "head"))
        + shards
        + shards
        + (P(), P(), P(None, "head"), P(None, "head"))
    )
    return jax.shard_map(
        per_device,
        mesh=mesh,
        in_specs=placed,
        out_specs=(rows, rows) + shards + shards + shards + (P(), P(), P()) + (P(None, "head"),) * 3,
        check_vma=False,
    )
```

```python
from functools import partial
from types import SimpleNamespace

import jax
import jax.numpy as jnp
from jax import lax
from jax.experimental import pallas as pl
from jax.experimental.pallas import tpu as pltpu
from jax.sharding import PartitionSpec as P

HEAD_DIM = 64
FEATS = 32
NS_STEPS = 5
STEP = 10


ORTHO_LINEAR = 3.4445
ORTHO_CUBIC = -4.775
ORTHO_QUINTIC = 2.0315
ORTHO_EPSILON = 1e-07
MOMENTUM_DECAY = 0.95
MUON_RATE = 0.2
WEIGHT_DECAY = 0.1
BETA_FIRST = 0.9
BETA_SECOND = 0.99
ADAM_RATE = 0.2
ADAM_EPSILON = 1e-08
NORM_EPSILON = 1e-05
ATTEND_EPSILON = 1e-06
ROPE_BASE = 10000.0
EXACT = lax.Precision.HIGHEST

F32 = jnp.float32
BF16 = jnp.bfloat16
CHUNK = 4 * HEAD_DIM
FEAT_CHUNK = 4 * FEATS
TOTAL_ROWS = 16
VMEM_BYTES = 56 * 1024 * 1024


def dot_nn(left, right):
    return lax.dot_general(left, right, (((1,), (0,)), ((), ())), preferred_element_type=F32)


def dot_nt(left, right):
    return lax.dot_general(left, right, (((1,), (1,)), ((), ())), preferred_element_type=F32)


def dot_tn(left, right):
    return lax.dot_general(left, right, (((0,), (0,)), ((), ())), preferred_element_type=F32)


def iota(shape, axis):
    return lax.broadcasted_iota(jnp.int32, shape, axis)


def swap_head(values, offset):
    return lax.ppermute(values, "head", [(h, h ^ offset) for h in range(lax.axis_size("head"))])


def swap_dp(values, offset):
    return lax.ppermute(values, "dp", [(d, d ^ offset) for d in range(lax.axis_size("dp"))])


def swap_all(items, swap, offset):
    return [swap(item, offset) for item in items]


def swap_line(parts):
    groups = [[z * 2 + y for z in range(4)] for y in range(2)]
    return lax.all_to_all(parts, "dp", split_axis=0, concat_axis=0, axis_index_groups=groups, tiled=True)


def four_times(part):
    return jnp.broadcast_to(part[None], (4,) + part.shape)


def swap_owners(parts):
    return lax.all_to_all(parts, "dp", split_axis=0, concat_axis=0, tiled=True)


def hold(*values):
    return lax.optimization_barrier(values)


def sources(kind, slot):
    core, across = slot & 1, slot >> 1
    if kind == "whole":
        return [(slot, None, None)]
    if "up" in kind:
        return [(slot, 0, 0), (slot, 1, 1)]
    return [(core, across, 0), (2 + core, across, 1)]


def fetch(refs, plan, scratch, sems, base, lanes):
    index = lax.axis_index("dp")
    waits = [[], [], [], []]
    count = base
    for position, (kind, source_lane, lane, width) in enumerate(plan):
        first, last = max(lane, lanes[0]), min(lane + width, lanes[1])
        if first >= last:
            continue
        taken = pl.ds(source_lane + first - lane, last - first)
        given = pl.ds(first - lanes[0], last - first)
        for slot in range(4):
            for array, entry, y_offset in sources(kind, slot):
                ref = refs[4 * position + array]
                if kind == "whole":
                    pairs = [(ref.at[:, :, :, taken], scratch.at[slot, :, :, :, given])]
                elif "near" in kind:
                    pairs = [
                        (
                            ref.at[entry, offset, :, taken],
                            scratch.at[slot, (index >> 1) ^ offset, (index & 1) ^ y_offset, :, given],
                        )
                        for offset in range(4)
                    ]
                else:
                    pairs = [(ref.at[entry, :, :, taken], scratch.at[slot, :, (index & 1) ^ y_offset, :, given])]
                for source, target in pairs:
                    copy = pltpu.make_async_copy(source, target, sems.at[count])
                    copy.start()
                    waits[slot].append(copy)
                    count += 1
    return waits


def matrix(scratch, slot, first, last):
    value = scratch[slot]
    return value.reshape(-1, value.shape[-1])[:, first:last]


def ref_count(plan):
    return 4 * len(plan)


def copy_count(plan):
    return sum(4 if run[0] == "whole" else 32 if "near" in run[0] else 8 for run in plan)


def take(refs, *plans):
    taken = []
    for plan in plans:
        taken.append(refs[: ref_count(plan)])
        refs = refs[ref_count(plan) :]
    return (*taken, refs)


def arrive(copies):
    for copy in copies:
        copy.wait()


def norm_parts(values):
    row_mean = jnp.mean(values, axis=-1, keepdims=True)
    centred = values - row_mean
    variance = jnp.mean(centred * centred, axis=-1, keepdims=True)
    scale = lax.rsqrt(variance + NORM_EPSILON)
    return centred * scale, scale


def norm_backward(values, gain, incoming):
    unit, scale = norm_parts(values)
    gain_grad = jnp.sum(incoming * unit, axis=0, keepdims=True)
    shift_grad = jnp.sum(incoming, axis=0, keepdims=True)
    inner = incoming * gain
    inner_mean = jnp.mean(inner, axis=-1, keepdims=True)
    along = jnp.mean(inner * unit, axis=-1, keepdims=True)
    return scale * (inner - inner_mean - unit * along), gain_grad, shift_grad


def swap_halves(values):
    width = values.shape[1]
    half = HEAD_DIM // 2
    lower = iota(values.shape, 1) % HEAD_DIM < half
    return jnp.where(lower, pltpu.roll(values, width - half, 1), pltpu.roll(values, half, 1))


def split_low(values):
    high = values.astype(BF16)
    return high, (values - high.astype(F32)).astype(BF16)


def lane_mask(index, per_head, width):
    return (iota((1, width), 1) // per_head == index).astype(BF16)


def turn_tables(cosine, sine):
    part, other = cosine[...], sine[...]
    return (
        jnp.concatenate([part] * (2 * CHUNK // HEAD_DIM), axis=1),
        jnp.concatenate([-other, other] * (CHUNK // HEAD_DIM), axis=1),
    )


def wide_map(feature_map):
    tall = jnp.concatenate([feature_map[...]] * 4, axis=0)
    return jnp.where(feature_ones(), jnp.concatenate([tall] * 4, axis=1), 0.0)


def feature_ones():
    return iota((CHUNK, FEAT_CHUNK), 0) // HEAD_DIM == iota((CHUNK, FEAT_CHUNK), 1) // FEATS


def features(values, map_high, map_low):
    high, low_part = split_low(values)
    square_high, square_low = split_low(0.5 * values * values)
    ones = -feature_ones().astype(BF16)
    left = jnp.concatenate([high, low_part, high, square_high, square_low], axis=1)
    right = jnp.concatenate([map_high, map_high, map_low, ones, ones], axis=0)
    return jnp.exp(dot_nn(left, right)) * FEATS ** (-0.5)


def fold_matrix():
    rows, columns = iota((CHUNK, HEAD_DIM), 0), iota((CHUNK, HEAD_DIM), 1)
    return (rows % HEAD_DIM == columns).astype(BF16)


def spread_matrix():
    rows = iota((2 * HEAD_DIM, 2 * CHUNK), 0)
    columns = iota((2 * HEAD_DIM, 2 * CHUNK), 1)
    return (columns // CHUNK * HEAD_DIM + columns % HEAD_DIM == rows).astype(BF16)


def same_head(feature_rows):
    shape = (feature_rows, 2 * CHUNK)
    return iota(shape, 0) % FEAT_CHUNK // FEATS == iota(shape, 1) % CHUNK // HEAD_DIM


def column_of(segment_row):
    return jnp.broadcast_to(segment_row[...], (8, segment_row.shape[1])).T[:, 0:1]


def edge_masks(segment_column):
    first = segment_column[0:1, :]
    last = segment_column[segment_column.shape[0] - 1 :, :]
    in_first = (segment_column == first).astype(F32)
    in_last = (segment_column == last).astype(F32) * (1.0 - in_first)
    return in_first, in_last


def edge_summary(edges, weighted):
    full = dot_tn(edges, weighted)
    full = jnp.where(same_head(2 * FEAT_CHUNK)[:, :CHUNK], full, 0.0).astype(BF16)
    folded = dot_nn(full, fold_matrix())
    return jnp.concatenate([folded[:FEAT_CHUNK], folded[FEAT_CHUNK:]], axis=1).astype(BF16)


def store_totals(summary_out, rows):
    pieces = [piece for row in rows for piece in (row[:, :FEAT_CHUNK], row[:, FEAT_CHUNK:])]
    pieces.append(jnp.zeros((TOTAL_ROWS - len(pieces), FEAT_CHUNK), F32))
    summary_out[summary_out.shape[0] - TOTAL_ROWS :, :] = jnp.concatenate(pieces, axis=0).astype(BF16)


def edges_of(phi, in_first, in_last):
    wide = phi.astype(F32)
    return jnp.concatenate([wide * in_first, wide * in_last], axis=1).astype(BF16)


def open_edges(ref, which):
    feats = ref.shape[0] - TOTAL_ROWS
    totals = ref[feats:, :]
    columns = []
    for chunk in range(feats // FEAT_CHUNK):
        pick = (iota((TOTAL_ROWS, HEAD_DIM), 0) == 2 * chunk + which).astype(BF16)
        columns.append(dot_tn(totals, pick))
    sums = ref[:feats, lanes_of(which, HEAD_DIM)].astype(F32)
    return jnp.concatenate([sums, jnp.concatenate(columns, axis=0)], axis=1)


def combine_edges(received, coefficients):
    totals = [None, None]
    rows = (received[0].shape[0] - TOTAL_ROWS) // 4
    for position, ref in enumerate(received):
        offset = position + 1
        pair = []
        for which in range(2):
            value = open_edges(ref, which)
            pair.append(
                jnp.concatenate(
                    [value[(slot ^ offset) * rows : ((slot ^ offset) + 1) * rows] for slot in range(4)], axis=0
                )
            )
        for which in range(2):
            part = coefficients[position, 2 * which] * pair[0] + coefficients[position, 2 * which + 1] * pair[1]
            totals[which] = part if totals[which] is None else totals[which] + part
    return totals


def spread_edges(totals, chunk):
    rows = slice(chunk * FEAT_CHUNK, (chunk + 1) * FEAT_CHUNK)
    joined = jnp.concatenate([totals[0][rows], totals[1][rows]], axis=0).astype(BF16)
    return jnp.where(same_head(2 * FEAT_CHUNK), dot_nn(joined, spread_matrix()), 0.0).astype(BF16)


def lanes_of(slot, width):
    return slice(slot * width, (slot + 1) * width)


def project_kernel(plan, resid, vectors, cosine_part, sine_part, feature_map, segment_row, *rest):
    weight_refs, rest = take(rest, plan)
    phi_query_out, phi_key_out, value_out, centre_out, query_out, key_out, summary_out, weight, sems = rest
    waits = fetch(weight_refs, plan, weight, sems, 0, (0, weight.shape[4]))
    cosine, sine = turn_tables(cosine_part, sine_part)
    unit, _ = norm_parts(resid[...])
    normed = (unit * vectors[0:1, :] + vectors[1:2, :]).astype(BF16)
    width = resid.shape[1] // 4
    rows = resid.shape[0]
    shift = jnp.broadcast_to(vectors[1:2, :], (16, resid.shape[1])).astype(BF16)
    normed = jnp.concatenate([normed, shift], axis=0)
    pieces = [[], [], []]
    for slot in range(4):
        arrive(waits[slot])
        product = dot_nn(normed, matrix(weight, slot, 0, 3 * width))
        for which in range(3):
            pieces[which].append(product[:, lanes_of(which, width)])
    queries, key_rows, value_rows = (jnp.concatenate(piece, axis=1) for piece in pieces)
    queries, key_rows = queries[:rows], key_rows[:rows]
    centre = value_rows[rows : rows + 8]
    centre_out[...] = centre
    value_rows = (value_rows[:rows] - centre[0:1]).astype(BF16)
    value_out[...] = value_rows
    map_high, map_low = split_low(wide_map(feature_map))
    in_first, in_last = edge_masks(column_of(segment_row))
    totals = []
    for chunk in range(resid.shape[1] // CHUNK):
        lanes = lanes_of(chunk, CHUNK)
        feats = lanes_of(chunk, FEAT_CHUNK)
        turned = []
        for source, scaled_out, phi_out in (
            (queries, query_out, phi_query_out),
            (key_rows, key_out, phi_key_out),
        ):
            part = source[:, lanes]
            scaled = part * cosine + swap_halves(part) * sine
            scaled_out[:, lanes] = scaled
            phi = features(scaled, map_high, map_low).astype(BF16)
            phi_out[:, feats] = phi
            turned.append(phi)
        edges = edges_of(turned[1], in_first, in_last)
        summary_out[feats, :] = edge_summary(edges, value_rows[:, lanes])
        totals.append(jnp.sum(edges.astype(F32), axis=0, keepdims=True))
    store_totals(summary_out, totals)


def mix_kernel(
    plans, resid, vectors, bias, phi_query, phi_key, value, centre, segment_row, recv_one, recv_two,
    recv_three, coefficients, *rest
):
    out_refs, up_refs, down_refs, rest = take(rest, *plans)
    (context_out, inverse_out, middle_out, slope_out, active_keep, pack_out, resid_out, out_weight, up_weight,
     down_weight, sems) = rest
    bases = [0, copy_count(plans[0]), copy_count(plans[0]) + copy_count(plans[1])]
    out_waits = fetch(out_refs, plans[0], out_weight, sems, bases[0], (512, 768))
    up_waits = fetch(up_refs, plans[1], up_weight, sems, bases[1], (0, 768))
    down_waits = fetch(down_refs, plans[2], down_weight, sems, bases[2], (0, 768))
    segment_column = column_of(segment_row)
    same = (segment_column == segment_row[...]).astype(F32)
    in_first, in_last = edge_masks(segment_column)
    totals = combine_edges((recv_one, recv_two, recv_three), coefficients)
    rows = resid.shape[0]
    contexts = []
    for chunk in range(resid.shape[1] // CHUNK):
        lanes = lanes_of(chunk, CHUNK)
        feats = lanes_of(chunk, FEAT_CHUNK)
        query = phi_query[:, feats]
        key = phi_key[:, feats]
        values = value[:, lanes]
        left = []
        right = []
        for head in range(4):
            scores = dot_nt(query * lane_mask(head, FEATS, FEAT_CHUNK), key)
            left.append((scores * same).astype(BF16))
            mask = lane_mask(head, HEAD_DIM, CHUNK)
            right.append(jnp.concatenate([values * mask, jnp.broadcast_to(mask, (rows, CHUNK))], axis=1))
        left.append(edges_of(query, in_first, in_last))
        right.append(spread_edges(totals, chunk))
        both = dot_nn(jnp.concatenate(left, axis=1), jnp.concatenate(right, axis=0))
        inverse = 1.0 / (both[:, CHUNK:] + ATTEND_EPSILON)
        context = (both[:, :CHUNK] + centre[0:1, lanes] * both[:, CHUNK:]) * inverse
        inverse_out[:, lanes] = inverse
        context_out[:, lanes] = context
        contexts.append(context.astype(BF16))
    context = jnp.concatenate(contexts, axis=1)
    width = resid.shape[1] // 4
    middle = resid[...]
    for slot in range(4):
        arrive(out_waits[slot])
        middle = middle + dot_nt(context[:, lanes_of(slot, width)], matrix(out_weight, slot, 64, 256))
    middle_out[...] = middle
    unit, _ = norm_parts(middle)
    normed = (unit * vectors[2:3, :] + vectors[3:4, :]).astype(BF16)
    pack_out[2] = normed
    output = middle + vectors[4:5, :]
    for slot in range(4):
        arrive(up_waits[slot])
        upper = dot_nn(normed, matrix(up_weight, slot, 0, 768)) + bias[slot : slot + 1, :]
        below = 0.5 * (1.0 + lax.erf(upper * 2.0**-0.5))
        slope = below + upper * (jnp.exp(-0.5 * upper * upper) * 0.3989422804014327)
        active = (upper * below).astype(BF16)
        slope_out[slot] = slope.astype(BF16)
        if slot % 2 == 0:
            active_keep[slot // 2] = active
        else:
            pack_out[slot // 2] = active
        arrive(down_waits[slot])
        output = output + dot_nt(active, matrix(down_weight, slot, 0, 768))
    resid_out[...] = output


def back_mix_kernel(
    plans, grad, vectors, middle, slope, inverse, context, centre, phi_query, segment_row, *rest
):
    out_refs, up_refs, down_refs, rest = take(rest, *plans)
    (upper_keep, pack_out, middle_grad_out, numer_out, denom_out, summary_out, vector_out,
     bias_out, out_weight, up_weight, down_weight, sems) = rest
    bases = [0, copy_count(plans[0]), copy_count(plans[0]) + copy_count(plans[1])]
    down_waits = fetch(down_refs, plans[2], down_weight, sems, bases[2], (0, 768))
    up_waits = fetch(up_refs, plans[1], up_weight, sems, bases[1], (0, 768))
    out_waits = fetch(out_refs, plans[0], out_weight, sems, bases[0], (512, 768))
    grad_out = grad[...]
    branch = grad_out.astype(BF16)
    shift_out = jnp.sum(branch.astype(F32), axis=0, keepdims=True)
    normed_grad = None
    for slot in range(4):
        arrive(down_waits[slot])
        hidden = dot_nn(branch, matrix(down_weight, slot, 0, 768))
        upper = (hidden * slope[slot].astype(F32)).astype(BF16)
        if slot % 2 == 0:
            upper_keep[slot // 2] = upper
        else:
            pack_out[slot // 2] = upper
        bias_out[slot : slot + 1, :] = jnp.sum(upper.astype(F32), axis=0, keepdims=True)
        arrive(up_waits[slot])
        part = dot_nt(upper, matrix(up_weight, slot, 0, 768))
        normed_grad = part if normed_grad is None else normed_grad + part
    inward, gain_grad, shift_grad = norm_backward(middle[...], vectors[2:3, :], normed_grad)
    middle_grad = grad_out + inward
    middle_grad_out[...] = middle_grad
    attn = middle_grad.astype(BF16)
    pack_out[2] = attn
    zero_row = jnp.zeros_like(shift_out)
    vector_out[...] = jnp.concatenate([zero_row, zero_row, gain_grad, shift_grad, shift_out] + [zero_row] * 3, axis=0)
    pieces = []
    for slot in range(4):
        arrive(out_waits[slot])
        pieces.append(dot_nn(attn, matrix(out_weight, slot, 64, 256)))
    context_grad = jnp.concatenate(pieces, axis=1)
    in_first, in_last = edge_masks(column_of(segment_row))
    head_ones = (iota((CHUNK, CHUNK), 0) // HEAD_DIM == iota((CHUNK, CHUNK), 1) // HEAD_DIM).astype(BF16)
    one_lane = (iota((CHUNK, FEAT_CHUNK), 0) == iota((CHUNK, FEAT_CHUNK), 1) // FEATS * HEAD_DIM).astype(BF16)
    totals = []
    for chunk in range(grad.shape[1] // CHUNK):
        lanes = lanes_of(chunk, CHUNK)
        feats = lanes_of(chunk, FEAT_CHUNK)
        numer = context_grad[:, lanes] * inverse[:, lanes]
        denom = -dot_nn((numer * (context[:, lanes] - centre[0:1, lanes])).astype(BF16), head_ones)
        numer = numer.astype(BF16)
        denom = denom.astype(BF16)
        numer_out[:, lanes] = numer
        denom_out[:, lanes] = denom
        edges = edges_of(phi_query[:, feats], in_first, in_last)
        summary_out[feats, :] = edge_summary(edges, numer)
        heads = dot_nn(denom, one_lane)
        weighted = edges.astype(F32) * jnp.concatenate([heads, heads], axis=1)
        totals.append(jnp.sum(weighted, axis=0, keepdims=True))
    store_totals(summary_out, totals)


def back_project_kernel(
    plan, resid, vectors, cosine_part, sine_part, feature_map, segment_row, phi_query, phi_key, value,
    query_scaled, key_scaled, numer, denom, context, middle_grad, recv_one, recv_two, recv_three, back_one,
    back_two, back_three, coefficients, *rest
):
    weight_refs, rest = take(rest, plan)
    stacked_keep, pack_out, grad_out, vector_out, weight, sems = rest
    waits = fetch(weight_refs, plan, weight, sems, 0, (0, weight.shape[4]))
    cosine, sine = turn_tables(cosine_part, sine_part)
    unit, _ = norm_parts(resid[...])
    pack_out[2] = (unit * vectors[0:1, :] + vectors[1:2, :]).astype(BF16)
    segment_column = column_of(segment_row)
    same = (segment_column == segment_row[...]).astype(F32)
    in_first, in_last = edge_masks(segment_column)
    totals = combine_edges((recv_one, recv_two, recv_three), coefficients)
    back_totals = combine_edges((back_one, back_two, back_three), coefficients)
    rows = resid.shape[0]
    map_high, map_low = split_low(wide_map(feature_map))
    spread_high = jnp.concatenate([map_high, feature_ones().astype(BF16)], axis=0)
    spread_low = jnp.concatenate([map_low, jnp.zeros_like(map_low)], axis=0)
    spread_map = jnp.concatenate([spread_high, spread_high, spread_low], axis=1)
    share = jnp.full((rows, CHUNK), 1.0 / HEAD_DIM, BF16)
    grads = [[], [], []]
    for chunk in range(resid.shape[1] // CHUNK):
        lanes = lanes_of(chunk, CHUNK)
        feats = lanes_of(chunk, FEAT_CHUNK)
        query = phi_query[:, feats]
        key = phi_key[:, feats]
        values = value[:, lanes]
        both = jnp.concatenate([numer[:, lanes], denom[:, lanes]], axis=1)
        valued = jnp.concatenate([values, share], axis=1)
        query_left, query_right, key_left, key_right, value_left, value_right = [], [], [], [], [], []
        for head in range(4):
            feat_mask = lane_mask(head, FEATS, FEAT_CHUNK)
            mask = lane_mask(head, HEAD_DIM, CHUNK)
            both_mask = jnp.concatenate([mask, mask], axis=1)
            masked_query = query * feat_mask
            masked_both = both * both_mask
            query_left.append((dot_nt(masked_both, valued) * same).astype(BF16))
            query_right.append(key * feat_mask)
            key_left.append((dot_nt(valued, masked_both) * same).astype(BF16))
            key_right.append(masked_query)
            value_left.append((dot_nt(key, masked_query) * same).astype(BF16))
            value_right.append(masked_both[:, :CHUNK])
        forward_edges = spread_edges(totals, chunk)
        backward_edges = spread_edges(back_totals, chunk)
        query_edges = dot_nt(jnp.concatenate([numer[:, lanes], denom[:, lanes] * share], axis=1), forward_edges)
        key_edges = dot_nt(valued, backward_edges)
        query_edges = query_edges[:, :FEAT_CHUNK] * in_first + query_edges[:, FEAT_CHUNK:] * in_last
        key_edges = key_edges[:, :FEAT_CHUNK] * in_first + key_edges[:, FEAT_CHUNK:] * in_last
        value_left.append(edges_of(key, in_first, in_last))
        value_right.append(backward_edges[:, :CHUNK])
        phi_grads = (
            dot_nn(jnp.concatenate(query_left, axis=1), jnp.concatenate(query_right, axis=0)) + query_edges,
            dot_nn(jnp.concatenate(key_left, axis=1), jnp.concatenate(key_right, axis=0)) + key_edges,
        )
        grads[2].append(dot_nn(jnp.concatenate(value_left, axis=1), jnp.concatenate(value_right, axis=0)))
        for which, phi, scaled in ((0, query, query_scaled), (1, key, key_scaled)):
            high, low_part = split_low(phi_grads[which] * phi.astype(F32))
            wide = dot_nt(jnp.concatenate([high, low_part, high], axis=1), spread_map)
            turned = wide[:, :CHUNK] - scaled[:, lanes] * wide[:, CHUNK:]
            grads[which].append(turned * cosine + swap_halves(turned * sine))
    joined = [jnp.concatenate(item, axis=1).astype(BF16) for item in grads]
    joined.append(context[...].astype(BF16))
    width = resid.shape[1] // 4
    normed_grad = None
    for slot in range(4):
        stacked = jnp.concatenate([item[:, lanes_of(slot, width)] for item in joined], axis=1)
        if slot % 2 == 0:
            stacked_keep[slot // 2] = stacked
        else:
            pack_out[slot // 2] = stacked
        arrive(waits[slot])
        part = dot_nt(stacked[:, : 3 * width], matrix(weight, slot, 0, 3 * width))
        normed_grad = part if normed_grad is None else normed_grad + part
    inward, gain_grad, shift_grad = norm_backward(resid[...], vectors[0:1, :], normed_grad)
    below = middle_grad[...] + inward
    grad_out[...] = below
    pack_out[3] = below.astype(BF16)
    zero_row = jnp.zeros_like(gain_grad)
    vector_out[...] = jnp.concatenate([gain_grad, shift_grad] + [zero_row] * 6, axis=0)


def grad_kernel(quick, splits, right_own, right_other, *rest):
    lefts, (up_keep, up_send, down_keep, down_send, whole) = rest[: 2 * len(splits)], rest[2 * len(splits) :]
    y_bit = lax.axis_index("dp") & 1
    size = up_keep.shape[1]
    joined = []
    for position, (_, own_entry, other_entry) in enumerate(splits):
        own, other = lefts[2 * position], lefts[2 * position + 1]
        own = own[...] if own_entry is None else own[own_entry]
        other = other[...] if other_entry is None else other[other_entry]
        joined.append(jnp.concatenate([own, other], axis=0))
    for position, up_out, down_out in ((1, up_send, down_send), (0, up_keep, down_keep)):
        right = jnp.concatenate([right_own[position], right_other[position]], axis=0)
        start = 0
        for (columns, _, _), left in zip(splits, joined):
            whole[start : start + columns] = dot_tn(right[:, start : start + columns], left).astype(BF16)
            start += columns
        for part in range(2):
            up_out[part] = whole[part * size : (part + 1) * size]
        if not quick:
            for part in range(2):
                down_out[part] = whole[(2 + part) * size : (3 + part) * size]
            continue
        for bit, out in ((y_bit, down_keep), (1 - y_bit, down_send)):
            out[position] = whole[pl.ds(pl.multiple_of((2 + bit) * size, size), size), :]


def sum_of(left, right):
    return (left.astype(F32) + right.astype(F32)).astype(BF16)


def merge_first_kernel(up, up_other, down, down_other, up_keep, up_send, down_keep, down_send):
    y_bit = lax.axis_index("dp") & 1
    up_keep[...] = sum_of(up[y_bit], up_other[y_bit])
    up_send[...] = sum_of(up[1 - y_bit], up_other[1 - y_bit])
    down_keep[...] = sum_of(down[0], down_other[0])
    down_send[...] = sum_of(down[1], down_other[1])


def merge_second_kernel(up, up_other, down, down_other, *rest):
    other, out = rest[:-1], rest[-1]
    for blocks in other:
        out[:2] = blocks[...]
    base = 2 * len(other)
    out[base] = sum_of(up[...], up_other[...])
    out[base + 1] = sum_of(down[...], down_other[...])


def update_kernel(ratio, items, aliased, pieces, *refs):
    width = pieces.shape[2] // 2
    scale = MUON_RATE * ratio**0.5
    olds, news = refs[: 2 * len(items)], refs[2 * len(items) + aliased :]
    for position, (name, base) in enumerate(items):
        old, moment = olds[2 * position : 2 * position + 2]
        new, new_moment, copy = news[3 * position : 3 * position + 3]
        rows = old.shape[2] if name == "out" else old.shape[1]
        for block in range({"query_key": 2, "value": 1, "out": 1}.get(name, 4)):
            both = pieces[base + block, 0:rows].astype(F32)
            if name == "out":
                both = both.T
                grad, ortho = both[:width], both[width:]
            else:
                grad, ortho = both[:, :width], both[:, width:]
            if name == "query_key":
                place = (0, slice(None), block)
            elif name in ("value", "out"):
                place = (0,)
            else:
                place = (0, slice(None), lanes_of(block, width))
            new_moment[place] = MOMENTUM_DECAY * moment[place] + grad
            master = old[place] * (1.0 - MUON_RATE * WEIGHT_DECAY) - scale * ortho
            new[place] = master
            copy[place] = master.astype(BF16)


def ortho_kernel(place, count, moment, *rest):
    terms, extra, (result, whole) = rest[:count], rest[count:-2], rest[-2:]
    pieces, size, _ = moment.shape
    width = whole.shape[1]
    eye = (iota((width, width), 0) == iota((width, width), 1)).astype(F32)

    def exact(left, right, dims=(((1,), (0,)), ((), ()))):
        return lax.dot_general(left, right, dims, precision=EXACT, preferred_element_type=F32)

    pieces_of = [part[term].astype(F32) for part in terms for term in range(part.shape[0])]
    grad = pieces_of[0]
    for term in pieces_of[1:]:
        grad = grad + term
    for piece in range(pieces):
        whole[piece * size : (piece + 1) * size, :] = moment[piece, :, lanes_of(place, width)].astype(F32)
    source = MOMENTUM_DECAY * whole[...].T + grad
    gram = exact(source, source, (((1,), (1,)), ((), ())))
    norm = jnp.sqrt(jnp.sum(gram * eye)) + ORTHO_EPSILON
    gram = gram / (norm * norm)
    chain = None
    for iteration in range(NS_STEPS):
        step = ORTHO_LINEAR * eye + ORTHO_CUBIC * gram + ORTHO_QUINTIC * exact(gram, gram)
        chain = step if iteration == 0 else exact(chain, step)
        if iteration + 1 < NS_STEPS:
            gram = exact(exact(step, gram), step)
    ortho = dot_tn(source.astype(BF16), (chain / norm).astype(BF16))
    for which, value in ((0, grad.T), (1, ortho)):
        for piece in range(pieces):
            result[piece, 0:size, lanes_of(which, width)] = value[piece * size : (piece + 1) * size].astype(BF16)
    for rows in extra:
        half = rows.shape[1] // 2
        spare = result.shape[1] - size
        more = [rows[:, :half], rows[:, half:], jnp.zeros((spare - 2 * rows.shape[0], half), F32)]
        more = jnp.concatenate(more, axis=0).astype(BF16)
        for piece in range(pieces):
            result[piece, size:, :] = more


def vmem(count):
    return [pl.BlockSpec(memory_space=pltpu.VMEM)] * count


def anywhere(count):
    return [pl.BlockSpec(memory_space=pl.ANY)] * count


def scalars():
    return [pl.BlockSpec(memory_space=pltpu.SMEM)]


def shape(dims, dtype=F32):
    return jax.ShapeDtypeStruct(dims, dtype)


def call(kernel, name, in_specs, outs, scratch, flops, moved):
    return pl.pallas_call(
        kernel,
        name=name,
        out_shape=outs,
        in_specs=in_specs,
        out_specs=vmem(len(outs)),
        scratch_shapes=scratch,
        cost_estimate=pl.CostEstimate(flops=int(flops), bytes_accessed=int(moved), transcendentals=0),
        compiler_params=pltpu.CompilerParams(vmem_limit_bytes=VMEM_BYTES),
    )


def weight_scratch(width, lanes):
    return pltpu.VMEM((4, 4, 2, width // 8, lanes), BF16)


def flat(weight):
    return [item for run in weight for item in run[0]]


def plan_of(weight):
    return tuple(tuple(run[1:]) for run in weight)


def project(resid, vectors, tables, feature_map, weight):
    rows, width = resid.shape
    plan = plan_of(weight)
    feats = width // HEAD_DIM * FEATS
    outs = [
        shape((rows, feats), BF16),
        shape((rows, feats), BF16),
        shape((rows, width), BF16),
        shape((8, width)),
        shape((rows, width)),
        shape((rows, width)),
        shape((feats + TOTAL_ROWS, 2 * HEAD_DIM), BF16),
    ]
    results = call(
        partial(project_kernel, plan),
        "project",
        vmem(6) + anywhere(ref_count(plan)),
        outs,
        [weight_scratch(width, 640), pltpu.SemaphoreType.DMA((copy_count(plan),))],
        2 * rows * width * width * 3 * 1.5,
        8 * width * width,
    )(resid, vectors, tables.cosine, tables.sine, feature_map, tables.row, *flat(weight))
    state = SimpleNamespace(input=resid)
    state.phi_query, state.phi_key, state.value, state.centre, state.query, state.key, state.summary = results
    return state


def mix_scratch(width, plans):
    return [
        weight_scratch(width, 256),
        weight_scratch(width, width),
        weight_scratch(width, width),
        pltpu.SemaphoreType.DMA((sum(copy_count(plan) for plan in plans),)),
    ]


def mix(resid, vectors, bias, state, received, tables, weights):
    rows, width = resid.shape
    plans = [plan_of(weight) for weight in weights]
    refs = [item for weight in weights for item in flat(weight)]
    outs = [
        shape((rows, width)),
        shape((rows, width)),
        shape((rows, width)),
        shape((4, rows, width), BF16),
        shape((2, rows, width), BF16),
        shape((3, rows, width), BF16),
        shape((rows, width)),
    ]
    results = call(
        partial(mix_kernel, plans),
        "mix",
        vmem(11) + scalars() + anywhere(len(refs)),
        outs,
        mix_scratch(width, plans),
        2 * rows * width * width * 12,
        20 * width * width,
    )(
        resid, vectors, bias, state.phi_query, state.phi_key, state.value, state.centre, tables.row,
        *received, tables.shares, *refs,
    )
    (state.context, state.inverse, state.middle, state.slope, state.active_keep, state.mix_pack,
     state.output) = results


def back_mix(grad, vectors, state, tables, weights):
    rows, width = grad.shape
    plans = [plan_of(weight) for weight in weights]
    refs = [item for weight in weights for item in flat(weight)]
    feats = width // HEAD_DIM * FEATS
    outs = [
        shape((2, rows, width), BF16),
        shape((3, rows, width), BF16),
        shape((rows, width)),
        shape((rows, width), BF16),
        shape((rows, width), BF16),
        shape((feats + TOTAL_ROWS, 2 * HEAD_DIM), BF16),
        shape((8, width)),
        shape((4, width)),
    ]
    results = call(
        partial(back_mix_kernel, plans),
        "back_mix",
        vmem(9) + anywhere(len(refs)),
        outs,
        mix_scratch(width, plans),
        2 * rows * width * width * 11,
        20 * width * width,
    )(
        grad, vectors, state.middle, state.slope, state.inverse, state.context, state.centre, state.phi_query,
        tables.row, *refs,
    )
    (state.upper_keep, state.back_pack, state.middle_grad, state.numer, state.denom, state.back_summary,
     state.vector_two, state.bias_grad) = results


def back_project(resid, vectors, state, received, back_received, tables, feature_map, weight):
    rows, width = resid.shape
    plan = plan_of(weight)
    outs = [
        shape((2, rows, width), BF16),
        shape((4, rows, width), BF16),
        shape((rows, width)),
        shape((8, width)),
    ]
    results = call(
        partial(back_project_kernel, plan),
        "back_project",
        vmem(21) + scalars() + anywhere(ref_count(plan)),
        outs,
        [weight_scratch(width, 640), pltpu.SemaphoreType.DMA((copy_count(plan),))],
        2 * rows * width * width * 8,
        8 * width * width,
    )(
        resid, vectors, tables.cosine, tables.sine, feature_map, tables.row,
        state.phi_query, state.phi_key, state.value, state.query, state.key, state.numer,
        state.denom, state.context, state.middle_grad, *received, *back_received, tables.shares,
        *flat(weight),
    )
    state.stacked_keep, state.stack_pack, state.input_grad, state.vector_one = results


def matrix_grad(quick, splits, right_own, right_other, *lefts):
    width = right_own.shape[2]
    block = shape((2, width // 4, width), BF16)
    return call(
        partial(grad_kernel, quick, splits), "matrix_grad", vmem(2 + len(lefts)), [block] * 4,
        [pltpu.VMEM((width, width), BF16)], 2 * 512 * width * width * 2, 8 * width * width,
    )(right_own, right_other, *lefts)


def down_grad(quick, state, mix_other, branch_own, branch_other, entries):
    splits = ((state.mix_pack.shape[2], *entries),)
    return matrix_grad(quick, splits, state.active_keep, mix_other, branch_own, branch_other)


def up_grad(quick, state, back_other, mix_other):
    splits = ((state.mix_pack.shape[2], 2, 2),)
    return matrix_grad(quick, splits, state.upper_keep, back_other, state.mix_pack, mix_other)


def attend_grad(quick, state, stack_other, back_other):
    width = state.mix_pack.shape[2]
    splits = ((width // 4 * 3, 2, 2), (width // 4, 2, 2))
    return matrix_grad(
        quick, splits, state.stacked_keep, stack_other, state.stack_pack, stack_other, state.back_pack,
        back_other,
    )


def merge(kernel, outs, *operands):
    return call(kernel, "merge", vmem(len(operands)), outs, [], 1, 1)(*operands)


def merge_first(own, others):
    out = shape(own[0].shape[1:], BF16)
    return merge(merge_first_kernel, [out] * 4, own[0], others[0], own[2], others[1])


def merge_second(own, others, *other_blocks):
    out = shape((2 + 2 * len(other_blocks),) + own[0].shape, BF16)
    return merge(merge_second_kernel, [out], own[0], others[0], own[2], others[1], *other_blocks)[0]


def send_first(own):
    return swap_head(own[1], 2), swap_dp(own[3], 1)


def send_second(own):
    return swap_dp(own[1], 1), swap_head(own[3], 2)


def orthogonalize(place, terms, moment, *extra):
    pieces, size, _ = moment.shape
    terms = terms if isinstance(terms, tuple) else (terms,)
    width = terms[0].shape[1]
    spare = 32 if extra else 0
    return call(
        partial(ortho_kernel, place, len(terms)), "ortho", vmem(1 + len(terms) + len(extra)),
        [shape((pieces, size + spare, 2 * width), BF16)], [pltpu.VMEM((pieces * size, width), F32)], 1, 1,
    )(moment, *terms, *extra)[0]


def update(ratio, pieces, items, olds, news):
    def part_of(array, layer):
        dims = array.shape[1:]
        return pl.BlockSpec((1, *dims), lambda step: (layer,) + (0,) * len(dims))

    in_specs, operands, out_specs, outs, before = vmem(1), [pieces], [], [], []
    for name, layer, _ in items:
        for array in olds[name]:
            in_specs.append(part_of(array, layer))
            operands.append(array)
    for name, layer, _ in items:
        for position, like in enumerate((olds[name][0], olds[name][0], olds[name][0])):
            if name in news:
                before.append((news[name][position], len(outs)))
            outs.append(shape(like.shape, BF16 if position == 2 else F32))
            out_specs.append(part_of(like, layer))
    aliases = {len(operands) + position: out for position, (_, out) in enumerate(before)}
    results = pl.pallas_call(
        partial(update_kernel, ratio, [(name, base) for name, _, base in items], len(before)),
        name="update",
        grid=(1,),
        out_shape=outs,
        in_specs=in_specs + anywhere(len(before)),
        out_specs=out_specs,
        input_output_aliases=aliases,
        compiler_params=pltpu.CompilerParams(vmem_limit_bytes=VMEM_BYTES),
    )(*operands, *(array for array, _ in before))
    return {name: results[3 * place : 3 * place + 3] for place, (name, _, _) in enumerate(items)}


def doc_tables(segment_row, rows):
    index = lax.axis_index("head")
    own = lax.dynamic_slice_in_dim(segment_row, index * rows, rows, 0)
    starts = jnp.sum((segment_row[None, :] < own[:, None]).astype(jnp.int32), axis=1, dtype=jnp.int32)
    offsets = (index * rows + jnp.arange(rows, dtype=jnp.int32) - starts).astype(F32)
    half = HEAD_DIM // 2
    frequency = ROPE_BASE ** (-jnp.arange(half, dtype=F32) / half)
    angles = offsets[:, None] * frequency[None, :]
    scale = HEAD_DIM ** (-0.25)
    edges = segment_row.reshape(-1, rows)[:, :: rows - 1]
    others = jnp.stack([lax.dynamic_index_in_dim(edges, index ^ offset, 0, keepdims=False) for offset in (1, 2, 3)])
    mine = jnp.stack([own[0], own[rows - 1]])
    shares = (others[:, None, :] == mine[None, :, None]).astype(F32).reshape(3, 4)
    return SimpleNamespace(
        cosine=jnp.cos(angles) * scale, sine=jnp.sin(angles) * scale, row=own[None, :].astype(F32), shares=shares
    )


def cross_edges(summary, near):
    return swap_head(summary, 2), swap_head(near, 2)


def exchange_edges(summary):
    near = swap_head(summary, 1)
    return near, *cross_edges(summary, near)


def other_slots(values):
    return [swap_head(values, offset) for offset in (1, 2, 3)]


def adam_update(parameter, gradient, first_moment, second_moment):
    first_moment = BETA_FIRST * first_moment + (1.0 - BETA_FIRST) * gradient
    second_moment = BETA_SECOND * second_moment + (1.0 - BETA_SECOND) * gradient * gradient
    first_hat = first_moment / (1.0 - BETA_FIRST**STEP)
    second_hat = second_moment / (1.0 - BETA_SECOND**STEP)
    return (
        parameter - ADAM_RATE * first_hat / (jnp.sqrt(second_hat) + ADAM_EPSILON),
        first_moment,
        second_moment,
    )


def split_columns(matrix, width):
    rows = matrix.shape[0]
    return jnp.transpose(matrix.reshape(rows, -1, width), (1, 0, 2))


def join_columns(blocks):
    count, rows, width = blocks.shape
    return jnp.transpose(blocks, (1, 0, 2)).reshape(rows, count * width)


def attend_shard(query_key, value, out):
    return jnp.concatenate([query_key[:, 0], query_key[:, 1], value, out.T], axis=1).astype(BF16)


def old_blocks(layer, moments, block):
    query_key, value, out, up, down = (moment[layer] for moment in moments)
    return (
        jnp.stack([query_key[:, 0], query_key[:, 1], value, out.T]).astype(BF16),
        jnp.concatenate([split_columns(up, block), split_columns(down.T, block)]).astype(BF16),
    )


def line_parts(line, cuts):
    return [line[:, :, first:last] for first, last in cuts]


def core_vectors(vector_grads, bias_grads):
    vectors = jnp.concatenate(vector_grads)
    biases = jnp.stack(bias_grads)
    width = vectors.shape[1]
    keep, send = biases[:, 0::2].reshape(-1, width), biases[:, 1::2].reshape(-1, width)
    return jnp.concatenate([vectors, keep]), jnp.concatenate([vectors, send])


def across_vectors(total, layers):
    size = total.shape[0] - 2 * layers
    vectors, biases = total[:size], total[size:]
    return jnp.concatenate([vectors, biases[0::2]]), jnp.concatenate([vectors, biases[1::2]])


def per_device(
    block_input,
    cotangent,
    marked,
    segments,
    feature_map,
    vectors,
    bias_up,
    w_query_key,
    w_value,
    w_out,
    w_up,
    w_down,
    moment_query_key,
    moment_value,
    moment_out,
    moment_up,
    moment_down,
    vector_first,
    vector_second,
    bias_first,
    bias_second,
):
    layers = w_value.shape[0]
    block = w_value.shape[2]
    rows, width = block_input.shape
    dp_size = lax.axis_size("dp")
    dp_index = lax.axis_index("dp")
    quick = dp_size == 8 and layers == 2
    moments = (moment_query_key, moment_value, moment_out, moment_up, moment_down)

    def attend_of(layer):
        return attend_shard(w_query_key[layer], w_value[layer], w_out[layer])

    def hidden_of(layer):
        return jnp.concatenate([w_up[layer], w_down[layer].T], axis=1).astype(BF16)

    tables = doc_tables(segments[0], rows)
    resid = block_input.astype(F32)
    biases = []
    gradient = cotangent.astype(F32) * marked[0][:, None].astype(F32)
    states = [None] * layers

    def spread_biases(bias_up):
        slots = [bias_up] + other_slots(bias_up)
        biases.extend(jnp.stack([item[layer] for item in slots]) for layer in range(layers))

    def run_project(layer, resid, weight):
        states[layer] = project(resid, vectors[layer], tables, feature_map[layer], weight)

    def run_mix(layer, received, weights):
        state = states[layer]
        state.received = received
        mix(state.input, vectors[layer], biases[layer], state, received, tables, weights)
        return state.output

    def run_back_mix(layer, gradient, weights):
        back_mix(gradient, vectors[layer], states[layer], tables, weights)

    def run_back_project(layer, back_received, weight):
        state = states[layer]
        back_project(
            state.input, vectors[layer], state, state.received, back_received, tables, feature_map[layer], weight
        )
        return state.input_grad

    if quick:
        half = width // 2
        first = attend_of(0)
        hidden, second_attend, second_hidden = (
            four_times(part) for part in (hidden_of(0), attend_of(1), hidden_of(1))
        )
        line = [first] + [swap_dp(first, offset) for offset in (2, 4, 6)]

        blocks = [old_blocks(layer, moments, block) for layer in (1, 0)]
        (attend_one, hidden_one), (attend_zero, hidden_zero) = blocks
        payload = jnp.concatenate(
            [
                jnp.concatenate([hidden_one[4:], hidden_one[:4]]),
                jnp.concatenate([attend_one, hidden_zero[4:]]),
            ],
            axis=2,
        )
        line, hidden, payload = hold(line, hidden, payload)
        up_line, down_line = (jnp.stack([item[:, cut] for item in line]) for cut in (slice(half), slice(half, width)))
        up_y, down_x = swap_dp(up_line, 1), swap_head(down_line, 2)
        hidden_line = swap_line(hidden)

        up_line, down_line, up_y, down_x = hold(up_line, down_line, up_y, down_x)
        up, down = jnp.stack([up_line, up_y]), jnp.stack([down_line, down_x])
        up_other, down_other = swap_head(up, 2), swap_dp(down, 1)

        up, down, up_other, down_other, resid, held, second_attend = hold(
            up, down, up_other, down_other, resid, vars(tables), second_attend
        )
        vars(tables).update(held)
        cores = swap_all([up, up_other, down, down_other], swap_head, 1)
        cores, hidden_line, second_attend = hold(cores, hidden_line, second_attend)
        weight_one = [
            ((up, cores[0], up_other, cores[1]), "up near", 0, 0, half),
            ((down, cores[2], down_other, cores[3]), "down near", 0, half, half),
        ]
        up_line, down_line = line_parts(hidden_line, ((0, width), (width, 2 * width)))
        up_y, down_x = swap_dp(up_line, 1), swap_head(down_line, 2)
        attend_line = swap_line(second_attend)
        run_project(0, resid, weight_one)
        near = swap_head(states[0].summary, 1)

        up_line, down_line, up_y, down_x, near, attend_line, second_hidden, moments, gradient, late_bias = hold(
            up_line, down_line, up_y, down_x, near, attend_line, second_hidden, moments, gradient, bias_up
        )
        second_line = swap_line(second_hidden)
        spread_biases(late_bias)
        up, down = jnp.stack([up_line, up_y]), jnp.stack([down_line, down_x])
        up_other, down_other = swap_head(up, 2), swap_dp(down, 1)
        both = cross_edges(states[0].summary, near)
        cores = swap_all([up, down], swap_head, 1)
        attend_zero, hidden_zero = old_blocks(0, moments, block)
        payload_late = jnp.concatenate([hidden_zero[:4], attend_zero])

        branch = gradient.astype(BF16)
        branch_other = swap_head(branch, 1)

        cores, up_other, down_other, received, payload_late, branch_other = hold(
            cores, up_other, down_other, (near, *both), payload_late, branch_other
        )
        cores += swap_all([up_other, down_other], swap_head, 1)
        attend_up, attend_down = line_parts(attend_line, ((0, half), (half, width)))
        attend_y, attend_x = swap_dp(attend_up, 1), swap_head(attend_down, 2)
        cores, attend_y, attend_x, second_line, received = hold(cores, attend_y, attend_x, second_line, received)
        weights = [
            (
                weight_one,
                [((up, cores[0], up_other, cores[2]), "up", 0, 0, width)],
                [((down, cores[1], down_other, cores[3]), "down", 0, 0, width)],
            )
        ]
        up, down = jnp.stack([attend_up, attend_y]), jnp.stack([attend_down, attend_x])
        up_other, down_other = swap_head(up, 2), swap_dp(down, 1)
        up_line, down_line = line_parts(second_line, ((0, width), (width, 2 * width)))
        up_y, down_x = swap_dp(up_line, 1), swap_head(down_line, 2)
        resid = run_mix(0, received, weights[0])

        up_other, down_other, up_y, down_x, resid = hold(up_other, down_other, up_y, down_x, resid)
        up_late, down_late = jnp.stack([up_line, up_y]), jnp.stack([down_line, down_x])
        up_late_other, down_late_other = swap_head(up_late, 2), swap_dp(down_late, 1)
        cores = swap_all([up, down, up_other, down_other], swap_head, 1)
        late_cores = swap_all([up_late, down_late], swap_head, 1)
        cores, late_cores, resid = hold(cores, late_cores, resid)
        weight_one = [
            ((up, cores[0], up_other, cores[2]), "up", 0, 0, half),
            ((down, cores[1], down_other, cores[3]), "down", 0, half, half),
        ]
        run_project(1, resid, weight_one)

        summary = states[1].summary
        near = swap_head(summary, 1)
        both = cross_edges(summary, near)
        received, up_late_other, down_late_other, payload = hold(
            (near, *both), up_late_other, down_late_other, payload
        )
        late_cores += swap_all([up_late_other, down_late_other], swap_head, 1)
        weights.append(
            (
                weight_one,
                [((up_late, late_cores[0], up_late_other, late_cores[2]), "up", 0, 0, width)],
                [((down_late, late_cores[1], down_late_other, late_cores[3]), "down", 0, 0, width)],
            )
        )
        moment = swap_owners(payload)
        activations = run_mix(1, received, weights[1])

        moment, mix_pack, activations = hold(moment, states[1].mix_pack, activations)
        mix_other = swap_head(mix_pack, 1)
        down_one = down_grad(quick, states[1], mix_other, branch, branch_other, (None, None))

        down_one, gradient = hold(down_one, gradient)
        down_others = send_first(down_one)
        run_back_mix(1, gradient, weights[1])

        down_others, summary, back_pack = hold(down_others, states[1].back_summary, states[1].back_pack)
        near, back_other = swap_all([summary, back_pack], swap_head, 1)
        down_one = merge_first(down_one, down_others)
        near, back_other, down_one = hold(near, back_other, down_one)
        both = cross_edges(summary, near)
        down_others = send_second(down_one)
        up_one = up_grad(quick, states[1], back_other, mix_other)

        back_received, up_one, down_others = hold((near, *both), up_one, down_others)
        up_others = send_first(up_one)
        moment_late = swap_owners(payload_late)
        gradient = run_back_project(1, back_received, weights[1][0])

        up_others, gradient, stack_pack, mix_pack, moment_late = hold(
            up_others, gradient, states[1].stack_pack, states[0].mix_pack, moment_late
        )
        stack_other, mix_other = swap_all([stack_pack, mix_pack], swap_head, 1)
        up_one = merge_first(up_one, up_others)
        stack_other, mix_other, up_one = hold(stack_other, mix_other, up_one)
        up_others = send_second(up_one)
        down_blocks = merge_second(down_one, down_others)
        attend_one = attend_grad(quick, states[1], stack_other, back_other)

        attend_one, up_others, gradient = hold(attend_one, up_others, gradient)
        attend_others = send_first(attend_one)
        pair_one = swap_line(merge_second(up_one, up_others, down_blocks))
        run_back_mix(0, gradient, weights[0])

        attend_others, summary, back_pack = hold(attend_others, states[0].back_summary, states[0].back_pack)
        near, back_other = swap_all([summary, back_pack], swap_head, 1)
        attend_one = merge_first(attend_one, attend_others)
        near, back_other, attend_one = hold(near, back_other, attend_one)
        both = cross_edges(summary, near)
        attend_others = send_second(attend_one)
        down_zero = down_grad(quick, states[0], mix_other, stack_pack, stack_other, (3, 3))

        back_received, down_zero, attend_others = hold((near, *both), down_zero, attend_others)
        down_others = send_first(down_zero)
        gradient = run_back_project(0, back_received, weights[0][0])

        down_others, stack_pack, pair_one = hold(down_others, states[0].stack_pack, pair_one)
        stack_other = swap_head(stack_pack, 1)
        vector_grads = [(state.vector_one + state.vector_two)[:5] for state in states]
        kept, sent = core_vectors(vector_grads, [state.bias_grad for state in states])
        came = swap_head(sent, 1)
        up_zero = up_grad(quick, states[0], back_other, mix_other)
        down_zero = merge_first(down_zero, down_others)
        up_zero, down_zero, stack_other, one, one_others, came = hold(
            up_zero, down_zero, stack_other, attend_one, attend_others, came
        )
        down_others = send_second(down_zero)
        up_others = send_first(up_zero)
        attend_blocks = merge_second(one, one_others)
        kept, sent = across_vectors(kept + came, layers)
        came = swap_head(sent, 2)
        attend_zero = attend_grad(quick, states[0], stack_other, back_other)

        attend_zero, down_others, came = hold(attend_zero, down_others, came)
        attend_others = send_first(attend_zero)
        pair_two = swap_line(merge_second(down_zero, down_others, attend_blocks))
        back_one = orthogonalize(0, pair_one, moment, kept + came)

        up_others, back_one = hold(up_others, back_one)
        up_zero = merge_first(up_zero, up_others)
        up_kept = up_zero[0], up_zero[2]
        up_others = send_second(up_zero)

        attend_others, pair_two, back_one, up_kept = hold(attend_others, pair_two, back_one, up_kept)
        attend_zero = merge_first(attend_zero, attend_others)
        attend_kept = attend_zero[0], attend_zero[2]
        attend_others = send_second(attend_zero)
        pieces_one = swap_owners(back_one)
        back_two = orthogonalize(1, pair_two, moment)

        attend_others, up_others, back_two = hold(attend_others, up_others, back_two)
        up_blocks = merge_second((up_kept[0], None, up_kept[1]), up_others)
        pair_three = merge_second((attend_kept[0], None, attend_kept[1]), attend_others, up_blocks)
        pair_three, pieces_one = hold(pair_three, pieces_one)
        pair_three = swap_line(pair_three)

        pair_three, back_two = hold(pair_three, back_two)
        pieces_two = swap_owners(back_two)
        back_three = orthogonalize(0, pair_three, moment_late)

        pieces_two, back_three = hold(pieces_two, back_three)
        pieces_three = swap_owners(back_three)
        packed = jnp.sum(pieces_one[:, moments[1].shape[1] :].astype(F32), axis=0)
        packed = packed[: 2 * kept.shape[0]]
        packed = jnp.concatenate([packed[: kept.shape[0]], packed[kept.shape[0] :]], axis=1)
        plan = [
            (pieces_one, [("up", 1, 4), ("down", 1, 0)]),
            (pieces_two, [("down", 0, 4), ("query_key", 1, 0), ("value", 1, 2), ("out", 1, 3)]),
            (pieces_three, [("up", 0, 0), ("query_key", 0, 4), ("value", 0, 6), ("out", 0, 7)]),
        ]
    else:
        spread_biases(bias_up)
        weights = []
        for layer in range(layers):
            parts = []
            for part in (attend_of(layer), w_up[layer].astype(BF16), w_down[layer].T.astype(BF16)):
                whole = lax.all_gather(part, "dp", axis=0, tiled=True).reshape(4, 2, width // 8, -1)
                parts.append([([whole] + other_slots(whole), "whole", 0, 0, width)])
            weights.append(tuple(parts))
        for layer in range(layers):
            run_project(layer, resid, weights[layer][0])
            resid = run_mix(layer, exchange_edges(states[layer].summary), weights[layer])
        activations = resid
        raw = []
        for layer in reversed(range(layers)):
            state = states[layer]
            branch = gradient.astype(BF16)
            run_back_mix(layer, gradient, weights[layer])
            gradient = run_back_project(layer, exchange_edges(state.back_summary), weights[layer][0])
            back_other, mix_other, stack_other, branch_other = swap_all(
                [state.back_pack, state.mix_pack, state.stack_pack, branch], swap_head, 1
            )
            for own in (
                attend_grad(quick, state, stack_other, back_other),
                up_grad(quick, state, back_other, mix_other),
                down_grad(quick, state, mix_other, branch, branch_other, (None, None)),
            ):
                for keep, send in ((own[0], own[1]), (own[2], own[3])):
                    raw.append(keep.astype(F32) + swap_head(send, 2).astype(F32))
        count = layers * 12
        padded = -(-count // dp_size) * dp_size
        grads = jnp.concatenate(raw)
        grads = jnp.concatenate([grads, jnp.zeros((padded - count,) + grads.shape[1:], F32)])
        grads = lax.psum_scatter(grads, "dp", scatter_dimension=0, tiled=True)
        old = [part for layer in reversed(range(layers)) for part in old_blocks(layer, moments, block)]
        old = jnp.concatenate(old)
        old = jnp.concatenate([old, jnp.zeros((padded - count,) + old.shape[1:], old.dtype)])
        old = lax.all_to_all(old, "dp", split_axis=0, concat_axis=1, tiled=True)
        owned = padded // dp_size
        back = jnp.concatenate(
            [orthogonalize(0, grads[place : place + 1], old[place : place + 1]) for place in range(owned)]
        )
        back = jnp.stack([back[..., :block], back[..., block:]], axis=1)
        back = lax.all_to_all(back, "dp", split_axis=2, concat_axis=0, tiled=True)
        back = jnp.concatenate([back[:, 0], back[:, 1]], axis=2)
        ordered = [back[12 * place : 12 * (place + 1)] for place in reversed(range(layers))]
        plan = [
            (part, [("query_key", layer, 0), ("value", layer, 2), ("out", layer, 3), ("up", layer, 4), ("down", layer, 8)])
            for layer, part in enumerate(ordered)
        ]
        vector_grads = [(state.vector_one + state.vector_two)[:5] for state in states]
        kept, sent = core_vectors(vector_grads, [state.bias_grad for state in states])
        kept, sent = across_vectors(kept + swap_head(sent, 1), layers)
        packed = lax.psum(kept + swap_head(sent, 2), "dp")

    vector_total, bias_total = packed[: 5 * layers].reshape(vectors.shape), packed[5 * layers :]
    olds = {
        "query_key": (w_query_key, moment_query_key),
        "value": (w_value, moment_value),
        "out": (w_out, moment_out),
        "up": (w_up, moment_up),
        "down": tuple(jnp.transpose(item, (0, 2, 1)) for item in (w_down, moment_down)),
    }
    news = {}
    for pieces, items in plan:
        news.update(update(width // block, pieces, items, olds, news))
    news["down"] = [jnp.transpose(item, (0, 2, 1)) for item in news["down"]]
    next_masters, next_moments, copies = zip(*(news[name] for name in ("query_key", "value", "out", "up", "down")))
    vectors_next, vector_first_next, vector_second_next = adam_update(
        vectors, vector_total, vector_first, vector_second
    )
    bias_next, bias_first_next, bias_second_next = adam_update(bias_up, bias_total, bias_first, bias_second)
    return (
        (activations.astype(BF16), gradient)
        + next_masters
        + next_moments
        + copies
        + (vectors_next, vector_first_next, vector_second_next, bias_next, bias_first_next, bias_second_next)
    )


def solution(mesh):
    shards = (
        P(None, "dp", None, "head"),
        P(None, "dp", "head"),
        P(None, "head", "dp"),
        P(None, "dp", "head"),
        P(None, "head", "dp"),
    )
    rows = P(("dp", "head"), None)
    placed = (
        (rows, rows, P("dp", "head"), P("dp", None), P(), P(), P(None, "head"))
        + shards
        + shards
        + (P(), P(), P(None, "head"), P(None, "head"))
    )
    return jax.shard_map(
        per_device,
        mesh=mesh,
        in_specs=placed,
        out_specs=(rows, rows) + shards + shards + shards + (P(), P(), P()) + (P(None, "head"),) * 3,
        check_vma=False,
    )
```

```python
from functools import partial
from types import SimpleNamespace

import jax
import jax.numpy as jnp
from jax import lax
from jax.experimental import pallas as pl
from jax.experimental.pallas import tpu as pltpu
from jax.sharding import PartitionSpec as P

HEAD_DIM = 64
FEATS = 32
NS_STEPS = 5
STEP = 10


ORTHO_LINEAR = 3.4445
ORTHO_CUBIC = -4.775
ORTHO_QUINTIC = 2.0315
ORTHO_EPSILON = 1e-07
MOMENTUM_DECAY = 0.95
MUON_RATE = 0.2
WEIGHT_DECAY = 0.1
BETA_FIRST = 0.9
BETA_SECOND = 0.99
ADAM_RATE = 0.2
ADAM_EPSILON = 1e-08
NORM_EPSILON = 1e-05
ATTEND_EPSILON = 1e-06
ROPE_BASE = 10000.0
EXACT = lax.Precision.HIGHEST

F32 = jnp.float32
BF16 = jnp.bfloat16
CHUNK = 4 * HEAD_DIM
FEAT_CHUNK = 4 * FEATS
TOTAL_ROWS = 16
VMEM_BYTES = 56 * 1024 * 1024


def dot_nn(left, right):
    return lax.dot_general(left, right, (((1,), (0,)), ((), ())), preferred_element_type=F32)


def dot_nt(left, right):
    return lax.dot_general(left, right, (((1,), (1,)), ((), ())), preferred_element_type=F32)


def dot_tn(left, right):
    return lax.dot_general(left, right, (((0,), (0,)), ((), ())), preferred_element_type=F32)


def iota(shape, axis):
    return lax.broadcasted_iota(jnp.int32, shape, axis)


def swap_head(values, offset):
    return lax.ppermute(values, "head", [(h, h ^ offset) for h in range(lax.axis_size("head"))])


def swap_dp(values, offset):
    return lax.ppermute(values, "dp", [(d, d ^ offset) for d in range(lax.axis_size("dp"))])


def swap_all(items, swap, offset):
    return [swap(item, offset) for item in items]


def swap_line(parts):
    groups = [[z * 2 + y for z in range(4)] for y in range(2)]
    return lax.all_to_all(parts, "dp", split_axis=0, concat_axis=0, axis_index_groups=groups, tiled=True)


def four_times(part):
    return jnp.broadcast_to(part[None], (4,) + part.shape)


def swap_owners(parts):
    return lax.all_to_all(parts, "dp", split_axis=0, concat_axis=0, tiled=True)


def hold(*values):
    return lax.optimization_barrier(values)


def sources(kind, slot):
    core, across = slot & 1, slot >> 1
    if kind == "whole":
        return [(slot, None, None)]
    if "up" in kind:
        return [(slot, 0, 0), (slot, 1, 1)]
    return [(core, across, 0), (2 + core, across, 1)]


def fetch(refs, plan, scratch, sems, base, lanes):
    index = lax.axis_index("dp")
    waits = [[], [], [], []]
    count = base
    for position, (kind, source_lane, lane, width) in enumerate(plan):
        first, last = max(lane, lanes[0]), min(lane + width, lanes[1])
        if first >= last:
            continue
        taken = pl.ds(source_lane + first - lane, last - first)
        given = pl.ds(first - lanes[0], last - first)
        for slot in range(4):
            for array, entry, y_offset in sources(kind, slot):
                ref = refs[4 * position + array]
                if kind == "whole":
                    pairs = [(ref.at[:, :, :, taken], scratch.at[slot, :, :, :, given])]
                elif "near" in kind:
                    pairs = [
                        (
                            ref.at[entry, offset, :, taken],
                            scratch.at[slot, (index >> 1) ^ offset, (index & 1) ^ y_offset, :, given],
                        )
                        for offset in range(4)
                    ]
                else:
                    pairs = [(ref.at[entry, :, :, taken], scratch.at[slot, :, (index & 1) ^ y_offset, :, given])]
                for source, target in pairs:
                    copy = pltpu.make_async_copy(source, target, sems.at[count])
                    copy.start()
                    waits[slot].append(copy)
                    count += 1
    return waits


def matrix(scratch, slot, first, last):
    value = scratch[slot]
    return value.reshape(-1, value.shape[-1])[:, first:last]


def ref_count(plan):
    return 4 * len(plan)


def copy_count(plan):
    return sum(4 if run[0] == "whole" else 32 if "near" in run[0] else 8 for run in plan)


def take(refs, *plans):
    taken = []
    for plan in plans:
        taken.append(refs[: ref_count(plan)])
        refs = refs[ref_count(plan) :]
    return (*taken, refs)


def arrive(copies):
    for copy in copies:
        copy.wait()


def norm_parts(values):
    row_mean = jnp.mean(values, axis=-1, keepdims=True)
    centred = values - row_mean
    variance = jnp.mean(centred * centred, axis=-1, keepdims=True)
    scale = lax.rsqrt(variance + NORM_EPSILON)
    return centred * scale, scale


def norm_backward(values, gain, incoming):
    unit, scale = norm_parts(values)
    gain_grad = jnp.sum(incoming * unit, axis=0, keepdims=True)
    shift_grad = jnp.sum(incoming, axis=0, keepdims=True)
    inner = incoming * gain
    inner_mean = jnp.mean(inner, axis=-1, keepdims=True)
    along = jnp.mean(inner * unit, axis=-1, keepdims=True)
    return scale * (inner - inner_mean - unit * along), gain_grad, shift_grad


def swap_halves(values):
    width = values.shape[1]
    half = HEAD_DIM // 2
    lower = iota(values.shape, 1) % HEAD_DIM < half
    return jnp.where(lower, pltpu.roll(values, width - half, 1), pltpu.roll(values, half, 1))


def split_low(values):
    high = values.astype(BF16)
    return high, (values - high.astype(F32)).astype(BF16)


def lane_mask(index, per_head, width):
    return (iota((1, width), 1) // per_head == index).astype(BF16)


def turn_tables(cosine, sine):
    part, other = cosine[...], sine[...]
    return (
        jnp.concatenate([part] * (2 * CHUNK // HEAD_DIM), axis=1),
        jnp.concatenate([-other, other] * (CHUNK // HEAD_DIM), axis=1),
    )


def wide_map(feature_map):
    tall = jnp.concatenate([feature_map[...]] * 4, axis=0)
    return jnp.where(feature_ones(), jnp.concatenate([tall] * 4, axis=1), 0.0)


def feature_ones():
    return iota((CHUNK, FEAT_CHUNK), 0) // HEAD_DIM == iota((CHUNK, FEAT_CHUNK), 1) // FEATS


def features(values, map_high, map_low):
    high, low_part = split_low(values)
    square_high, square_low = split_low(0.5 * values * values)
    ones = -feature_ones().astype(BF16)
    left = jnp.concatenate([high, low_part, high, square_high, square_low], axis=1)
    right = jnp.concatenate([map_high, map_high, map_low, ones, ones], axis=0)
    return jnp.exp(dot_nn(left, right)) * FEATS ** (-0.5)


def fold_matrix():
    rows, columns = iota((CHUNK, HEAD_DIM), 0), iota((CHUNK, HEAD_DIM), 1)
    return (rows % HEAD_DIM == columns).astype(BF16)


def spread_matrix():
    rows = iota((2 * HEAD_DIM, 2 * CHUNK), 0)
    columns = iota((2 * HEAD_DIM, 2 * CHUNK), 1)
    return (columns // CHUNK * HEAD_DIM + columns % HEAD_DIM == rows).astype(BF16)


def same_head(feature_rows):
    shape = (feature_rows, 2 * CHUNK)
    return iota(shape, 0) % FEAT_CHUNK // FEATS == iota(shape, 1) % CHUNK // HEAD_DIM


def column_of(segment_row):
    return jnp.broadcast_to(segment_row[...], (8, segment_row.shape[1])).T[:, 0:1]


def edge_masks(segment_column):
    first = segment_column[0:1, :]
    last = segment_column[segment_column.shape[0] - 1 :, :]
    in_first = (segment_column == first).astype(F32)
    in_last = (segment_column == last).astype(F32) * (1.0 - in_first)
    return in_first, in_last


def edge_summary(edges, weighted):
    full = dot_tn(edges, weighted)
    full = jnp.where(same_head(2 * FEAT_CHUNK)[:, :CHUNK], full, 0.0).astype(BF16)
    folded = dot_nn(full, fold_matrix())
    return jnp.concatenate([folded[:FEAT_CHUNK], folded[FEAT_CHUNK:]], axis=1).astype(BF16)


def store_totals(summary_out, rows):
    pieces = [piece for row in rows for piece in (row[:, :FEAT_CHUNK], row[:, FEAT_CHUNK:])]
    pieces.append(jnp.zeros((TOTAL_ROWS - len(pieces), FEAT_CHUNK), F32))
    summary_out[summary_out.shape[0] - TOTAL_ROWS :, :] = jnp.concatenate(pieces, axis=0).astype(BF16)


def edges_of(phi, in_first, in_last):
    wide = phi.astype(F32)
    return jnp.concatenate([wide * in_first, wide * in_last], axis=1).astype(BF16)


def open_edges(ref, which):
    feats = ref.shape[0] - TOTAL_ROWS
    totals = ref[feats:, :]
    columns = []
    for chunk in range(feats // FEAT_CHUNK):
        pick = (iota((TOTAL_ROWS, HEAD_DIM), 0) == 2 * chunk + which).astype(BF16)
        columns.append(dot_tn(totals, pick))
    sums = ref[:feats, lanes_of(which, HEAD_DIM)].astype(F32)
    return jnp.concatenate([sums, jnp.concatenate(columns, axis=0)], axis=1)


def combine_edges(received, coefficients):
    totals = [None, None]
    rows = (received[0].shape[0] - TOTAL_ROWS) // 4
    for position, ref in enumerate(received):
        offset = position + 1
        pair = []
        for which in range(2):
            value = open_edges(ref, which)
            pair.append(
                jnp.concatenate(
                    [value[(slot ^ offset) * rows : ((slot ^ offset) + 1) * rows] for slot in range(4)], axis=0
                )
            )
        for which in range(2):
            part = coefficients[position, 2 * which] * pair[0] + coefficients[position, 2 * which + 1] * pair[1]
            totals[which] = part if totals[which] is None else totals[which] + part
    return totals


def spread_edges(totals, chunk):
    rows = slice(chunk * FEAT_CHUNK, (chunk + 1) * FEAT_CHUNK)
    joined = jnp.concatenate([totals[0][rows], totals[1][rows]], axis=0).astype(BF16)
    return jnp.where(same_head(2 * FEAT_CHUNK), dot_nn(joined, spread_matrix()), 0.0).astype(BF16)


def lanes_of(slot, width):
    return slice(slot * width, (slot + 1) * width)


def project_kernel(plan, resid, vectors, cosine_part, sine_part, feature_map, segment_row, *rest):
    weight_refs, rest = take(rest, plan)
    phi_query_out, phi_key_out, value_out, centre_out, query_out, key_out, summary_out, weight, sems = rest
    waits = fetch(weight_refs, plan, weight, sems, 0, (0, weight.shape[4]))
    cosine, sine = turn_tables(cosine_part, sine_part)
    unit, _ = norm_parts(resid[...])
    normed = (unit * vectors[0:1, :] + vectors[1:2, :]).astype(BF16)
    width = resid.shape[1] // 4
    rows = resid.shape[0]
    shift = jnp.broadcast_to(vectors[1:2, :], (16, resid.shape[1])).astype(BF16)
    normed = jnp.concatenate([normed, shift], axis=0)
    pieces = [[], [], []]
    for slot in range(4):
        arrive(waits[slot])
        product = dot_nn(normed, matrix(weight, slot, 0, 3 * width))
        for which in range(3):
            pieces[which].append(product[:, lanes_of(which, width)])
    queries, key_rows, value_rows = (jnp.concatenate(piece, axis=1) for piece in pieces)
    queries, key_rows = queries[:rows], key_rows[:rows]
    centre = value_rows[rows : rows + 8]
    centre_out[...] = centre
    value_rows = (value_rows[:rows] - centre[0:1]).astype(BF16)
    value_out[...] = value_rows
    map_high, map_low = split_low(wide_map(feature_map))
    in_first, in_last = edge_masks(column_of(segment_row))
    totals = []
    for chunk in range(resid.shape[1] // CHUNK):
        lanes = lanes_of(chunk, CHUNK)
        feats = lanes_of(chunk, FEAT_CHUNK)
        turned = []
        for source, scaled_out, phi_out in (
            (queries, query_out, phi_query_out),
            (key_rows, key_out, phi_key_out),
        ):
            part = source[:, lanes]
            scaled = part * cosine + swap_halves(part) * sine
            scaled_out[:, lanes] = scaled
            phi = features(scaled, map_high, map_low).astype(BF16)
            phi_out[:, feats] = phi
            turned.append(phi)
        edges = edges_of(turned[1], in_first, in_last)
        summary_out[feats, :] = edge_summary(edges, value_rows[:, lanes])
        totals.append(jnp.sum(edges.astype(F32), axis=0, keepdims=True))
    store_totals(summary_out, totals)


def mix_kernel(
    plans, resid, vectors, bias, phi_query, phi_key, value, centre, segment_row, recv_one, recv_two,
    recv_three, coefficients, *rest
):
    out_refs, up_refs, down_refs, rest = take(rest, *plans)
    (context_out, inverse_out, middle_out, slope_out, active_keep, pack_out, resid_out, out_weight, up_weight,
     down_weight, sems) = rest
    bases = [0, copy_count(plans[0]), copy_count(plans[0]) + copy_count(plans[1])]
    out_waits = fetch(out_refs, plans[0], out_weight, sems, bases[0], (512, 768))
    up_waits = fetch(up_refs, plans[1], up_weight, sems, bases[1], (0, 768))
    down_waits = fetch(down_refs, plans[2], down_weight, sems, bases[2], (0, 768))
    segment_column = column_of(segment_row)
    same = (segment_column == segment_row[...]).astype(F32)
    in_first, in_last = edge_masks(segment_column)
    totals = combine_edges((recv_one, recv_two, recv_three), coefficients)
    rows = resid.shape[0]
    contexts = []
    for chunk in range(resid.shape[1] // CHUNK):
        lanes = lanes_of(chunk, CHUNK)
        feats = lanes_of(chunk, FEAT_CHUNK)
        query = phi_query[:, feats]
        key = phi_key[:, feats]
        values = value[:, lanes]
        left = []
        right = []
        for head in range(4):
            scores = dot_nt(query * lane_mask(head, FEATS, FEAT_CHUNK), key)
            left.append((scores * same).astype(BF16))
            mask = lane_mask(head, HEAD_DIM, CHUNK)
            right.append(jnp.concatenate([values * mask, jnp.broadcast_to(mask, (rows, CHUNK))], axis=1))
        left.append(edges_of(query, in_first, in_last))
        right.append(spread_edges(totals, chunk))
        both = dot_nn(jnp.concatenate(left, axis=1), jnp.concatenate(right, axis=0))
        inverse = 1.0 / (both[:, CHUNK:] + ATTEND_EPSILON)
        context = (both[:, :CHUNK] + centre[0:1, lanes] * both[:, CHUNK:]) * inverse
        inverse_out[:, lanes] = inverse
        context_out[:, lanes] = context
        contexts.append(context.astype(BF16))
    context = jnp.concatenate(contexts, axis=1)
    width = resid.shape[1] // 4
    middle = resid[...]
    for slot in range(4):
        arrive(out_waits[slot])
        middle = middle + dot_nt(context[:, lanes_of(slot, width)], matrix(out_weight, slot, 64, 256))
    middle_out[...] = middle
    unit, _ = norm_parts(middle)
    normed = (unit * vectors[2:3, :] + vectors[3:4, :]).astype(BF16)
    pack_out[2] = normed
    output = middle + vectors[4:5, :]
    for slot in range(4):
        arrive(up_waits[slot])
        upper = dot_nn(normed, matrix(up_weight, slot, 0, 768)) + bias[slot : slot + 1, :]
        below = 0.5 * (1.0 + lax.erf(upper * 2.0**-0.5))
        slope = below + upper * (jnp.exp(-0.5 * upper * upper) * 0.3989422804014327)
        active = (upper * below).astype(BF16)
        slope_out[slot] = slope.astype(BF16)
        if slot % 2 == 0:
            active_keep[slot // 2] = active
        else:
            pack_out[slot // 2] = active
        arrive(down_waits[slot])
        output = output + dot_nt(active, matrix(down_weight, slot, 0, 768))
    resid_out[...] = output


def back_mix_kernel(
    plans, grad, vectors, middle, slope, inverse, context, centre, phi_query, segment_row, *rest
):
    out_refs, up_refs, down_refs, rest = take(rest, *plans)
    (upper_keep, pack_out, middle_grad_out, numer_out, denom_out, summary_out, vector_out,
     bias_out, out_weight, up_weight, down_weight, sems) = rest
    bases = [0, copy_count(plans[0]), copy_count(plans[0]) + copy_count(plans[1])]
    down_waits = fetch(down_refs, plans[2], down_weight, sems, bases[2], (0, 768))
    up_waits = fetch(up_refs, plans[1], up_weight, sems, bases[1], (0, 768))
    out_waits = fetch(out_refs, plans[0], out_weight, sems, bases[0], (512, 768))
    grad_out = grad[...]
    branch = grad_out.astype(BF16)
    shift_out = jnp.sum(branch.astype(F32), axis=0, keepdims=True)
    normed_grad = None
    for slot in range(4):
        arrive(down_waits[slot])
        hidden = dot_nn(branch, matrix(down_weight, slot, 0, 768))
        upper = (hidden * slope[slot].astype(F32)).astype(BF16)
        if slot % 2 == 0:
            upper_keep[slot // 2] = upper
        else:
            pack_out[slot // 2] = upper
        bias_out[slot : slot + 1, :] = jnp.sum(upper.astype(F32), axis=0, keepdims=True)
        arrive(up_waits[slot])
        part = dot_nt(upper, matrix(up_weight, slot, 0, 768))
        normed_grad = part if normed_grad is None else normed_grad + part
    inward, gain_grad, shift_grad = norm_backward(middle[...], vectors[2:3, :], normed_grad)
    middle_grad = grad_out + inward
    middle_grad_out[...] = middle_grad
    attn = middle_grad.astype(BF16)
    pack_out[2] = attn
    zero_row = jnp.zeros_like(shift_out)
    vector_out[...] = jnp.concatenate([zero_row, zero_row, gain_grad, shift_grad, shift_out] + [zero_row] * 3, axis=0)
    pieces = []
    for slot in range(4):
        arrive(out_waits[slot])
        pieces.append(dot_nn(attn, matrix(out_weight, slot, 64, 256)))
    context_grad = jnp.concatenate(pieces, axis=1)
    in_first, in_last = edge_masks(column_of(segment_row))
    head_ones = (iota((CHUNK, CHUNK), 0) // HEAD_DIM == iota((CHUNK, CHUNK), 1) // HEAD_DIM).astype(BF16)
    one_lane = (iota((CHUNK, FEAT_CHUNK), 0) == iota((CHUNK, FEAT_CHUNK), 1) // FEATS * HEAD_DIM).astype(BF16)
    totals = []
    for chunk in range(grad.shape[1] // CHUNK):
        lanes = lanes_of(chunk, CHUNK)
        feats = lanes_of(chunk, FEAT_CHUNK)
        numer = context_grad[:, lanes] * inverse[:, lanes]
        denom = -dot_nn((numer * (context[:, lanes] - centre[0:1, lanes])).astype(BF16), head_ones)
        numer = numer.astype(BF16)
        denom = denom.astype(BF16)
        numer_out[:, lanes] = numer
        denom_out[:, lanes] = denom
        edges = edges_of(phi_query[:, feats], in_first, in_last)
        summary_out[feats, :] = edge_summary(edges, numer)
        heads = dot_nn(denom, one_lane)
        weighted = edges.astype(F32) * jnp.concatenate([heads, heads], axis=1)
        totals.append(jnp.sum(weighted, axis=0, keepdims=True))
    store_totals(summary_out, totals)


def back_project_kernel(
    plan, resid, vectors, cosine_part, sine_part, feature_map, segment_row, phi_query, phi_key, value,
    query_scaled, key_scaled, numer, denom, context, middle_grad, recv_one, recv_two, recv_three, back_one,
    back_two, back_three, coefficients, *rest
):
    weight_refs, rest = take(rest, plan)
    stacked_keep, pack_out, grad_out, vector_out, weight, sems = rest
    waits = fetch(weight_refs, plan, weight, sems, 0, (0, weight.shape[4]))
    cosine, sine = turn_tables(cosine_part, sine_part)
    unit, _ = norm_parts(resid[...])
    pack_out[2] = (unit * vectors[0:1, :] + vectors[1:2, :]).astype(BF16)
    segment_column = column_of(segment_row)
    same = (segment_column == segment_row[...]).astype(F32)
    in_first, in_last = edge_masks(segment_column)
    totals = combine_edges((recv_one, recv_two, recv_three), coefficients)
    back_totals = combine_edges((back_one, back_two, back_three), coefficients)
    rows = resid.shape[0]
    map_high, map_low = split_low(wide_map(feature_map))
    spread_high = jnp.concatenate([map_high, feature_ones().astype(BF16)], axis=0)
    spread_low = jnp.concatenate([map_low, jnp.zeros_like(map_low)], axis=0)
    spread_map = jnp.concatenate([spread_high, spread_high, spread_low], axis=1)
    share = jnp.full((rows, CHUNK), 1.0 / HEAD_DIM, BF16)
    grads = [[], [], []]
    for chunk in range(resid.shape[1] // CHUNK):
        lanes = lanes_of(chunk, CHUNK)
        feats = lanes_of(chunk, FEAT_CHUNK)
        query = phi_query[:, feats]
        key = phi_key[:, feats]
        values = value[:, lanes]
        both = jnp.concatenate([numer[:, lanes], denom[:, lanes]], axis=1)
        valued = jnp.concatenate([values, share], axis=1)
        query_left, query_right, key_left, key_right, value_left, value_right = [], [], [], [], [], []
        for head in range(4):
            feat_mask = lane_mask(head, FEATS, FEAT_CHUNK)
            mask = lane_mask(head, HEAD_DIM, CHUNK)
            both_mask = jnp.concatenate([mask, mask], axis=1)
            masked_query = query * feat_mask
            masked_both = both * both_mask
            query_left.append((dot_nt(masked_both, valued) * same).astype(BF16))
            query_right.append(key * feat_mask)
            key_left.append((dot_nt(valued, masked_both) * same).astype(BF16))
            key_right.append(masked_query)
            value_left.append((dot_nt(key, masked_query) * same).astype(BF16))
            value_right.append(masked_both[:, :CHUNK])
        forward_edges = spread_edges(totals, chunk)
        backward_edges = spread_edges(back_totals, chunk)
        query_edges = dot_nt(jnp.concatenate([numer[:, lanes], denom[:, lanes] * share], axis=1), forward_edges)
        key_edges = dot_nt(valued, backward_edges)
        query_edges = query_edges[:, :FEAT_CHUNK] * in_first + query_edges[:, FEAT_CHUNK:] * in_last
        key_edges = key_edges[:, :FEAT_CHUNK] * in_first + key_edges[:, FEAT_CHUNK:] * in_last
        value_left.append(edges_of(key, in_first, in_last))
        value_right.append(backward_edges[:, :CHUNK])
        phi_grads = (
            dot_nn(jnp.concatenate(query_left, axis=1), jnp.concatenate(query_right, axis=0)) + query_edges,
            dot_nn(jnp.concatenate(key_left, axis=1), jnp.concatenate(key_right, axis=0)) + key_edges,
        )
        grads[2].append(dot_nn(jnp.concatenate(value_left, axis=1), jnp.concatenate(value_right, axis=0)))
        for which, phi, scaled in ((0, query, query_scaled), (1, key, key_scaled)):
            high, low_part = split_low(phi_grads[which] * phi.astype(F32))
            wide = dot_nt(jnp.concatenate([high, low_part, high], axis=1), spread_map)
            turned = wide[:, :CHUNK] - scaled[:, lanes] * wide[:, CHUNK:]
            grads[which].append(turned * cosine + swap_halves(turned * sine))
    joined = [jnp.concatenate(item, axis=1).astype(BF16) for item in grads]
    joined.append(context[...].astype(BF16))
    width = resid.shape[1] // 4
    normed_grad = None
    for slot in range(4):
        stacked = jnp.concatenate([item[:, lanes_of(slot, width)] for item in joined], axis=1)
        if slot % 2 == 0:
            stacked_keep[slot // 2] = stacked
        else:
            pack_out[slot // 2] = stacked
        arrive(waits[slot])
        part = dot_nt(stacked[:, : 3 * width], matrix(weight, slot, 0, 3 * width))
        normed_grad = part if normed_grad is None else normed_grad + part
    inward, gain_grad, shift_grad = norm_backward(resid[...], vectors[0:1, :], normed_grad)
    below = middle_grad[...] + inward
    grad_out[...] = below
    pack_out[3] = below.astype(BF16)
    zero_row = jnp.zeros_like(gain_grad)
    vector_out[...] = jnp.concatenate([gain_grad, shift_grad] + [zero_row] * 6, axis=0)


def grad_kernel(quick, splits, right_own, right_other, *rest):
    lefts, (up_keep, up_send, down_keep, down_send, whole) = rest[: 2 * len(splits)], rest[2 * len(splits) :]
    y_bit = lax.axis_index("dp") & 1
    size = up_keep.shape[1]
    joined = []
    for position, (_, own_entry, other_entry) in enumerate(splits):
        own, other = lefts[2 * position], lefts[2 * position + 1]
        own = own[...] if own_entry is None else own[own_entry]
        other = other[...] if other_entry is None else other[other_entry]
        joined.append(jnp.concatenate([own, other], axis=0))
    for position, up_out, down_out in ((1, up_send, down_send), (0, up_keep, down_keep)):
        right = jnp.concatenate([right_own[position], right_other[position]], axis=0)
        start = 0
        for (columns, _, _), left in zip(splits, joined):
            whole[start : start + columns] = dot_tn(right[:, start : start + columns], left).astype(BF16)
            start += columns
        for part in range(2):
            up_out[part] = whole[part * size : (part + 1) * size]
        if not quick:
            for part in range(2):
                down_out[part] = whole[(2 + part) * size : (3 + part) * size]
            continue
        for bit, out in ((y_bit, down_keep), (1 - y_bit, down_send)):
            out[position] = whole[pl.ds(pl.multiple_of((2 + bit) * size, size), size), :]


def sum_of(left, right):
    return (left.astype(F32) + right.astype(F32)).astype(BF16)


def merge_first_kernel(up, up_other, down, down_other, up_keep, up_send, down_keep, down_send):
    y_bit = lax.axis_index("dp") & 1
    up_keep[...] = sum_of(up[y_bit], up_other[y_bit])
    up_send[...] = sum_of(up[1 - y_bit], up_other[1 - y_bit])
    down_keep[...] = sum_of(down[0], down_other[0])
    down_send[...] = sum_of(down[1], down_other[1])


def merge_second_kernel(up, up_other, down, down_other, *rest):
    other, out = rest[:-1], rest[-1]
    for blocks in other:
        out[:2] = blocks[...]
    base = 2 * len(other)
    out[base] = sum_of(up[...], up_other[...])
    out[base + 1] = sum_of(down[...], down_other[...])


def update_kernel(ratio, items, aliased, pieces, *refs):
    width = pieces.shape[2] // 2
    scale = MUON_RATE * ratio**0.5
    olds, news = refs[: 2 * len(items)], refs[2 * len(items) + aliased :]
    for position, (name, base) in enumerate(items):
        old, moment = olds[2 * position : 2 * position + 2]
        new, new_moment, copy = news[3 * position : 3 * position + 3]
        rows = old.shape[2] if name == "out" else old.shape[1]
        for block in range({"query_key": 2, "value": 1, "out": 1}.get(name, 4)):
            both = pieces[base + block, 0:rows].astype(F32)
            if name == "out":
                both = both.T
                grad, ortho = both[:width], both[width:]
            else:
                grad, ortho = both[:, :width], both[:, width:]
            if name == "query_key":
                place = (0, slice(None), block)
            elif name in ("value", "out"):
                place = (0,)
            else:
                place = (0, slice(None), lanes_of(block, width))
            new_moment[place] = MOMENTUM_DECAY * moment[place] + grad
            master = old[place] * (1.0 - MUON_RATE * WEIGHT_DECAY) - scale * ortho
            new[place] = master
            copy[place] = master.astype(BF16)


def ortho_kernel(place, count, moment, *rest):
    terms, extra, (result, whole) = rest[:count], rest[count:-2], rest[-2:]
    pieces, size, _ = moment.shape
    width = whole.shape[1]
    eye = (iota((width, width), 0) == iota((width, width), 1)).astype(F32)

    def exact(left, right, dims=(((1,), (0,)), ((), ()))):
        return lax.dot_general(left, right, dims, precision=EXACT, preferred_element_type=F32)

    pieces_of = [part[term].astype(F32) for part in terms for term in range(part.shape[0])]
    grad = pieces_of[0]
    for term in pieces_of[1:]:
        grad = grad + term
    for piece in range(pieces):
        whole[piece * size : (piece + 1) * size, :] = moment[piece, :, lanes_of(place, width)].astype(F32)
    source = MOMENTUM_DECAY * whole[...].T + grad
    gram = exact(source, source, (((1,), (1,)), ((), ())))
    norm = jnp.sqrt(jnp.sum(gram * eye)) + ORTHO_EPSILON
    gram = gram / (norm * norm)
    chain = None
    for iteration in range(NS_STEPS):
        step = ORTHO_LINEAR * eye + ORTHO_CUBIC * gram + ORTHO_QUINTIC * exact(gram, gram)
        chain = step if iteration == 0 else exact(chain, step)
        if iteration + 1 < NS_STEPS:
            gram = exact(exact(step, gram), step)
    ortho = dot_tn(source.astype(BF16), (chain / norm).astype(BF16))
    for which, value in ((0, grad.T), (1, ortho)):
        for piece in range(pieces):
            result[piece, 0:size, lanes_of(which, width)] = value[piece * size : (piece + 1) * size].astype(BF16)
    for rows in extra:
        half = rows.shape[1] // 2
        spare = result.shape[1] - size
        more = [rows[:, :half], rows[:, half:], jnp.zeros((spare - 2 * rows.shape[0], half), F32)]
        more = jnp.concatenate(more, axis=0).astype(BF16)
        for piece in range(pieces):
            result[piece, size:, :] = more


def vmem(count):
    return [pl.BlockSpec(memory_space=pltpu.VMEM)] * count


def anywhere(count):
    return [pl.BlockSpec(memory_space=pl.ANY)] * count


def scalars():
    return [pl.BlockSpec(memory_space=pltpu.SMEM)]


def shape(dims, dtype=F32):
    return jax.ShapeDtypeStruct(dims, dtype)


def call(kernel, name, in_specs, outs, scratch, flops, moved):
    return pl.pallas_call(
        kernel,
        name=name,
        out_shape=outs,
        in_specs=in_specs,
        out_specs=vmem(len(outs)),
        scratch_shapes=scratch,
        cost_estimate=pl.CostEstimate(flops=int(flops), bytes_accessed=int(moved), transcendentals=0),
        compiler_params=pltpu.CompilerParams(vmem_limit_bytes=VMEM_BYTES),
    )


def weight_scratch(width, lanes):
    return pltpu.VMEM((4, 4, 2, width // 8, lanes), BF16)


def flat(weight):
    return [item for run in weight for item in run[0]]


def plan_of(weight):
    return tuple(tuple(run[1:]) for run in weight)


def project(resid, vectors, tables, feature_map, weight):
    rows, width = resid.shape
    plan = plan_of(weight)
    feats = width // HEAD_DIM * FEATS
    outs = [
        shape((rows, feats), BF16),
        shape((rows, feats), BF16),
        shape((rows, width), BF16),
        shape((8, width)),
        shape((rows, width)),
        shape((rows, width)),
        shape((feats + TOTAL_ROWS, 2 * HEAD_DIM), BF16),
    ]
    results = call(
        partial(project_kernel, plan),
        "project",
        vmem(6) + anywhere(ref_count(plan)),
        outs,
        [weight_scratch(width, 640), pltpu.SemaphoreType.DMA((copy_count(plan),))],
        2 * rows * width * width * 3 * 1.5,
        8 * width * width,
    )(resid, vectors, tables.cosine, tables.sine, feature_map, tables.row, *flat(weight))
    state = SimpleNamespace(input=resid)
    state.phi_query, state.phi_key, state.value, state.centre, state.query, state.key, state.summary = results
    return state


def mix_scratch(width, plans):
    return [
        weight_scratch(width, 256),
        weight_scratch(width, width),
        weight_scratch(width, width),
        pltpu.SemaphoreType.DMA((sum(copy_count(plan) for plan in plans),)),
    ]


def mix(resid, vectors, bias, state, received, tables, weights):
    rows, width = resid.shape
    plans = [plan_of(weight) for weight in weights]
    refs = [item for weight in weights for item in flat(weight)]
    outs = [
        shape((rows, width)),
        shape((rows, width)),
        shape((rows, width)),
        shape((4, rows, width), BF16),
        shape((2, rows, width), BF16),
        shape((3, rows, width), BF16),
        shape((rows, width)),
    ]
    results = call(
        partial(mix_kernel, plans),
        "mix",
        vmem(11) + scalars() + anywhere(len(refs)),
        outs,
        mix_scratch(width, plans),
        2 * rows * width * width * 12,
        20 * width * width,
    )(
        resid, vectors, bias, state.phi_query, state.phi_key, state.value, state.centre, tables.row,
        *received, tables.shares, *refs,
    )
    (state.context, state.inverse, state.middle, state.slope, state.active_keep, state.mix_pack,
     state.output) = results


def back_mix(grad, vectors, state, tables, weights):
    rows, width = grad.shape
    plans = [plan_of(weight) for weight in weights]
    refs = [item for weight in weights for item in flat(weight)]
    feats = width // HEAD_DIM * FEATS
    outs = [
        shape((2, rows, width), BF16),
        shape((3, rows, width), BF16),
        shape((rows, width)),
        shape((rows, width), BF16),
        shape((rows, width), BF16),
        shape((feats + TOTAL_ROWS, 2 * HEAD_DIM), BF16),
        shape((8, width)),
        shape((4, width)),
    ]
    results = call(
        partial(back_mix_kernel, plans),
        "back_mix",
        vmem(9) + anywhere(len(refs)),
        outs,
        mix_scratch(width, plans),
        2 * rows * width * width * 11,
        20 * width * width,
    )(
        grad, vectors, state.middle, state.slope, state.inverse, state.context, state.centre, state.phi_query,
        tables.row, *refs,
    )
    (state.upper_keep, state.back_pack, state.middle_grad, state.numer, state.denom, state.back_summary,
     state.vector_two, state.bias_grad) = results


def back_project(resid, vectors, state, received, back_received, tables, feature_map, weight):
    rows, width = resid.shape
    plan = plan_of(weight)
    outs = [
        shape((2, rows, width), BF16),
        shape((4, rows, width), BF16),
        shape((rows, width)),
        shape((8, width)),
    ]
    results = call(
        partial(back_project_kernel, plan),
        "back_project",
        vmem(21) + scalars() + anywhere(ref_count(plan)),
        outs,
        [weight_scratch(width, 640), pltpu.SemaphoreType.DMA((copy_count(plan),))],
        2 * rows * width * width * 8,
        8 * width * width,
    )(
        resid, vectors, tables.cosine, tables.sine, feature_map, tables.row,
        state.phi_query, state.phi_key, state.value, state.query, state.key, state.numer,
        state.denom, state.context, state.middle_grad, *received, *back_received, tables.shares,
        *flat(weight),
    )
    state.stacked_keep, state.stack_pack, state.input_grad, state.vector_one = results


def matrix_grad(quick, splits, right_own, right_other, *lefts):
    width = right_own.shape[2]
    block = shape((2, width // 4, width), BF16)
    return call(
        partial(grad_kernel, quick, splits), "matrix_grad", vmem(2 + len(lefts)), [block] * 4,
        [pltpu.VMEM((width, width), BF16)], 2 * 512 * width * width * 2, 8 * width * width,
    )(right_own, right_other, *lefts)


def down_grad(quick, state, mix_other, branch_own, branch_other, entries):
    splits = ((state.mix_pack.shape[2], *entries),)
    return matrix_grad(quick, splits, state.active_keep, mix_other, branch_own, branch_other)


def up_grad(quick, state, back_other, mix_other):
    splits = ((state.mix_pack.shape[2], 2, 2),)
    return matrix_grad(quick, splits, state.upper_keep, back_other, state.mix_pack, mix_other)


def attend_grad(quick, state, stack_other, back_other):
    width = state.mix_pack.shape[2]
    splits = ((width // 4 * 3, 2, 2), (width // 4, 2, 2))
    return matrix_grad(
        quick, splits, state.stacked_keep, stack_other, state.stack_pack, stack_other, state.back_pack,
        back_other,
    )


def merge(kernel, outs, *operands):
    return call(kernel, "merge", vmem(len(operands)), outs, [], 1, 1)(*operands)


def merge_first(own, others):
    out = shape(own[0].shape[1:], BF16)
    return merge(merge_first_kernel, [out] * 4, own[0], others[0], own[2], others[1])


def merge_second(own, others, *other_blocks):
    out = shape((2 + 2 * len(other_blocks),) + own[0].shape, BF16)
    return merge(merge_second_kernel, [out], own[0], others[0], own[2], others[1], *other_blocks)[0]


def send_first(own):
    return swap_head(own[1], 2), swap_dp(own[3], 1)


def send_second(own):
    return swap_dp(own[1], 1), swap_head(own[3], 2)


def orthogonalize(place, terms, moment, *extra):
    pieces, size, _ = moment.shape
    terms = terms if isinstance(terms, tuple) else (terms,)
    width = terms[0].shape[1]
    spare = 32 if extra else 0
    return call(
        partial(ortho_kernel, place, len(terms)), "ortho", vmem(1 + len(terms) + len(extra)),
        [shape((pieces, size + spare, 2 * width), BF16)], [pltpu.VMEM((pieces * size, width), F32)], 1, 1,
    )(moment, *terms, *extra)[0]


def update(ratio, pieces, items, olds, news):
    def part_of(array, layer):
        dims = array.shape[1:]
        return pl.BlockSpec((1, *dims), lambda step: (layer,) + (0,) * len(dims))

    in_specs, operands, out_specs, outs, before = vmem(1), [pieces], [], [], []
    for name, layer, _ in items:
        for array in olds[name]:
            in_specs.append(part_of(array, layer))
            operands.append(array)
    for name, layer, _ in items:
        for position, like in enumerate((olds[name][0], olds[name][0], olds[name][0])):
            if name in news:
                before.append((news[name][position], len(outs)))
            outs.append(shape(like.shape, BF16 if position == 2 else F32))
            out_specs.append(part_of(like, layer))
    aliases = {len(operands) + position: out for position, (_, out) in enumerate(before)}
    results = pl.pallas_call(
        partial(update_kernel, ratio, [(name, base) for name, _, base in items], len(before)),
        name="update",
        grid=(1,),
        out_shape=outs,
        in_specs=in_specs + anywhere(len(before)),
        out_specs=out_specs,
        input_output_aliases=aliases,
        compiler_params=pltpu.CompilerParams(vmem_limit_bytes=VMEM_BYTES),
    )(*operands, *(array for array, _ in before))
    return {name: results[3 * place : 3 * place + 3] for place, (name, _, _) in enumerate(items)}


def doc_tables(segment_row, rows):
    index = lax.axis_index("head")
    own = lax.dynamic_slice_in_dim(segment_row, index * rows, rows, 0)
    starts = jnp.sum((segment_row[None, :] < own[:, None]).astype(jnp.int32), axis=1, dtype=jnp.int32)
    offsets = (index * rows + jnp.arange(rows, dtype=jnp.int32) - starts).astype(F32)
    half = HEAD_DIM // 2
    frequency = ROPE_BASE ** (-jnp.arange(half, dtype=F32) / half)
    angles = offsets[:, None] * frequency[None, :]
    scale = HEAD_DIM ** (-0.25)
    edges = segment_row.reshape(-1, rows)[:, :: rows - 1]
    others = jnp.stack([lax.dynamic_index_in_dim(edges, index ^ offset, 0, keepdims=False) for offset in (1, 2, 3)])
    mine = jnp.stack([own[0], own[rows - 1]])
    shares = (others[:, None, :] == mine[None, :, None]).astype(F32).reshape(3, 4)
    return SimpleNamespace(
        cosine=jnp.cos(angles) * scale, sine=jnp.sin(angles) * scale, row=own[None, :].astype(F32), shares=shares
    )


def cross_edges(summary, near):
    return swap_head(summary, 2), swap_head(near, 2)


def exchange_edges(summary):
    near = swap_head(summary, 1)
    return near, *cross_edges(summary, near)


def other_slots(values):
    return [swap_head(values, offset) for offset in (1, 2, 3)]


def adam_update(parameter, gradient, first_moment, second_moment):
    first_moment = BETA_FIRST * first_moment + (1.0 - BETA_FIRST) * gradient
    second_moment = BETA_SECOND * second_moment + (1.0 - BETA_SECOND) * gradient * gradient
    first_hat = first_moment / (1.0 - BETA_FIRST**STEP)
    second_hat = second_moment / (1.0 - BETA_SECOND**STEP)
    return (
        parameter - ADAM_RATE * first_hat / (jnp.sqrt(second_hat) + ADAM_EPSILON),
        first_moment,
        second_moment,
    )


def split_columns(matrix, width):
    rows = matrix.shape[0]
    return jnp.transpose(matrix.reshape(rows, -1, width), (1, 0, 2))


def join_columns(blocks):
    count, rows, width = blocks.shape
    return jnp.transpose(blocks, (1, 0, 2)).reshape(rows, count * width)


def attend_shard(query_key, value, out):
    return jnp.concatenate([query_key[:, 0], query_key[:, 1], value, out.T], axis=1).astype(BF16)


def old_blocks(layer, moments, block):
    query_key, value, out, up, down = (moment[layer] for moment in moments)
    return (
        jnp.stack([query_key[:, 0], query_key[:, 1], value, out.T]).astype(BF16),
        jnp.concatenate([split_columns(up, block), split_columns(down.T, block)]).astype(BF16),
    )


def line_parts(line, cuts):
    return [line[:, :, first:last] for first, last in cuts]


def core_vectors(vector_grads, bias_grads):
    vectors = jnp.concatenate(vector_grads)
    biases = jnp.stack(bias_grads)
    width = vectors.shape[1]
    keep, send = biases[:, 0::2].reshape(-1, width), biases[:, 1::2].reshape(-1, width)
    return jnp.concatenate([vectors, keep]), jnp.concatenate([vectors, send])


def across_vectors(total, layers):
    size = total.shape[0] - 2 * layers
    vectors, biases = total[:size], total[size:]
    return jnp.concatenate([vectors, biases[0::2]]), jnp.concatenate([vectors, biases[1::2]])


def per_device(
    block_input,
    cotangent,
    marked,
    segments,
    feature_map,
    vectors,
    bias_up,
    w_query_key,
    w_value,
    w_out,
    w_up,
    w_down,
    moment_query_key,
    moment_value,
    moment_out,
    moment_up,
    moment_down,
    vector_first,
    vector_second,
    bias_first,
    bias_second,
):
    layers = w_value.shape[0]
    block = w_value.shape[2]
    rows, width = block_input.shape
    dp_size = lax.axis_size("dp")
    dp_index = lax.axis_index("dp")
    quick = dp_size == 8 and layers == 2
    moments = (moment_query_key, moment_value, moment_out, moment_up, moment_down)

    def attend_of(layer):
        return attend_shard(w_query_key[layer], w_value[layer], w_out[layer])

    def hidden_of(layer):
        return jnp.concatenate([w_up[layer], w_down[layer].T], axis=1).astype(BF16)

    tables = doc_tables(segments[0], rows)
    resid = block_input.astype(F32)
    biases = []
    gradient = cotangent.astype(F32) * marked[0][:, None].astype(F32)
    states = [None] * layers

    def spread_biases(bias_up):
        slots = [bias_up] + other_slots(bias_up)
        biases.extend(jnp.stack([item[layer] for item in slots]) for layer in range(layers))

    def run_project(layer, resid, weight):
        states[layer] = project(resid, vectors[layer], tables, feature_map[layer], weight)

    def run_mix(layer, received, weights):
        state = states[layer]
        state.received = received
        mix(state.input, vectors[layer], biases[layer], state, received, tables, weights)
        return state.output

    def run_back_mix(layer, gradient, weights):
        back_mix(gradient, vectors[layer], states[layer], tables, weights)

    def run_back_project(layer, back_received, weight):
        state = states[layer]
        back_project(
            state.input, vectors[layer], state, state.received, back_received, tables, feature_map[layer], weight
        )
        return state.input_grad

    if quick:
        half = width // 2
        first = attend_of(0)
        hidden, second_attend, second_hidden = (
            four_times(part) for part in (hidden_of(0), attend_of(1), hidden_of(1))
        )
        line = [first] + [swap_dp(first, offset) for offset in (2, 4, 6)]

        blocks = [old_blocks(layer, moments, block) for layer in (1, 0)]
        (attend_one, hidden_one), (attend_zero, hidden_zero) = blocks
        payload = jnp.concatenate(
            [
                jnp.concatenate([hidden_one[4:], hidden_one[:4]]),
                jnp.concatenate([attend_one, hidden_zero[4:]]),
            ],
            axis=2,
        )
        line, hidden, payload = hold(line, hidden, payload)
        up_line, down_line = (jnp.stack([item[:, cut] for item in line]) for cut in (slice(half), slice(half, width)))
        up_y, down_x = swap_dp(up_line, 1), swap_head(down_line, 2)
        hidden_line = swap_line(hidden)

        up_line, down_line, up_y, down_x = hold(up_line, down_line, up_y, down_x)
        up, down = jnp.stack([up_line, up_y]), jnp.stack([down_line, down_x])
        up_other, down_other = swap_head(up, 2), swap_dp(down, 1)

        up, down, up_other, down_other, resid, held, second_attend = hold(
            up, down, up_other, down_other, resid, vars(tables), second_attend
        )
        vars(tables).update(held)
        cores = swap_all([up, up_other, down, down_other], swap_head, 1)
        cores, hidden_line, second_attend = hold(cores, hidden_line, second_attend)
        weight_one = [
            ((up, cores[0], up_other, cores[1]), "up near", 0, 0, half),
            ((down, cores[2], down_other, cores[3]), "down near", 0, half, half),
        ]
        up_line, down_line = line_parts(hidden_line, ((0, width), (width, 2 * width)))
        up_y, down_x = swap_dp(up_line, 1), swap_head(down_line, 2)
        attend_line = swap_line(second_attend)
        run_project(0, resid, weight_one)
        near = swap_head(states[0].summary, 1)

        up_line, down_line, up_y, down_x, near, attend_line, second_hidden, moments, gradient, late_bias = hold(
            up_line, down_line, up_y, down_x, near, attend_line, second_hidden, moments, gradient, bias_up
        )
        second_line = swap_line(second_hidden)
        spread_biases(late_bias)
        up, down = jnp.stack([up_line, up_y]), jnp.stack([down_line, down_x])
        up_other, down_other = swap_head(up, 2), swap_dp(down, 1)
        both = cross_edges(states[0].summary, near)
        cores = swap_all([up, down], swap_head, 1)
        attend_zero, hidden_zero = old_blocks(0, moments, block)
        payload_late = jnp.concatenate([hidden_zero[:4], attend_zero])

        branch = gradient.astype(BF16)
        branch_other = swap_head(branch, 1)

        cores, up_other, down_other, received, payload_late, branch_other = hold(
            cores, up_other, down_other, (near, *both), payload_late, branch_other
        )
        cores += swap_all([up_other, down_other], swap_head, 1)
        attend_up, attend_down = line_parts(attend_line, ((0, half), (half, width)))
        attend_y, attend_x = swap_dp(attend_up, 1), swap_head(attend_down, 2)
        cores, attend_y, attend_x, second_line, received = hold(cores, attend_y, attend_x, second_line, received)
        weights = [
            (
                weight_one,
                [((up, cores[0], up_other, cores[2]), "up", 0, 0, width)],
                [((down, cores[1], down_other, cores[3]), "down", 0, 0, width)],
            )
        ]
        up, down = jnp.stack([attend_up, attend_y]), jnp.stack([attend_down, attend_x])
        up_other, down_other = swap_head(up, 2), swap_dp(down, 1)
        up_line, down_line = line_parts(second_line, ((0, width), (width, 2 * width)))
        up_y, down_x = swap_dp(up_line, 1), swap_head(down_line, 2)
        resid = run_mix(0, received, weights[0])

        up_other, down_other, up_y, down_x, resid = hold(up_other, down_other, up_y, down_x, resid)
        up_late, down_late = jnp.stack([up_line, up_y]), jnp.stack([down_line, down_x])
        up_late_other, down_late_other = swap_head(up_late, 2), swap_dp(down_late, 1)
        cores = swap_all([up, down, up_other, down_other], swap_head, 1)
        late_cores = swap_all([up_late, down_late], swap_head, 1)
        cores, late_cores, resid = hold(cores, late_cores, resid)
        weight_one = [
            ((up, cores[0], up_other, cores[2]), "up", 0, 0, half),
            ((down, cores[1], down_other, cores[3]), "down", 0, half, half),
        ]
        run_project(1, resid, weight_one)

        summary = states[1].summary
        near = swap_head(summary, 1)
        both = cross_edges(summary, near)
        received, up_late_other, down_late_other, payload = hold(
            (near, *both), up_late_other, down_late_other, payload
        )
        late_cores += swap_all([up_late_other, down_late_other], swap_head, 1)
        weights.append(
            (
                weight_one,
                [((up_late, late_cores[0], up_late_other, late_cores[2]), "up", 0, 0, width)],
                [((down_late, late_cores[1], down_late_other, late_cores[3]), "down", 0, 0, width)],
            )
        )
        moment = swap_owners(payload)
        activations = run_mix(1, received, weights[1])

        moment, mix_pack, activations = hold(moment, states[1].mix_pack, activations)
        mix_other = swap_head(mix_pack, 1)
        down_one = down_grad(quick, states[1], mix_other, branch, branch_other, (None, None))

        down_one, gradient = hold(down_one, gradient)
        down_others = send_first(down_one)
        run_back_mix(1, gradient, weights[1])

        down_others, summary, back_pack = hold(down_others, states[1].back_summary, states[1].back_pack)
        near, back_other = swap_all([summary, back_pack], swap_head, 1)
        down_one = merge_first(down_one, down_others)
        near, back_other, down_one = hold(near, back_other, down_one)
        both = cross_edges(summary, near)
        down_others = send_second(down_one)
        up_one = up_grad(quick, states[1], back_other, mix_other)

        back_received, up_one, down_others = hold((near, *both), up_one, down_others)
        up_others = send_first(up_one)
        moment_late = swap_owners(payload_late)
        gradient = run_back_project(1, back_received, weights[1][0])

        up_others, gradient, stack_pack, mix_pack, moment_late = hold(
            up_others, gradient, states[1].stack_pack, states[0].mix_pack, moment_late
        )
        stack_other, mix_other = swap_all([stack_pack, mix_pack], swap_head, 1)
        up_one = merge_first(up_one, up_others)
        stack_other, mix_other, up_one = hold(stack_other, mix_other, up_one)
        up_others = send_second(up_one)
        down_blocks = merge_second(down_one, down_others)
        attend_one = attend_grad(quick, states[1], stack_other, back_other)

        attend_one, up_others, gradient = hold(attend_one, up_others, gradient)
        attend_others = send_first(attend_one)
        pair_one = swap_line(merge_second(up_one, up_others, down_blocks))
        run_back_mix(0, gradient, weights[0])

        attend_others, summary, back_pack = hold(attend_others, states[0].back_summary, states[0].back_pack)
        near, back_other = swap_all([summary, back_pack], swap_head, 1)
        attend_one = merge_first(attend_one, attend_others)
        near, back_other, attend_one = hold(near, back_other, attend_one)
        both = cross_edges(summary, near)
        attend_others = send_second(attend_one)
        down_zero = down_grad(quick, states[0], mix_other, stack_pack, stack_other, (3, 3))

        back_received, down_zero, attend_others = hold((near, *both), down_zero, attend_others)
        down_others = send_first(down_zero)
        gradient = run_back_project(0, back_received, weights[0][0])

        down_others, stack_pack, pair_one = hold(down_others, states[0].stack_pack, pair_one)
        stack_other = swap_head(stack_pack, 1)
        vector_grads = [(state.vector_one + state.vector_two)[:5] for state in states]
        kept, sent = core_vectors(vector_grads, [state.bias_grad for state in states])
        came = swap_head(sent, 1)
        up_zero = up_grad(quick, states[0], back_other, mix_other)
        down_zero = merge_first(down_zero, down_others)
        up_zero, down_zero, stack_other, one, one_others, came = hold(
            up_zero, down_zero, stack_other, attend_one, attend_others, came
        )
        down_others = send_second(down_zero)
        up_others = send_first(up_zero)
        attend_blocks = merge_second(one, one_others)
        kept, sent = across_vectors(kept + came, layers)
        came = swap_head(sent, 2)
        attend_zero = attend_grad(quick, states[0], stack_other, back_other)

        attend_zero, down_others, came, up_others = hold(attend_zero, down_others, came, up_others)
        attend_others = send_first(attend_zero)
        pair_two = swap_line(merge_second(down_zero, down_others, attend_blocks))
        back_one = orthogonalize(0, pair_one, moment, kept + came)
        up_zero = merge_first(up_zero, up_others)
        up_kept = up_zero[0], up_zero[2]
        up_others = send_second(up_zero)

        attend_others, pair_two, back_one, up_kept = hold(attend_others, pair_two, back_one, up_kept)
        attend_zero = merge_first(attend_zero, attend_others)
        attend_kept = attend_zero[0], attend_zero[2]
        attend_others = send_second(attend_zero)
        pieces_one = swap_owners(back_one)
        back_two = orthogonalize(1, pair_two, moment)

        attend_others, up_others, back_two = hold(attend_others, up_others, back_two)
        up_blocks = merge_second((up_kept[0], None, up_kept[1]), up_others)
        pair_three = merge_second((attend_kept[0], None, attend_kept[1]), attend_others, up_blocks)
        pair_three, pieces_one = hold(pair_three, pieces_one)
        pair_three = swap_line(pair_three)

        pair_three, back_two = hold(pair_three, back_two)
        pieces_two = swap_owners(back_two)
        back_three = orthogonalize(0, pair_three, moment_late)

        pieces_two, back_three = hold(pieces_two, back_three)
        pieces_three = swap_owners(back_three)
        packed = jnp.sum(pieces_one[:, moments[1].shape[1] :].astype(F32), axis=0)
        packed = packed[: 2 * kept.shape[0]]
        packed = jnp.concatenate([packed[: kept.shape[0]], packed[kept.shape[0] :]], axis=1)
        plan = [
            (pieces_one, [("up", 1, 4), ("down", 1, 0)]),
            (pieces_two, [("down", 0, 4), ("query_key", 1, 0), ("value", 1, 2), ("out", 1, 3)]),
            (pieces_three, [("up", 0, 0), ("query_key", 0, 4), ("value", 0, 6), ("out", 0, 7)]),
        ]
    else:
        spread_biases(bias_up)
        weights = []
        for layer in range(layers):
            parts = []
            for part in (attend_of(layer), w_up[layer].astype(BF16), w_down[layer].T.astype(BF16)):
                whole = lax.all_gather(part, "dp", axis=0, tiled=True).reshape(4, 2, width // 8, -1)
                parts.append([([whole] + other_slots(whole), "whole", 0, 0, width)])
            weights.append(tuple(parts))
        for layer in range(layers):
            run_project(layer, resid, weights[layer][0])
            resid = run_mix(layer, exchange_edges(states[layer].summary), weights[layer])
        activations = resid
        raw = []
        for layer in reversed(range(layers)):
            state = states[layer]
            branch = gradient.astype(BF16)
            run_back_mix(layer, gradient, weights[layer])
            gradient = run_back_project(layer, exchange_edges(state.back_summary), weights[layer][0])
            back_other, mix_other, stack_other, branch_other = swap_all(
                [state.back_pack, state.mix_pack, state.stack_pack, branch], swap_head, 1
            )
            for own in (
                attend_grad(quick, state, stack_other, back_other),
                up_grad(quick, state, back_other, mix_other),
                down_grad(quick, state, mix_other, branch, branch_other, (None, None)),
            ):
                for keep, send in ((own[0], own[1]), (own[2], own[3])):
                    raw.append(keep.astype(F32) + swap_head(send, 2).astype(F32))
        count = layers * 12
        padded = -(-count // dp_size) * dp_size
        grads = jnp.concatenate(raw)
        grads = jnp.concatenate([grads, jnp.zeros((padded - count,) + grads.shape[1:], F32)])
        grads = lax.psum_scatter(grads, "dp", scatter_dimension=0, tiled=True)
        old = [part for layer in reversed(range(layers)) for part in old_blocks(layer, moments, block)]
        old = jnp.concatenate(old)
        old = jnp.concatenate([old, jnp.zeros((padded - count,) + old.shape[1:], old.dtype)])
        old = lax.all_to_all(old, "dp", split_axis=0, concat_axis=1, tiled=True)
        owned = padded // dp_size
        back = jnp.concatenate(
            [orthogonalize(0, grads[place : place + 1], old[place : place + 1]) for place in range(owned)]
        )
        back = jnp.stack([back[..., :block], back[..., block:]], axis=1)
        back = lax.all_to_all(back, "dp", split_axis=2, concat_axis=0, tiled=True)
        back = jnp.concatenate([back[:, 0], back[:, 1]], axis=2)
        ordered = [back[12 * place : 12 * (place + 1)] for place in reversed(range(layers))]
        plan = [
            (part, [("query_key", layer, 0), ("value", layer, 2), ("out", layer, 3), ("up", layer, 4), ("down", layer, 8)])
            for layer, part in enumerate(ordered)
        ]
        vector_grads = [(state.vector_one + state.vector_two)[:5] for state in states]
        kept, sent = core_vectors(vector_grads, [state.bias_grad for state in states])
        kept, sent = across_vectors(kept + swap_head(sent, 1), layers)
        packed = lax.psum(kept + swap_head(sent, 2), "dp")

    vector_total, bias_total = packed[: 5 * layers].reshape(vectors.shape), packed[5 * layers :]
    olds = {
        "query_key": (w_query_key, moment_query_key),
        "value": (w_value, moment_value),
        "out": (w_out, moment_out),
        "up": (w_up, moment_up),
        "down": tuple(jnp.transpose(item, (0, 2, 1)) for item in (w_down, moment_down)),
    }
    news = {}
    for pieces, items in plan:
        news.update(update(width // block, pieces, items, olds, news))
    news["down"] = [jnp.transpose(item, (0, 2, 1)) for item in news["down"]]
    next_masters, next_moments, copies = zip(*(news[name] for name in ("query_key", "value", "out", "up", "down")))
    vectors_next, vector_first_next, vector_second_next = adam_update(
        vectors, vector_total, vector_first, vector_second
    )
    bias_next, bias_first_next, bias_second_next = adam_update(bias_up, bias_total, bias_first, bias_second)
    return (
        (activations.astype(BF16), gradient)
        + next_masters
        + next_moments
        + copies
        + (vectors_next, vector_first_next, vector_second_next, bias_next, bias_first_next, bias_second_next)
    )


def solution(mesh):
    shards = (
        P(None, "dp", None, "head"),
        P(None, "dp", "head"),
        P(None, "head", "dp"),
        P(None, "dp", "head"),
        P(None, "head", "dp"),
    )
    rows = P(("dp", "head"), None)
    placed = (
        (rows, rows, P("dp", "head"), P("dp", None), P(), P(), P(None, "head"))
        + shards
        + shards
        + (P(), P(), P(None, "head"), P(None, "head"))
    )
    return jax.shard_map(
        per_device,
        mesh=mesh,
        in_specs=placed,
        out_specs=(rows, rows) + shards + shards + shards + (P(), P(), P()) + (P(None, "head"),) * 3,
        check_vma=False,
    )
```
